128 devices in a mesh: lev: 4 (over x), band: 32 (over z, y, core).
Axes of the slice: x: 4, y: 4, z: 4, core: 2. Of those that a mesh axis runs over, the one named last changes fastest.
Arguments:
- spectra: bfloat16 [4, 4, 2, 2, 2048, 2048], P('lev', None, None, None, 'band'), may hold values from -1 to 1
- legendre: bfloat16 [2048, 64, 2048], P('band'), may hold values from -0.0034179688 to 0.0034179688
- wave_order: int32 [2048], replicated, may hold values from 0 to 2047, each once
- cand_block: int32 [6144], P('band'), may hold values from 0 to 255
- cand_owner: int32 [6144, 1], P('band'), may hold values from 0 to 31; in each aligned block of 192 rows (0 to 191, 192 to 383, ...) at most 12 rows name the same one
Outputs:
- vorticity: float32 [4, 4, 128, 8192], P('lev', None, 'band')
- okubo_weiss: float32 [4, 4, 128, 8192], P('lev', None, 'band')
- track_fits: float32 [12288, 20], P('band')
The draws below stay inside these ranges and needn't reach their ends.
Inputs may be any that keep to these rules, and one draw needn't show every extreme that they name: Each wavenumber appears once; slot s of spectra and legendre belongs to wavenumber wave_order[s]. `cand_owner`: among the 192 candidates of one band no owner is named more than 12 times, a bound that some block reaches.
All inputs are finite; a program needn't handle non-finite values.
Results may differ from the reference program's by a relative error of at most 0.0053.
Values may be sent and summed in bfloat16 or wider, within the bound.
A program may use at most 128 MiB of HBM per device.

```python
import math
import jax
import jax.numpy as jnp
import numpy as np
from jax import lax

K = 2048
NLON = 8192
ROWS = 4
BLON = 128
TIMES = 4
CAND_DEV = 192
LEVELS = 4
LAT = 128
HALF = 64
OWNERS = 32
CAP = 12
BLOCKS = 256
CANDS = 6144


def draw_spectra(key, part):
    key = jax.random.fold_in(key, 11)
    degree = jnp.arange(K, dtype=jnp.float32)
    ramp = degree * (degree + 1.0) / (K * K)
    shape = (LEVELS, TIMES, 2, 2, K, K)
    base = jnp.clip(0.5 * jax.random.normal(key, shape, jnp.float32), -1.0, 1.0)
    return (base * ramp).astype(jnp.bfloat16)


def touch_ends(drawn, rng, low, high):
    dims = drawn.shape
    index_at = [jax.random.randint(jax.random.fold_in(rng, axis), (), 0, dims[axis]) for axis in range(len(dims))]
    drawn = drawn.at[tuple(index_at)].set(low)
    longest = dims.index(max(dims))
    index_at[longest] = (index_at[longest] + 1) % dims[longest]
    return drawn.at[tuple(index_at)].set(high)


def block_levels(own_key, extent, pieces, least, largest):
    factor_of, own = 1.0, jax.random.fold_in(own_key, 6)
    for position, blocks in pieces:
        steps = jnp.exp(jax.random.uniform(jax.random.fold_in(own, position), (blocks,), jnp.float32, least / len(pieces), largest / len(pieces)))
        factor_of = factor_of * jnp.repeat(steps, extent[position] // blocks).reshape([-1 if axis == position else 1 for axis in range(len(extent))])
    return factor_of


def routed_block(rng, own, number, rows, count, top, limit, skew):
    sequence = jax.random.permutation(rng, count)
    packed, usual = shares(count, rows * top, limit, skew, True), shares(count, rows * top, limit, skew, False)
    places = jnp.arange(count)

    def named(sizes, offset_by):
        used = int((sizes > 0).sum())
        fixed = max(1, used // 4)
        moved = fixed + (places - fixed + offset_by * (used - fixed)) % max(1, count - fixed)
        return jnp.zeros((count,), jnp.int32).at[sequence[jnp.where(places < fixed, places, moved)]].set(jnp.asarray(sizes, jnp.int32))

    sizes = jnp.where(number % 4 == 0, named(packed, number // 4), named(usual, number - number // 4 - 1))
    mixed = jax.random.permutation(jax.random.fold_in(own, 3), count)
    source_of, taker = mixed[0:count // 2 * 2:2], mixed[1:count // 2 * 2:2]
    room = jnp.minimum(sizes[source_of] - 1, limit - sizes[taker]) // 2
    room = jnp.where((source_of == sequence[0]) | (taker == sequence[0]) | (sizes[taker] == 0), 0, jnp.maximum(room, 0))
    moved = jax.random.randint(jax.random.fold_in(own, 4), (count // 2,), 0, 1 << 20) % (room + 1)
    sizes = sizes.at[source_of].add(-moved).at[taker].add(moved)
    items = jnp.searchsorted(jnp.cumsum(sizes), jnp.arange(rows * top), side="right").astype(jnp.int32)
    table = items.reshape(top, rows).T
    table = table[jax.random.permutation(jax.random.fold_in(own, 1), rows)]
    offset_by = jax.random.randint(jax.random.fold_in(own, 2), (rows, 1), 0, top)
    return jnp.take_along_axis(table, (jnp.arange(top)[None, :] + offset_by) % top, axis=1)


def shares(number_of, total, bound, lean, full):
    loads = [(1 << 20) // math.isqrt(grade ** lean) + 1 for grade in range(1, number_of + 1)]
    largest = bound if full else min(bound, max(-(-total // number_of), total * loads[0] // sum(loads)))
    least = 1 if total - largest >= number_of - 1 else 0
    counts, surplus = [largest] + [least] * (number_of - 1), total - largest - least * (number_of - 1)
    while surplus > 0:
        free = [i for i in range(1, number_of) if counts[i] < largest] or [i for i in range(1, number_of) if counts[i] < bound]
        pool, remaining = sum([loads[i] for i in free]), surplus
        for i in free:
            more = min(bound - counts[i], max(1, remaining * loads[i] // pool), surplus)
            counts[i] = counts[i] + more
            surplus = surplus - more
    return np.array(counts)


def normal_values(rng, shape, spread, most, shards=(), held_as=jnp.bfloat16):
    loudness = block_levels(rng, shape, shards, -0.22, 0.18) if shards else 1.0
    result = jax.random.normal(rng, shape, jnp.float32) * spread * loudness
    return jnp.minimum(jnp.maximum(result, -most), most).astype(held_as)


def setup_inputs(seed: int = 0) -> dict:
    splits = jax.random.split(jax.random.key(seed), 6)
    spectra = draw_spectra(jax.random.fold_in(splits[5], 71), 0)
    legendre = normal_values(splits[1], (K, HALF, K), (2 * K * K // 3) ** -0.5, 0.0034179688, ((0, 32),))
    wave_order = jax.random.permutation(splits[2], K).astype(jnp.int32)
    cand_block = touch_ends(jax.random.randint(splits[3], (CANDS,), 0, BLOCKS), jax.random.fold_in(splits[3], 1), 0, BLOCKS - 1).astype(jnp.int32)
    cand_owner_keys = jax.random.split(jax.random.fold_in(splits[4], 1), CANDS // CAND_DEV)
    cand_owner_turns = jax.random.permutation(jax.random.fold_in(splits[4], 3), CANDS // CAND_DEV)
    cand_owner = jax.vmap(lambda own, number: routed_block(jax.random.fold_in(splits[4], 2), own, number, CAND_DEV, OWNERS, 1, CAP, 2))(cand_owner_keys, cand_owner_turns).reshape((CANDS, 1))
    return {"spectra": spectra, "legendre": legendre, "wave_order": wave_order, "cand_block": cand_block, "cand_owner": cand_owner}


def ortho_values(count):
    offset = jnp.arange(count, dtype=jnp.float32) - (count - 1) / 2.0
    constant = jnp.ones_like(offset)
    square = offset * offset - (count * count - 1) / 12.0
    cubic = offset * offset * offset - (3 * count * count - 7) / 20.0 * offset
    stacked = jnp.stack([constant, offset, square, cubic], 0)
    return stacked / jnp.sqrt(lax.optimization_barrier(jnp.sum(stacked * stacked, axis=1, keepdims=True)))

def fit_basis(row_count, col_count):
    across = ortho_values(col_count)
    upward = ortho_values(row_count)
    orders = ((0, 0), (1, 0), (0, 1), (2, 0), (1, 1), (0, 2), (3, 0), (2, 1), (1, 2), (0, 3))
    columns = [(upward[y_order][:, None] * across[x_order][None, :]).reshape(-1) for x_order, y_order in orders]
    return jnp.stack(columns, 1)

def metric_fields(psi_field, chi_field, lat_index, lat_total, wave_total, lon_total):
    step_y = math.pi / (2.0 * wave_total)
    latitude = (lat_total / 2.0 - lat_index - 0.5) * step_y
    step_x = (jnp.cos(latitude) * (2.0 * math.pi / lon_total)).reshape(-1, 1)

    def second_parts(values):
        centre = values[..., 1:-1, :]
        upper_row = values[..., :-2, :]
        lower_row = values[..., 2:, :]
        along_x = (jnp.roll(centre, -1, -1) - 2.0 * centre + jnp.roll(centre, 1, -1)) / (step_x * step_x)
        along_y = (upper_row - 2.0 * centre + lower_row) / (step_y * step_y)
        mixed_xy = (jnp.roll(upper_row, -1, -1) - jnp.roll(upper_row, 1, -1) - jnp.roll(lower_row, -1, -1) + jnp.roll(lower_row, 1, -1)) / (4.0 * step_x * step_y)
        return (along_x, along_y, mixed_xy)
    psi_xx, psi_yy, psi_xy = second_parts(psi_field)
    chi_xx, chi_yy, chi_xy = second_parts(chi_field)
    vorticity = psi_xx + psi_yy
    strain_normal = -2.0 * psi_xy + chi_xx - chi_yy
    strain_shear = psi_xx - psi_yy + 2.0 * chi_xy
    okubo_weiss = strain_normal * strain_normal + strain_shear * strain_shear - vorticity * vorticity
    return (vorticity, okubo_weiss)

def reference(spectra, legendre, wave_order, cand_block, cand_owner):
    span_slots = min(K, 64)
    block_count = K // span_slots
    degree = jnp.arange(K, dtype=jnp.int32)
    degree_f = degree.astype(jnp.float32)
    inverse = jnp.where(degree >= 1, -1.0 / jnp.maximum(degree_f * (degree_f + 1.0), 1.0), 0.0).astype(jnp.float32)

    def transform(index):
        first_slot = (index * span_slots).astype(jnp.int32)
        spec_part = lax.dynamic_slice_in_dim(spectra, first_slot, span_slots, 4).astype(jnp.float32)
        table_part = lax.dynamic_slice_in_dim(legendre, first_slot, span_slots, 0).astype(jnp.float32)
        wave_part = lax.dynamic_slice_in_dim(wave_order, first_slot, span_slots, 0)
        kept_mask = degree[None, :] >= wave_part[:, None]
        parity = jnp.where((degree[None, :] - wave_part[:, None]) % 2 == 0, 1.0, -1.0).astype(jnp.float32)
        scaled = spec_part * jnp.where(kept_mask, inverse[None, :], 0.0).astype(jnp.float32)
        even_input = lax.optimization_barrier(scaled.astype(jnp.bfloat16)).astype(jnp.float32)
        odd_input = lax.optimization_barrier((scaled * parity).astype(jnp.bfloat16)).astype(jnp.float32)
        northern = jnp.einsum('ltfcsn,shn->ltfcsh', even_input, table_part, precision=lax.Precision.HIGHEST).astype(jnp.bfloat16)
        southern = jnp.einsum('ltfcsn,shn->ltfcsh', odd_input, table_part, precision=lax.Precision.HIGHEST).astype(jnp.bfloat16)
        return (northern, southern)
    northern, southern = lax.map(transform, jnp.arange(block_count, dtype=jnp.int32))
    northern = jnp.moveaxis(northern, 0, 4).reshape(LEVELS, TIMES, 2, 2, K, HALF)
    southern = jnp.moveaxis(southern, 0, 4).reshape(LEVELS, TIMES, 2, 2, K, HALF)
    fourier = jnp.concatenate([northern, jnp.flip(southern, -1)], -1).astype(jnp.float32)
    real_part = jnp.swapaxes(fourier[:, :, :, 0], -1, -2)
    imag_part = jnp.swapaxes(fourier[:, :, :, 1], -1, -2)
    empty = jnp.zeros((LEVELS, TIMES, 2, LAT, NLON // 2 + 1), jnp.float32)
    real_full = empty.at[..., wave_order].set(real_part)
    imag_full = empty.at[..., wave_order].set(imag_part)
    spectrum = lax.complex(real_full, imag_full)
    grid_field = jnp.fft.irfft(spectrum, n=NLON, axis=-1) * NLON
    padded = jnp.pad(grid_field, ((0, 0), (0, 0), (0, 0), (1, 1), (0, 0)))
    lat_index = jnp.arange(LAT, dtype=jnp.int32).astype(jnp.float32)
    vorticity, okubo_weiss = metric_fields(padded[:, :, 0], padded[:, :, 1], lat_index, LAT, K, NLON)
    mean_vort = lax.optimization_barrier(jnp.sum(vorticity, 0)) / LEVELS
    mean_okubo = lax.optimization_barrier(jnp.sum(okubo_weiss, 0)) / LEVELS
    fields = jnp.stack([mean_vort, mean_okubo], 1)
    per_row = NLON // BLON
    blocks = fields.reshape(TIMES, 2, OWNERS, ROWS, per_row, BLON).transpose(2, 0, 4, 1, 3, 5).reshape(OWNERS, BLOCKS, 2, ROWS * BLON)
    source = jnp.arange(CANDS, dtype=jnp.int32) // CAND_DEV
    picked = blocks[source, cand_block]
    projections = jnp.einsum('qfp,pb->qfb', picked, fit_basis(ROWS, BLON), precision=lax.Precision.HIGHEST).reshape(CANDS, 20)
    owner_index = cand_owner[:, 0]
    onehot = (owner_index[:, None] == jnp.arange(OWNERS, dtype=jnp.int32)[None, :]).astype(jnp.int32).reshape(OWNERS, CAND_DEV, OWNERS)
    earlier = jnp.cumsum(onehot, 1) - onehot
    slot_index = lax.optimization_barrier(jnp.sum(earlier * onehot, -1)).reshape(CANDS)
    target = owner_index * (OWNERS * CAP) + source * CAP + slot_index
    track_fits = jnp.zeros((OWNERS * OWNERS * CAP, 20), jnp.float32).at[target].set(projections)
    return (vorticity, okubo_weiss, track_fits)
```

```python
import math

import jax
import jax.numpy as jnp
import ml_dtypes
import numpy as np
from jax import lax
from jax.experimental import pallas as pl
from jax.experimental.pallas import tpu as pltpu
from jax.sharding import PartitionSpec as P

MESH = pl.DeviceIdType.MESH
F32 = jnp.float32
BF16 = jnp.bfloat16

BANDS = 32
LEVS = 4
SLOTS = 64
K = 2048
NLON = 8192
HALF = 64
TIMES = 4
GROUP = 16
WIDTH = 128
CANDS = 192
CAP = 12
ROUNDS = CAP // 4


def bf16_split(table):
    high = table.astype(np.float32).astype(ml_dtypes.bfloat16)
    low = (table - high.astype(np.float64)).astype(np.float32).astype(ml_dtypes.bfloat16)
    return high, low


def degree_table():
    n = np.arange(K, dtype=np.float32)
    inverse = np.where(n >= 1, np.float32(-1.0) / np.maximum(n * (n + 1), np.float32(1.0)), 0.0)
    table = np.zeros((8, K), np.float32)
    table[0] = inverse
    table[1] = np.where(np.arange(K) % 2 == 0, 1.0, -1.0)
    return table


def row_table():
    hy = math.pi / 4096.0
    j = np.arange(HALF)
    hx = np.cos((63.5 - j) * hy) * 2.0 * math.pi / NLON
    table = np.zeros((8, WIDTH), np.float64)
    table[0, :HALF] = table[0, HALF:] = 1.0 / (hx * hx)
    table[1, :HALF] = 1.0 / (4.0 * hx * hy)
    table[1, HALF:] = -1.0 / (4.0 * hx * hy)
    table[2] = 1.0 / (hy * hy)
    return table.astype(np.float32)


def first_table():
    h = np.arange(32)[:, None]
    x = np.arange(WIDTH)[None, :]
    angle = 2.0 * np.pi * ((h * x) % 128) / 128.0
    cos, sin = np.cos(angle), np.sin(angle)
    table = np.concatenate(
        [np.concatenate([cos, sin], 1), np.concatenate([-sin, cos], 1)], 0
    )
    high, low = bf16_split(table)
    return np.concatenate([high, low], 0)


def twiddle_table():
    low = np.arange(64)[:, None]
    x = np.arange(WIDTH)[None, :]
    angle = 2.0 * np.pi * (low * x) / NLON
    cos, sin = np.cos(angle), np.sin(angle)
    return np.stack([np.concatenate([cos, cos], 0), np.concatenate([sin, sin], 0)], 0).astype(
        np.float32
    )


def second_table():
    y = np.arange(64)[:, None]
    low = np.arange(64)[None, :]
    angle = 2.0 * np.pi * ((y * low) % 64) / 64.0
    cos, sin = np.cos(angle), -np.sin(angle)
    zero = np.zeros_like(cos)
    table = np.concatenate(
        [
            np.concatenate([cos, zero, sin, zero], 1),
            np.concatenate([zero, cos, zero, sin], 1),
        ],
        0,
    )
    high, low_part = bf16_split(table)
    return np.concatenate([high, low_part, high], 1)


ORDERS = ((0, 0), (1, 0), (0, 1), (2, 0), (1, 1), (0, 2), (3, 0), (2, 1), (1, 2), (0, 3))


def ortho_values(count):
    u = np.arange(count, dtype=np.float64) - (count - 1) / 2.0
    q = np.stack(
        [
            np.ones_like(u),
            u,
            u * u - (count * count - 1) / 12.0,
            u * u * u - (3 * count * count - 7) / 20.0 * u,
        ],
        0,
    )
    return q / np.sqrt(np.sum(q * q, 1, keepdims=True))


def fit_tables():
    across, upward = ortho_values(WIDTH), ortho_values(4)
    columns = np.stack([across[a] for a, _ in ORDERS], 1)
    table = np.zeros((256, 32), np.float64)
    table[:128, 0:10] = columns
    table[128:, 10:20] = columns
    high, low = bf16_split(table)
    both = np.zeros((256, 128), high.dtype)
    both[:, 0:32] = high
    both[:, 32:64] = low
    rows = np.zeros((8, 128), np.float32)
    for r in range(4):
        line = [upward[b][r] / 4.0 for _, b in ORDERS]
        rows[r, 0:10] = line
        rows[r, 10:20] = line
    return both, rows


def column_of(row):
    return jnp.broadcast_to(row, (WIDTH, WIDTH)).T


def legendre_kernel(
    spec_hbm,
    leg_hbm,
    wave_ref,
    degree_ref,
    rows_ref,
    recv,
    spec,
    leg,
    scaled,
    factor,
    columns,
    sums,
    turned,
    send,
    spec_sem,
    leg_sem,
    own_sem,
    send_sem,
    recv_sem,
):
    me = lax.axis_index("band")
    groups = SLOTS // GROUP

    def spec_copy(g):
        window = pl.ds(g * GROUP, GROUP)
        return pltpu.make_async_copy(
            spec_hbm.at[:, window, :], spec.at[:, window, :], spec_sem.at[g]
        )

    def leg_copy(g):
        window = pl.ds(g * GROUP, GROUP)
        return pltpu.make_async_copy(leg_hbm.at[window], leg.at[window], leg_sem.at[g])

    for g in range(groups):
        spec_copy(g).start()
        leg_copy(g).start()

    barrier = pltpu.get_barrier_semaphore()

    def greet(k, carry):
        pl.semaphore_signal(
            barrier,
            inc=1,
            device_id={"band": lax.rem(me + k, BANDS)},
            device_id_type=MESH,
        )
        return carry

    lax.fori_loop(1, BANDS, greet, 0)

    line = wave_ref[pl.ds(me // 2, 1), :].astype(F32)
    columns[...] = column_of(line)
    first = pl.multiple_of(lax.rem(me, 2) * SLOTS, SLOTS)
    lane = lax.broadcasted_iota(jnp.int32, (1, K), 1).astype(F32)

    def one_group(g, carry):
        spec_copy(g).wait()
        own = columns[pl.ds(pl.multiple_of(first + g * GROUP, GROUP), GROUP), :]
        own = jnp.concatenate([own] * (K // WIDTH), axis=1)
        factor[...] = jnp.where(lane >= own, degree_ref[0:1, :], 0.0)
        start = pl.multiple_of(g * GROUP, GROUP)

        def scale(q, inner):
            part = spec[q, pl.ds(start, GROUP), :].astype(F32) * factor[...]
            window = pl.ds(pl.multiple_of(q * GROUP, GROUP), GROUP)
            for tile in range(K // WIDTH):
                scaled[tile, window, :] = part[:, tile * WIDTH : (tile + 1) * WIDTH]
            return inner

        lax.fori_loop(0, 16, scale, 0)
        leg_copy(g).wait()

        def one_slot(i, inner):
            even = jnp.concatenate(
                [scaled[tile, pl.ds(i, 16, stride=GROUP), :] for tile in range(K // WIDTH)],
                axis=1,
            )
            odd = even * degree_ref[1:2, :]
            both = jnp.concatenate([even.astype(BF16), odd.astype(BF16)], axis=0)
            result = lax.dot_general(
                both,
                leg[start + i],
                (((1,), (1,)), ((), ())),
                preferred_element_type=F32,
            )
            result = result.astype(BF16).astype(F32)
            sums[pl.ds(pl.multiple_of((start + i) * 16, 16), 16), :] = jnp.concatenate(
                [result[:16], result[16:]], axis=1
            )
            return inner

        lax.fori_loop(0, GROUP, one_slot, 0)
        return carry

    lax.fori_loop(0, groups, one_group, 0)

    m = columns[pl.ds(first, SLOTS), :]
    lanes = lax.broadcasted_iota(jnp.int32, (SLOTS, WIDTH), 1)
    half_m = jnp.floor(m * 0.5)
    parity = 1.0 - 2.0 * (m - 2.0 * half_m)
    weight = jnp.where(m == 0.0, 1.0, 2.0)
    sign = jnp.where(lanes >= HALF, parity, 1.0) * weight
    x = m * (math.pi / NLON)
    x2 = x * x
    sin = x * (
        1.0
        + x2 * (-1.0 / 6 + x2 * (1.0 / 120 + x2 * (-1.0 / 5040 + x2 * (1.0 / 362880))))
    )
    cos = 1.0 + x2 * (
        -0.5
        + x2 * (1.0 / 24 + x2 * (-1.0 / 720 + x2 * (1.0 / 40320 - x2 * (1.0 / 3628800))))
    )
    xx = -4.0 * sin * sin * rows_ref[0:1, :]
    xy = 2.0 * (2.0 * sin * cos) * rows_ref[1:2, :]
    yy = rows_ref[2:3, :]
    first_lane = (lanes == 0) | (lanes == HALF)
    last_lane = (lanes == HALF - 1) | (lanes == WIDTH - 1)

    def one_time(t, carry):
        def pieces(q):
            c = sums[pl.ds(t * 4 + q, SLOTS, stride=16), :] * sign
            before = jnp.where(first_lane, 0.0, pltpu.roll(c, 1, 1))
            after = jnp.where(last_lane, pltpu.roll(c, HALF, 1), pltpu.roll(c, WIDTH - 1, 1))
            return c * xx, (before + after - 2.0 * c) * yy, (before - after) * xy

        pr_xx, pr_yy, pr_xy = pieces(0)
        pi_xx, pi_yy, pi_xy = pieces(1)
        cr_xx, cr_yy, cr_xy = pieces(2)
        ci_xx, ci_yy, ci_xy = pieces(3)
        vort = (pr_xx + pr_yy, pi_xx + pi_yy)
        normal = (2.0 * pi_xy + cr_xx - cr_yy, -2.0 * pr_xy + ci_xx - ci_yy)
        shear = (pr_xx - pr_yy - 2.0 * ci_xy, pi_xx - pi_yy + 2.0 * cr_xy)
        for q, pair in enumerate((vort, normal, shear)):
            block = jnp.concatenate(pair, axis=0).T
            turned[q, pl.ds(t, WIDTH, stride=4), :] = block
        return carry

    lax.fori_loop(0, TIMES, one_time, 0)

    pl.semaphore_wait(barrier, BANDS - 1)

    def place(d):
        return jnp.where(d < BANDS // 2, d, BANDS + BANDS // 2 - 1 - d)

    def message(k):
        d = lax.rem(me + k, BANDS)
        return pltpu.make_async_remote_copy(
            src_ref=send.at[k],
            dst_ref=recv.at[me],
            send_sem=send_sem.at[k],
            recv_sem=recv_sem.at[me],
            device_id={"band": d},
            device_id_type=MESH,
        )

    def fill(k):
        p = place(lax.rem(me + k, BANDS))
        for q in range(3):
            send[k, 16 * q : 16 * q + 16, :] = turned[
                q, pl.ds(pl.multiple_of(p * 16, 16), 16), :
            ].astype(BF16)

    def post(k, carry):
        fill(k)
        message(k).start()
        return carry

    lax.fori_loop(1, BANDS, post, 0)
    fill(0)
    own_copy = pltpu.make_async_copy(send.at[0], recv.at[me], own_sem)
    own_copy.start()

    def finish(k, carry):
        message(k).wait_send()
        source = lax.rem(me + k, BANDS)
        pltpu.make_async_remote_copy(
            src_ref=send.at[k],
            dst_ref=recv.at[source],
            send_sem=send_sem.at[k],
            recv_sem=recv_sem.at[source],
            device_id={"band": source},
            device_id_type=MESH,
        ).wait_recv()
        return carry

    lax.fori_loop(1, BANDS, finish, 0)
    own_copy.wait()


def legendre_part(spectra, legendre, waves):
    vmem = pl.BlockSpec(memory_space=pltpu.VMEM)
    hbm = pl.BlockSpec(memory_space=pl.ANY)
    return pl.pallas_call(
        legendre_kernel,
        out_shape=jax.ShapeDtypeStruct((BANDS, 48, WIDTH), BF16),
        in_specs=[hbm, hbm, vmem, vmem, vmem],
        out_specs=vmem,
        scratch_shapes=[
            pltpu.VMEM((16, SLOTS, K), BF16),
            pltpu.VMEM((SLOTS, HALF, K), BF16),
            pltpu.VMEM((K // WIDTH, 16 * GROUP, WIDTH), F32),
            pltpu.VMEM((GROUP, K), F32),
            pltpu.VMEM((WIDTH, WIDTH), F32),
            pltpu.VMEM((SLOTS * 16, WIDTH), F32),
            pltpu.VMEM((3, 4 * WIDTH, WIDTH), F32),
            pltpu.VMEM((BANDS, 48, WIDTH), BF16),
            pltpu.SemaphoreType.DMA((SLOTS // GROUP,)),
            pltpu.SemaphoreType.DMA((SLOTS // GROUP,)),
            pltpu.SemaphoreType.DMA,
            pltpu.SemaphoreType.DMA((BANDS,)),
            pltpu.SemaphoreType.DMA((BANDS,)),
        ],
        compiler_params=pltpu.CompilerParams(
            collective_id=0, has_side_effects=True, vmem_limit_bytes=56 * 1024 * 1024
        ),
        name="legendre_transpose",
    )(spectra, legendre, waves, degree_table(), row_table())


def grid_kernel(
    coeffs,
    wave_ref,
    owner_ref,
    block_ref,
    first_ref,
    twiddle_ref,
    second_ref,
    fit_ref,
    fit_rows,
    vort_out,
    okubo_out,
    picked_out,
    ordered_in,
    onehot,
    spread,
    table,
):
    band = lax.axis_index("band")
    lane = lax.broadcasted_iota(jnp.int32, (WIDTH, WIDTH), 1)
    low_lanes = lane < 64

    def one_block(j, carry):
        column = column_of(wave_ref[pl.ds(j, 1), :].astype(F32))
        rows = pl.ds(pl.multiple_of(j * WIDTH, WIDTH), WIDTH)
        for tile in range(K // WIDTH):
            wanted = lane.astype(F32) + float(tile * WIDTH)
            onehot[rows, tile * WIDTH : (tile + 1) * WIDTH] = jnp.where(
                column == wanted, 1.0, 0.0
            ).astype(BF16)
        return carry

    lax.fori_loop(0, K // WIDTH, one_block, 0)

    pick = low_lanes[:48]
    for j in range(BANDS // 2):
        a = coeffs[2 * j].astype(F32)
        b = coeffs[2 * j + 1].astype(F32)
        real = jnp.where(pick, a, pltpu.roll(b, 64, 1))
        imag = jnp.where(pick, pltpu.roll(a, 64, 1), b)
        ordered_in[0:48, j * WIDTH : (j + 1) * WIDTH] = real.astype(BF16)
        ordered_in[48:96, j * WIDTH : (j + 1) * WIDTH] = imag.astype(BF16)

    pick = low_lanes[:8]
    for j in range(8):
        part = jnp.dot(
            ordered_in[...], onehot[:, 256 * j : 256 * (j + 1)], preferred_element_type=F32
        )
        for tile in range(2):
            h = 4 * j + 2 * tile
            for c in range(2):
                for f in range(3):
                    at = c * 48 + f * 16
                    a = part[at : at + 8, tile * WIDTH : (tile + 1) * WIDTH]
                    b = part[at + 8 : at + 16, tile * WIDTH : (tile + 1) * WIDTH]
                    to = c * 24 + f * 8
                    spread[h * 48 + to : h * 48 + to + 8, :] = jnp.where(
                        pick, a, pltpu.roll(b, 64, 1)
                    )
                    spread[(h + 1) * 48 + to : (h + 1) * 48 + to + 8, :] = jnp.where(
                        pick, pltpu.roll(a, 64, 1), b
                    )

    southern = band >= BANDS // 2
    table[...] = jnp.zeros_like(table)
    for rr in range(2):
        row_low = jnp.where(southern, 3 - rr, rr)
        row_high = jnp.where(southern, 1 - rr, 2 + rr)

        def one_time(t, carry, rr=rr, row_low=row_low, row_high=row_high):
            parts = []
            for f in range(3):
                i = f * 8 + rr * 4 + t
                c = jnp.concatenate(
                    [spread[pl.ds(i, 32, stride=48), :], spread[pl.ds(24 + i, 32, stride=48), :]],
                    axis=0,
                ).T.astype(BF16)
                z = jnp.dot(
                    jnp.concatenate([c, c], axis=1), first_ref[...], preferred_element_type=F32
                )
                zr, zi = z[:, :WIDTH], z[:, WIDTH:]
                tc, ts = twiddle_ref[0], twiddle_ref[1]
                parts.append(jnp.concatenate([zr * tc - zi * ts, zr * ts + zi * tc], axis=0))
            z = jnp.concatenate(parts, axis=1)
            high = z.astype(BF16)
            low = (z - high.astype(F32)).astype(BF16)
            grid = jnp.dot(
                second_ref[...],
                jnp.concatenate([high, high, low], axis=0),
                preferred_element_type=F32,
            )
            vort = grid[:, :WIDTH]
            normal = grid[:, WIDTH : 2 * WIDTH]
            shear = grid[:, 2 * WIDTH :]
            okubo = normal * normal + shear * shear - vort * vort
            vort_out[t, pl.ds(row_low, 64, stride=4), :] = vort[:64]
            vort_out[t, pl.ds(row_high, 64, stride=4), :] = vort[64:]
            okubo_out[t, pl.ds(row_low, 64, stride=4), :] = okubo[:64]
            okubo_out[t, pl.ds(row_high, 64, stride=4), :] = okubo[64:]
            both = jnp.concatenate([vort, okubo], axis=1)
            high = both.astype(BF16)
            low = (both - high.astype(F32)).astype(BF16)
            from_high = jnp.dot(high, fit_ref[...], preferred_element_type=F32)
            from_low = jnp.dot(low, fit_ref[...], preferred_element_type=F32)
            fits = from_high + pltpu.roll(from_high, WIDTH - 32, 1) + from_low
            window = pl.ds(pl.multiple_of(t * 64, 64), 64)
            table[window, :] += (
                fits[:64] * fit_rows[pl.ds(row_low, 1), :]
                + fits[64:] * fit_rows[pl.ds(row_high, 1), :]
            )
            return carry

        lax.fori_loop(0, TIMES, one_time, 0)

    lanes = lax.broadcasted_iota(jnp.int32, (CANDS, WIDTH), 1)
    owner = owner_ref[...]
    owned = jnp.where(owner == lanes, 1.0, 0.0)
    order = jnp.where(
        lax.broadcasted_iota(jnp.int32, (CANDS, CANDS), 1)
        < lax.broadcasted_iota(jnp.int32, (CANDS, CANDS), 0),
        1.0,
        0.0,
    ).astype(BF16)
    earlier = jnp.dot(order, owned.astype(BF16), preferred_element_type=F32)
    slot = jnp.sum(earlier * owned, axis=1, keepdims=True).astype(jnp.int32)
    target = (slot & 3) * WIDTH + owner * 4 + (slot >> 2)
    goal = jnp.where(
        lax.broadcasted_iota(jnp.int32, (CANDS, 4 * WIDTH), 1) == target, 1.0, 0.0
    )
    named = jnp.where(
        lax.broadcasted_iota(jnp.int32, (256, CANDS), 0) == block_ref[...], 1.0, 0.0
    )
    values = table[...]
    high = values.astype(BF16).astype(F32)
    low = values - high
    chosen = jnp.dot(
        named.T.astype(BF16),
        jnp.concatenate([high, low], axis=1).astype(BF16),
        preferred_element_type=F32,
    )
    total = jnp.zeros((WIDTH, WIDTH), F32)
    for g in range(4):
        high = chosen[:, :WIDTH]
        low = chosen[:, WIDTH:]
        if g:
            high = pltpu.roll(high, 32 * g, 1)
            low = pltpu.roll(low, 32 * g, 1)
        which = goal[:, g * WIDTH : (g + 1) * WIDTH].T.astype(BF16)
        total += jnp.dot(which, high.astype(BF16), preferred_element_type=F32)
        total += jnp.dot(which, low.astype(BF16), preferred_element_type=F32)
    picked_out[...] = total


def grid_part(coeffs, waves, owner, block):
    vmem = pl.BlockSpec(memory_space=pltpu.VMEM)
    fit_table, fit_rows = fit_tables()
    return pl.pallas_call(
        grid_kernel,
        out_shape=(
            jax.ShapeDtypeStruct((TIMES, 256, WIDTH), F32),
            jax.ShapeDtypeStruct((TIMES, 256, WIDTH), F32),
            jax.ShapeDtypeStruct((WIDTH, WIDTH), F32),
        ),
        in_specs=[vmem] * 9,
        out_specs=(vmem, vmem, vmem),
        scratch_shapes=[
            pltpu.VMEM((96, K), BF16),
            pltpu.VMEM((K, K), BF16),
            pltpu.VMEM((32 * 48, WIDTH), F32),
            pltpu.VMEM((256, WIDTH), F32),
        ],
        compiler_params=pltpu.CompilerParams(vmem_limit_bytes=48 * 1024 * 1024),
        name="grid_synthesis",
    )(
        coeffs,
        waves,
        owner,
        block,
        first_table(),
        twiddle_table(),
        second_table(),
        fit_table,
        fit_rows,
    )


def owner_kernel(mine, fits_out, parts, summed, arrived, own_sem, send_a, recv_a, send_b, recv_b):
    lev = lax.axis_index("lev")
    band = lax.axis_index("band")
    group = band // 8
    inside = group == lev

    barrier = pltpu.get_barrier_semaphore()
    for k in range(1, LEVS):
        pl.semaphore_signal(
            barrier,
            inc=1,
            device_id={"lev": lax.rem(lev + k, LEVS), "band": band},
            device_id_type=MESH,
        )

    def greet(k, carry):
        source = lax.rem(band + k, BANDS)

        @pl.when(jnp.logical_not(inside & (k == 0)))
        def _():
            pl.semaphore_signal(
                barrier,
                inc=1,
                device_id={"lev": group, "band": source},
                device_id_type=MESH,
            )

        return carry

    lax.fori_loop(0, BANDS, greet, 0)
    pl.semaphore_wait(barrier, LEVS - 1 + BANDS - inside.astype(jnp.int32))

    def level_copy(k):
        to = lax.rem(lev + k, LEVS)
        return pltpu.make_async_remote_copy(
            src_ref=mine.at[pl.ds(to * 8, 8)],
            dst_ref=parts.at[lev],
            send_sem=send_a.at[k],
            recv_sem=recv_a.at[lev],
            device_id={"lev": to, "band": band},
            device_id_type=MESH,
        )

    for k in range(1, LEVS):
        level_copy(k).start()
    parts[lev] = mine[pl.ds(lev * 8, 8)]
    for k in range(1, LEVS):
        source = lax.rem(lev + k, LEVS)
        pltpu.make_async_remote_copy(
            src_ref=mine.at[pl.ds(source * 8, 8)],
            dst_ref=parts.at[source],
            send_sem=send_a.at[k],
            recv_sem=recv_a.at[source],
            device_id={"lev": source, "band": band},
            device_id_type=MESH,
        ).wait_recv()
    summed[...] = (parts[0] + parts[1]) + (parts[2] + parts[3])

    def owner_copy(k):
        to = lax.rem(lev + k // 8, LEVS)
        o = lax.rem(band + k, 8)
        return (
            jnp.logical_not((to == lev) & (lev * 8 + o == band)),
            o,
            pltpu.make_async_remote_copy(
                src_ref=summed.at[o],
                dst_ref=arrived.at[band],
                send_sem=send_b.at[k],
                recv_sem=recv_b.at[band],
                device_id={"lev": to, "band": lev * 8 + o},
                device_id_type=MESH,
            ),
        )

    def post(k, carry):
        other, o, copy = owner_copy(k)

        @pl.when(other)
        def _():
            copy.start()

        @pl.when(jnp.logical_not(other))
        def _():
            pltpu.make_async_copy(summed.at[o], arrived.at[band], own_sem).start()

        return carry

    lax.fori_loop(0, BANDS, post, 0)

    def finish(k, carry):
        other, o, copy = owner_copy(k)

        @pl.when(other)
        def _():
            copy.wait_send()

        @pl.when(jnp.logical_not(other))
        def _():
            pltpu.make_async_copy(summed.at[o], arrived.at[band], own_sem).wait()

        source = lax.rem(band + k, BANDS)

        @pl.when(jnp.logical_not(inside & (k == 0)))
        def _():
            pltpu.make_async_remote_copy(
                src_ref=summed.at[o],
                dst_ref=arrived.at[source],
                send_sem=send_b.at[k],
                recv_sem=recv_b.at[source],
                device_id={"lev": group, "band": source},
                device_id_type=MESH,
            ).wait_recv()

        return carry

    lax.fori_loop(0, BANDS, finish, 0)
    for k in range(1, LEVS):
        level_copy(k).wait_send()

    for r in range(ROUNDS):
        line = arrived[:, r, :]
        for g in range(4):
            value = pltpu.roll(line, WIDTH - 32 * g, 1) if g else line
            fits_out[pl.ds(4 * r + g, BANDS, stride=CAP), :] = value


def owner_part(picked):
    vmem = pl.BlockSpec(memory_space=pltpu.VMEM)
    return pl.pallas_call(
        owner_kernel,
        out_shape=jax.ShapeDtypeStruct((BANDS * CAP, WIDTH), F32),
        in_specs=[vmem],
        out_specs=vmem,
        scratch_shapes=[
            pltpu.VMEM((LEVS, 8, 4, WIDTH), F32),
            pltpu.VMEM((8, 4, WIDTH), F32),
            pltpu.VMEM((BANDS, 4, WIDTH), F32),
            pltpu.SemaphoreType.DMA,
            pltpu.SemaphoreType.DMA((LEVS,)),
            pltpu.SemaphoreType.DMA((LEVS,)),
            pltpu.SemaphoreType.DMA((BANDS,)),
            pltpu.SemaphoreType.DMA((BANDS,)),
        ],
        compiler_params=pltpu.CompilerParams(
            collective_id=1, has_side_effects=True, vmem_limit_bytes=16 * 1024 * 1024
        ),
        name="owner_exchange",
    )(picked)


def local(spectra, legendre, wave_order, cand_block, cand_owner):
    waves = wave_order.reshape(K // WIDTH, WIDTH)
    coeffs = legendre_part(spectra.reshape(16, SLOTS, K), legendre, waves)
    vort, okubo, picked = grid_part(coeffs, waves, cand_owner, cand_block.reshape(1, CANDS))
    fits = owner_part(picked.reshape(BANDS, 4, WIDTH))[:, :20]

    def rows(field):
        shaped = field.reshape(TIMES, 64, 4, WIDTH).transpose(0, 2, 1, 3)
        return shaped.reshape(1, TIMES, 4, NLON)

    return rows(vort), rows(okubo), fits


def solution(mesh):
    placed = (
        P("lev", None, None, None, "band", None),
        P("band", None, None),
        P(),
        P("band"),
        P("band", None),
    )
    return jax.shard_map(
        local,
        mesh=mesh,
        in_specs=placed,
        out_specs=(P("lev", None, "band", None), P("lev", None, "band", None), P("band", None)),
        check_vma=False,
    )
```

```python
import math

import jax
import jax.numpy as jnp
import ml_dtypes
import numpy as np
from jax import lax
from jax.experimental import pallas as pl
from jax.experimental.pallas import tpu as pltpu
from jax.sharding import PartitionSpec as P

MESH = pl.DeviceIdType.MESH
F32 = jnp.float32
BF16 = jnp.bfloat16

BANDS = 32
LEVS = 4
SLOTS = 64
K = 2048
NLON = 8192
HALF = 64
TIMES = 4
GROUP = 16
PLANE = 8
PLANES = 4
MEMBERS = 128
WIDTH = 128
CANDS = 192
CAP = 12
ROUNDS = CAP // 4


def bf16_split(table):
    high = table.astype(np.float32).astype(ml_dtypes.bfloat16)
    low = (table - high.astype(np.float64)).astype(np.float32).astype(ml_dtypes.bfloat16)
    return high, low


def degree_table():
    n = np.arange(K, dtype=np.float32)
    inverse = np.where(n >= 1, np.float32(-1.0) / np.maximum(n * (n + 1), np.float32(1.0)), 0.0)
    table = np.zeros((8, K), np.float32)
    table[0] = inverse
    table[1] = np.where(np.arange(K) % 2 == 0, 1.0, -1.0)
    return table


def row_table():
    hy = math.pi / 4096.0
    j = np.arange(HALF)
    hx = np.cos((63.5 - j) * hy) * 2.0 * math.pi / NLON
    table = np.zeros((8, WIDTH), np.float64)
    table[0, :HALF] = table[0, HALF:] = 1.0 / (hx * hx)
    table[1, :HALF] = 1.0 / (4.0 * hx * hy)
    table[1, HALF:] = -1.0 / (4.0 * hx * hy)
    table[2] = 1.0 / (hy * hy)
    return table.astype(np.float32)


def first_table():
    h = np.arange(32)[:, None]
    x = np.arange(WIDTH)[None, :]
    angle = 2.0 * np.pi * ((h * x) % 128) / 128.0
    cos, sin = np.cos(angle), np.sin(angle)
    table = np.concatenate(
        [np.concatenate([cos, sin], 1), np.concatenate([-sin, cos], 1)], 0
    )
    high, low = bf16_split(table)
    return np.concatenate([high, low], 0)


def twiddle_table():
    low = np.arange(64)[:, None]
    x = np.arange(WIDTH)[None, :]
    angle = 2.0 * np.pi * (low * x) / NLON
    cos, sin = np.cos(angle), np.sin(angle)
    return np.stack([np.concatenate([cos, cos], 0), np.concatenate([sin, sin], 0)], 0).astype(
        np.float32
    )


def second_table():
    y = np.arange(64)[:, None]
    low = np.arange(64)[None, :]
    angle = 2.0 * np.pi * ((y * low) % 64) / 64.0
    cos, sin = np.cos(angle), -np.sin(angle)
    zero = np.zeros_like(cos)
    table = np.concatenate(
        [
            np.concatenate([cos, zero, sin, zero], 1),
            np.concatenate([zero, cos, zero, sin], 1),
        ],
        0,
    )
    high, low_part = bf16_split(table)
    return np.concatenate([high, low_part, high], 1)


ORDERS = ((0, 0), (1, 0), (0, 1), (2, 0), (1, 1), (0, 2), (3, 0), (2, 1), (1, 2), (0, 3))


def ortho_values(count):
    u = np.arange(count, dtype=np.float64) - (count - 1) / 2.0
    q = np.stack(
        [
            np.ones_like(u),
            u,
            u * u - (count * count - 1) / 12.0,
            u * u * u - (3 * count * count - 7) / 20.0 * u,
        ],
        0,
    )
    return q / np.sqrt(np.sum(q * q, 1, keepdims=True))


def fit_tables():
    across, upward = ortho_values(WIDTH), ortho_values(4)
    columns = np.stack([across[a] for a, _ in ORDERS], 1)
    table = np.zeros((256, 32), np.float64)
    table[:128, 0:10] = columns
    table[128:, 10:20] = columns
    high, low = bf16_split(table)
    both = np.zeros((256, 128), high.dtype)
    both[:, 0:32] = high
    both[:, 32:64] = low
    rows = np.zeros((8, 128), np.float32)
    for r in range(4):
        line = [upward[b][r] / 4.0 for _, b in ORDERS]
        rows[r, 0:10] = line
        rows[r, 10:20] = line
    return both, rows


def column_of(row):
    return jnp.broadcast_to(row, (WIDTH, WIDTH)).T


def greet_all(barrier, rank):
    def greet(k, carry):
        other = lax.rem(rank + k, MEMBERS)
        pl.semaphore_signal(
            barrier,
            inc=1,
            device_id={"lev": other // BANDS, "band": lax.rem(other, BANDS)},
            device_id_type=MESH,
        )
        return carry

    lax.fori_loop(1, MEMBERS, greet, 0)


def legendre_sums(first, waits, spec, leg, degree_ref, columns, scaled, factor, sums):
    spec_wait, leg_wait = waits
    lane = lax.broadcasted_iota(jnp.int32, (1, K), 1).astype(F32)

    def one_group(g, carry):
        spec_wait(g)
        start = pl.multiple_of(g * GROUP, GROUP)
        own = columns[pl.ds(pl.multiple_of(first + start, GROUP), GROUP), :]
        own = jnp.concatenate([own] * (K // WIDTH), axis=1)
        factor[...] = jnp.where(lane >= own, degree_ref[0:1, :], 0.0)

        def scale(q, inner):
            part = spec[q, pl.ds(start, GROUP), :].astype(F32) * factor[...]
            window = pl.ds(pl.multiple_of(q * GROUP, GROUP), GROUP)
            for tile in range(K // WIDTH):
                scaled[tile, window, :] = part[:, tile * WIDTH : (tile + 1) * WIDTH]
            return inner

        lax.fori_loop(0, 16, scale, 0)

        def one_slot(i, inner):
            even = jnp.concatenate(
                [scaled[tile, pl.ds(i, 16, stride=GROUP), :] for tile in range(K // WIDTH)],
                axis=1,
            )
            odd = even * degree_ref[1:2, :]
            both = jnp.concatenate([even.astype(BF16), odd.astype(BF16)], axis=0)
            result = lax.dot_general(
                both,
                leg[start + i],
                (((1,), (1,)), ((), ())),
                preferred_element_type=F32,
            )
            result = result.astype(BF16).astype(F32)
            sums[pl.ds(pl.multiple_of((start + i) * 16, 16), 16), :] = jnp.concatenate(
                [result[:16], result[16:]], axis=1
            )
            return inner

        for part in range(GROUP // LEG_PART):
            leg_wait(g * (GROUP // LEG_PART) + part)
            lax.fori_loop(
                part * LEG_PART, (part + 1) * LEG_PART, one_slot, 0, unroll=LEG_PART
            )
        return carry

    lax.fori_loop(0, SLOTS // GROUP, one_group, 0)


LEG_PART = 8


def combine_rows(first, columns, rows_ref, sums, turned):
    m = columns[pl.ds(first, SLOTS), :]
    lanes = lax.broadcasted_iota(jnp.int32, (SLOTS, WIDTH), 1)
    half_m = jnp.floor(m * 0.5)
    parity = 1.0 - 2.0 * (m - 2.0 * half_m)
    weight = jnp.where(m == 0.0, 1.0, 2.0)
    sign = jnp.where(lanes >= HALF, parity, 1.0) * weight
    x = m * (math.pi / NLON)
    x2 = x * x
    sin = x * (
        1.0
        + x2 * (-1.0 / 6 + x2 * (1.0 / 120 + x2 * (-1.0 / 5040 + x2 * (1.0 / 362880))))
    )
    cos = 1.0 + x2 * (
        -0.5
        + x2 * (1.0 / 24 + x2 * (-1.0 / 720 + x2 * (1.0 / 40320 - x2 * (1.0 / 3628800))))
    )
    xx = -4.0 * sin * sin * rows_ref[0:1, :]
    xy = 2.0 * (2.0 * sin * cos) * rows_ref[1:2, :]
    yy = rows_ref[2:3, :]
    first_lane = (lanes == 0) | (lanes == HALF)
    last_lane = (lanes == HALF - 1) | (lanes == WIDTH - 1)

    def one_time(t, carry):
        def pieces(q):
            c = sums[pl.ds(t * 4 + q, SLOTS, stride=16), :] * sign
            before = jnp.where(first_lane, 0.0, pltpu.roll(c, 1, 1))
            after = jnp.where(last_lane, pltpu.roll(c, HALF, 1), pltpu.roll(c, WIDTH - 1, 1))
            return c * xx, (before + after - 2.0 * c) * yy, (before - after) * xy

        pr_xx, pr_yy, pr_xy = pieces(0)
        pi_xx, pi_yy, pi_xy = pieces(1)
        cr_xx, cr_yy, cr_xy = pieces(2)
        ci_xx, ci_yy, ci_xy = pieces(3)
        a = (pr_xx - ci_xy, pi_xx + cr_xy)
        b = (-ci_xy - pr_yy, cr_xy - pi_yy)
        normal = (2.0 * pi_xy + cr_xx - cr_yy, -2.0 * pr_xy + ci_xx - ci_yy)
        for q, pair in enumerate((a, b, normal)):
            block = jnp.concatenate(pair, axis=0).T
            turned[q, pl.ds(t, WIDTH, stride=4), :] = block
        return carry

    lax.fori_loop(0, TIMES, one_time, 0, unroll=4)


def build_onehot(wave_ref, onehot):
    lane = lax.broadcasted_iota(jnp.int32, (WIDTH, WIDTH), 1).astype(F32)

    def one_block(j, carry):
        column = column_of(wave_ref[pl.ds(j, 1), :].astype(F32))
        rows = pl.ds(pl.multiple_of(j * WIDTH, WIDTH), WIDTH)
        for tile in range(K // WIDTH):
            onehot[rows, tile * WIDTH : (tile + 1) * WIDTH] = jnp.where(
                column == lane + float(tile * WIDTH), 1.0, 0.0
            ).astype(BF16)
        return carry

    lax.fori_loop(0, K // WIDTH, one_block, 0)


def candidate_tables(owner_ref, block_ref, goal, named):
    owner = owner_ref[...]
    owned = jnp.where(
        lax.broadcasted_iota(jnp.int32, (BANDS, CANDS), 0) == owner, 1.0, 0.0
    )
    order = jnp.where(
        lax.broadcasted_iota(jnp.int32, (CANDS, CANDS), 0)
        < lax.broadcasted_iota(jnp.int32, (CANDS, CANDS), 1),
        1.0,
        0.0,
    ).astype(BF16)
    earlier = jnp.dot(owned.astype(BF16), order, preferred_element_type=F32)
    slot = jnp.sum(earlier * owned, axis=0, keepdims=True).astype(jnp.int32)
    target = (slot & 3) * WIDTH + owner * 4 + (slot >> 2)
    goal[...] = jnp.where(
        lax.broadcasted_iota(jnp.int32, (4 * WIDTH, CANDS), 0) == target, 1.0, 0.0
    ).astype(BF16)
    cells = jnp.where(
        lax.broadcasted_iota(jnp.int32, (256, CANDS), 0) == block_ref[...], 1.0, 0.0
    )
    named[...] = cells.T.astype(BF16)


def join_plane(plane, coeffs, ordered_in):
    pick = lax.broadcasted_iota(jnp.int32, (48, WIDTH), 1) < 64
    for j in range(PLANE // 2):
        a = coeffs[plane * PLANE + 2 * j].astype(F32)
        b = coeffs[plane * PLANE + 2 * j + 1].astype(F32)
        real = jnp.where(pick, a, pltpu.roll(b, 64, 1))
        imag = jnp.where(pick, pltpu.roll(a, 64, 1), b)
        ordered_in[0:48, j * WIDTH : (j + 1) * WIDTH] = real.astype(BF16)
        ordered_in[48:96, j * WIDTH : (j + 1) * WIDTH] = imag.astype(BF16)


def order_plane(plane, number, ordered_in, onehot, ordered, spread):
    pick = lax.broadcasted_iota(jnp.int32, (8, WIDTH), 1) < 64
    depth = PLANE * SLOTS
    rows = pl.ds(pl.multiple_of(plane * depth, depth), depth)
    for j in range(8):
        at = slice(256 * j, 256 * (j + 1))
        part = jnp.dot(ordered_in[...], onehot[rows, at], preferred_element_type=F32)
        if number > 0:
            part = part + ordered[:, at]
        if number < PLANES - 1:
            ordered[:, at] = part
            continue
        for tile in range(2):
            h = 4 * j + 2 * tile
            for c in range(2):
                for f in range(3):
                    at = c * 48 + f * 16
                    a = part[at : at + 8, tile * WIDTH : (tile + 1) * WIDTH]
                    b = part[at + 8 : at + 16, tile * WIDTH : (tile + 1) * WIDTH]
                    to = c * 24 + f * 8
                    spread[h * 48 + to : h * 48 + to + 8, :] = jnp.where(
                        pick, a, pltpu.roll(b, 64, 1)
                    )
                    spread[(h + 1) * 48 + to : (h + 1) * 48 + to + 8, :] = jnp.where(
                        pick, pltpu.roll(a, 64, 1), b
                    )


def synthesis(band, spread, tables, vort_out, okubo_out, table):
    first_ref, twiddle_ref, second_ref, fit_ref, fit_rows = tables
    southern = band >= BANDS // 2
    for t in range(TIMES):
        for rr in range(2):
            row_low = jnp.where(southern, 3 - rr, rr)
            row_high = jnp.where(southern, 1 - rr, 2 + rr)
            parts = []
            for f in range(3):
                i = f * 8 + rr * 4 + t
                c = jnp.concatenate(
                    [spread[pl.ds(i, 32, stride=48), :], spread[pl.ds(24 + i, 32, stride=48), :]],
                    axis=0,
                ).T.astype(BF16)
                z = jnp.dot(
                    jnp.concatenate([c, c], axis=1), first_ref[...], preferred_element_type=F32
                )
                zr, zi = z[:, :WIDTH], z[:, WIDTH:]
                tc, ts = twiddle_ref[0], twiddle_ref[1]
                parts.append(jnp.concatenate([zr * tc - zi * ts, zr * ts + zi * tc], axis=0))
            z = jnp.concatenate(parts, axis=1)
            high = z.astype(BF16)
            low = (z - high.astype(F32)).astype(BF16)
            grid = jnp.dot(
                second_ref[...],
                jnp.concatenate([high, high, low], axis=0),
                preferred_element_type=F32,
            )
            a = grid[:, :WIDTH]
            b = grid[:, WIDTH : 2 * WIDTH]
            normal = grid[:, 2 * WIDTH :]
            vort = a - b
            okubo = normal * normal + 4.0 * (a * b)
            vort_out[t, pl.ds(row_low, 64, stride=4), :] = vort[:64]
            vort_out[t, pl.ds(row_high, 64, stride=4), :] = vort[64:]
            okubo_out[t, pl.ds(row_low, 64, stride=4), :] = okubo[:64]
            okubo_out[t, pl.ds(row_high, 64, stride=4), :] = okubo[64:]
            both = jnp.concatenate([vort, okubo], axis=1)
            high = both.astype(BF16)
            low = (both - high.astype(F32)).astype(BF16)
            from_high = jnp.dot(high, fit_ref[...], preferred_element_type=F32)
            from_low = jnp.dot(low, fit_ref[...], preferred_element_type=F32)
            fits = from_high + pltpu.roll(from_high, WIDTH - 32, 1) + from_low
            fits = (
                fits[:64] * fit_rows[pl.ds(row_low, 1), :]
                + fits[64:] * fit_rows[pl.ds(row_high, 1), :]
            )
            if rr == 0:
                table[t * 64 : (t + 1) * 64, :] = fits
            else:
                table[t * 64 : (t + 1) * 64, :] += fits


def pick_candidates(goal, named, table):
    values = table[...]
    high = values.astype(BF16).astype(F32)
    low = values - high
    chosen = jnp.dot(
        named[...],
        jnp.concatenate([high, low], axis=1).astype(BF16),
        preferred_element_type=F32,
    )
    total = jnp.zeros((WIDTH, 2 * WIDTH), F32)
    for g in range(4):
        high = chosen[:, :WIDTH]
        low = chosen[:, WIDTH:]
        if g:
            high = pltpu.roll(high, 32 * g, 1)
            low = pltpu.roll(low, 32 * g, 1)
        total += jnp.dot(
            goal[g * WIDTH : (g + 1) * WIDTH, :],
            jnp.concatenate([high, low], axis=1).astype(BF16),
            preferred_element_type=F32,
        )
    return total[:, :WIDTH] + total[:, WIDTH:]


def whole_kernel(
    spec_hbm,
    leg_hbm,
    wave_ref,
    owner_ref,
    block_ref,
    degree_ref,
    rows_ref,
    first_ref,
    twiddle_ref,
    second_ref,
    fit_ref,
    fit_rows,
    vort_hbm,
    okubo_hbm,
    fits_out,
    spec,
    leg,
    scaled,
    factor,
    columns,
    sums,
    turned,
    send,
    recv,
    onehot,
    goal,
    named,
    ordered_in,
    ordered,
    spread,
    vort,
    okubo,
    table,
    outgoing,
    arrived,
    lines,
    spec_sem,
    leg_sem,
    out_sem,
    send_sem,
    recv_sem,
    send_fit,
    recv_fit,
):
    lev = lax.axis_index("lev")
    me = lax.axis_index("band")
    rank = lev * BANDS + me

    def spec_copy(g):
        window = pl.ds(pl.multiple_of(g * GROUP, GROUP), GROUP)
        return pltpu.make_async_copy(
            spec_hbm.at[:, window, :], spec.at[:, window, :], spec_sem.at[g]
        )

    def leg_copy(g):
        window = pl.ds(g * LEG_PART, LEG_PART)
        return pltpu.make_async_copy(leg_hbm.at[window], leg.at[window], leg_sem.at[g])

    for g in range(SLOTS // GROUP):
        spec_copy(g).start()
        for part in range(GROUP // LEG_PART):
            leg_copy(g * (GROUP // LEG_PART) + part).start()

    barrier = pltpu.get_barrier_semaphore()
    greet_all(barrier, rank)

    columns[...] = column_of(wave_ref[pl.ds(me // 2, 1), :].astype(F32))
    first = pl.multiple_of(lax.rem(me, 2) * SLOTS, SLOTS)
    waits = (lambda g: spec_copy(g).wait(), lambda g: leg_copy(g).wait())
    legendre_sums(first, waits, spec, leg, degree_ref, columns, scaled, factor, sums)
    combine_rows(first, columns, rows_ref, sums, turned)

    pl.semaphore_wait(barrier, MEMBERS - 1)

    my_plane = me // PLANE
    my_place = lax.rem(me, PLANE)

    def fill(d):
        p = jnp.where(d < BANDS // 2, d, BANDS + BANDS // 2 - 1 - d)
        for q in range(3):
            send[d, 16 * q : 16 * q + 16, :] = turned[
                q, pl.ds(pl.multiple_of(p * 16, 16), 16), :
            ].astype(BF16)

    def message(d):
        return pltpu.make_async_remote_copy(
            src_ref=send.at[d],
            dst_ref=recv.at[me],
            send_sem=send_sem.at[d],
            recv_sem=recv_sem.at[me],
            device_id={"band": d},
            device_id_type=MESH,
        )

    def arrival(source):
        return pltpu.make_async_remote_copy(
            src_ref=send.at[source],
            dst_ref=recv.at[source],
            send_sem=send_sem.at[source],
            recv_sem=recv_sem.at[source],
            device_id={"band": source},
            device_id_type=MESH,
        )

    shifts = (0, 1, 3, 2)
    for shift in shifts:
        plane = lax.rem(my_plane + shift, PLANES)

        def post(k, carry, plane=plane):
            d = plane * PLANE + lax.rem(my_place + k, PLANE)
            fill(d)
            message(d).start()
            return carry

        lax.fori_loop(0 if shift else 1, PLANE, post, 0)
    fill(me)
    recv[me] = send[me]

    build_onehot(wave_ref, onehot)
    candidate_tables(owner_ref, block_ref, goal, named)

    for number, shift in enumerate(shifts):
        plane = lax.rem(my_plane + PLANES - shift, PLANES)

        def take(k, carry, plane=plane):
            arrival(plane * PLANE + lax.rem(my_place + k, PLANE)).wait_recv()
            return carry

        lax.fori_loop(0 if shift else 1, PLANE, take, 0)
        join_plane(plane, recv, ordered_in)
        order_plane(plane, number, ordered_in, onehot, ordered, spread)

    tables = (first_ref, twiddle_ref, second_ref, fit_ref, fit_rows)
    synthesis(me, spread, tables, vort, okubo, table)
    vort_copy = pltpu.make_async_copy(vort, vort_hbm, out_sem.at[0])
    okubo_copy = pltpu.make_async_copy(okubo, okubo_hbm, out_sem.at[1])
    vort_copy.start()
    okubo_copy.start()

    outgoing[...] = pick_candidates(goal, named, table).reshape(BANDS, 4, WIDTH)

    def fit_copy(other, place):
        return pltpu.make_async_remote_copy(
            src_ref=outgoing.at[lax.rem(other, BANDS)],
            dst_ref=arrived.at[place],
            send_sem=send_fit.at[other],
            recv_sem=recv_fit.at[place],
            device_id={"lev": other // BANDS, "band": lax.rem(other, BANDS)},
            device_id_type=MESH,
        )

    def post_fit(k, carry):
        fit_copy(lax.rem(rank + k, MEMBERS), rank).start()
        return carry

    lax.fori_loop(1, MEMBERS, post_fit, 0)
    arrived[rank] = outgoing[me]

    def take_fit(k, carry):
        other = lax.rem(rank + k, MEMBERS)
        fit_copy(other, other).wait_recv()
        return carry

    lax.fori_loop(1, MEMBERS, take_fit, 0)

    for r in range(ROUNDS):
        line = (arrived[0:32, r, :] + arrived[32:64, r, :]) + (
            arrived[64:96, r, :] + arrived[96:128, r, :]
        )
        for g in range(4):
            value = pltpu.roll(line, WIDTH - 32 * g, 1) if g else line
            lines[pl.ds(4 * r + g, BANDS, stride=CAP), :] = value
    fits_out[...] = lines[...].T[:20, :]

    def sent(d, carry):
        @pl.when(d != me)
        def _():
            message(d).wait_send()

        return carry

    lax.fori_loop(0, BANDS, sent, 0)

    def sent_fit(k, carry):
        fit_copy(lax.rem(rank + k, MEMBERS), rank).wait_send()
        return carry

    lax.fori_loop(1, MEMBERS, sent_fit, 0)
    vort_copy.wait()
    okubo_copy.wait()


def whole(spectra, legendre, waves, owner, block):
    vmem = pl.BlockSpec(memory_space=pltpu.VMEM)
    hbm = pl.BlockSpec(memory_space=pl.ANY)
    fit_table, fit_rows = fit_tables()
    grid = jax.ShapeDtypeStruct((TIMES, 256, WIDTH), F32)
    return pl.pallas_call(
        whole_kernel,
        out_shape=(grid, grid, jax.ShapeDtypeStruct((20, BANDS * CAP), F32)),
        in_specs=[hbm, hbm] + [vmem] * 10,
        out_specs=(hbm, hbm, vmem),
        scratch_shapes=[
            pltpu.VMEM((16, SLOTS, K), BF16),
            pltpu.VMEM((SLOTS, HALF, K), BF16),
            pltpu.VMEM((K // WIDTH, 16 * GROUP, WIDTH), F32),
            pltpu.VMEM((GROUP, K), F32),
            pltpu.VMEM((WIDTH, WIDTH), F32),
            pltpu.VMEM((SLOTS * 16, WIDTH), F32),
            pltpu.VMEM((3, 4 * WIDTH, WIDTH), F32),
            pltpu.VMEM((BANDS, 48, WIDTH), BF16),
            pltpu.VMEM((BANDS, 48, WIDTH), BF16),
            pltpu.VMEM((K, K), BF16),
            pltpu.VMEM((4 * WIDTH, CANDS), BF16),
            pltpu.VMEM((CANDS, 256), BF16),
            pltpu.VMEM((96, PLANE * SLOTS), BF16),
            pltpu.VMEM((96, K), F32),
            pltpu.VMEM((32 * 48, WIDTH), F32),
            pltpu.VMEM((TIMES, 256, WIDTH), F32),
            pltpu.VMEM((TIMES, 256, WIDTH), F32),
            pltpu.VMEM((256, WIDTH), F32),
            pltpu.VMEM((BANDS, 4, WIDTH), F32),
            pltpu.VMEM((MEMBERS, 4, WIDTH), F32),
            pltpu.VMEM((BANDS * CAP, WIDTH), F32),
            pltpu.SemaphoreType.DMA((SLOTS // GROUP,)),
            pltpu.SemaphoreType.DMA((SLOTS // LEG_PART,)),
            pltpu.SemaphoreType.DMA((2,)),
            pltpu.SemaphoreType.DMA((BANDS,)),
            pltpu.SemaphoreType.DMA((BANDS,)),
            pltpu.SemaphoreType.DMA((MEMBERS,)),
            pltpu.SemaphoreType.DMA((MEMBERS,)),
        ],
        compiler_params=pltpu.CompilerParams(
            collective_id=0, has_side_effects=True, vmem_limit_bytes=56 * 1024 * 1024
        ),
        name="spectral_analysis",
    )(
        spectra,
        legendre,
        waves,
        owner,
        block,
        degree_table(),
        row_table(),
        first_table(),
        twiddle_table(),
        second_table(),
        fit_table,
        fit_rows,
    )


def local(spectra, legendre, wave_order, cand_block, cand_owner):
    vort, okubo, fits = whole(
        spectra.reshape(16, SLOTS, K),
        legendre,
        wave_order.reshape(K // WIDTH, WIDTH),
        cand_owner.reshape(1, CANDS),
        cand_block.reshape(1, CANDS),
    )

    def rows(field):
        shaped = field.reshape(TIMES, 64, 4, WIDTH).transpose(0, 2, 1, 3)
        return shaped.reshape(1, TIMES, 4, NLON)

    return rows(vort), rows(okubo), fits.T


def solution(mesh):
    placed = (
        P("lev", None, None, None, "band", None),
        P("band", None, None),
        P(),
        P("band"),
        P("band", None),
    )
    return jax.shard_map(
        local,
        mesh=mesh,
        in_specs=placed,
        out_specs=(P("lev", None, "band", None), P("lev", None, "band", None), P("band", None)),
        check_vma=False,
    )
```

```python
import math

import jax
import jax.numpy as jnp
import ml_dtypes
import numpy as np
from jax import lax
from jax.experimental import pallas as pl
from jax.experimental.pallas import tpu as pltpu
from jax.sharding import PartitionSpec as P

MESH = pl.DeviceIdType.MESH
F32 = jnp.float32
BF16 = jnp.bfloat16

BANDS = 32
LEVS = 4
SLOTS = 64
K = 2048
NLON = 8192
HALF = 64
TIMES = 4
GROUP = 16
PLANE = 8
PLANES = 4
MEMBERS = 128
WIDTH = 128
CANDS = 192
CAP = 12
ROUNDS = CAP // 4


def bf16_split(table):
    high = table.astype(np.float32).astype(ml_dtypes.bfloat16)
    low = (table - high.astype(np.float64)).astype(np.float32).astype(ml_dtypes.bfloat16)
    return high, low


def degree_table():
    n = np.arange(K, dtype=np.float32)
    inverse = np.where(n >= 1, np.float32(-1.0) / np.maximum(n * (n + 1), np.float32(1.0)), 0.0)
    table = np.zeros((8, K), np.float32)
    table[0] = inverse
    table[1] = np.where(np.arange(K) % 2 == 0, 1.0, -1.0)
    return table


def row_table():
    hy = math.pi / 4096.0
    j = np.arange(HALF)
    hx = np.cos((63.5 - j) * hy) * 2.0 * math.pi / NLON
    table = np.zeros((8, WIDTH), np.float64)
    table[0, :HALF] = table[0, HALF:] = 1.0 / (hx * hx)
    table[1, :HALF] = 1.0 / (4.0 * hx * hy)
    table[1, HALF:] = -1.0 / (4.0 * hx * hy)
    table[2] = 1.0 / (hy * hy)
    return table.astype(np.float32)


def first_table():
    h = np.arange(32)[:, None]
    x = np.arange(WIDTH)[None, :]
    angle = 2.0 * np.pi * ((h * x) % 128) / 128.0
    cos, sin = np.cos(angle), np.sin(angle)
    table = np.concatenate(
        [np.concatenate([cos, sin], 1), np.concatenate([-sin, cos], 1)], 0
    )
    high, low = bf16_split(table)
    return np.concatenate([high, low], 0)


def twiddle_table():
    low = np.arange(64)[:, None]
    x = np.arange(WIDTH)[None, :]
    angle = 2.0 * np.pi * (low * x) / NLON
    cos, sin = np.cos(angle), np.sin(angle)
    return np.stack([np.concatenate([cos, cos], 0), np.concatenate([sin, sin], 0)], 0).astype(
        np.float32
    )


def second_table():
    y = np.arange(64)[:, None]
    low = np.arange(64)[None, :]
    angle = 2.0 * np.pi * ((y * low) % 64) / 64.0
    cos, sin = np.cos(angle), -np.sin(angle)
    zero = np.zeros_like(cos)
    table = np.concatenate(
        [
            np.concatenate([cos, zero, sin, zero], 1),
            np.concatenate([zero, cos, zero, sin], 1),
        ],
        0,
    )
    high, low_part = bf16_split(table)
    return np.concatenate([high, low_part, high], 1)


ORDERS = ((0, 0), (1, 0), (0, 1), (2, 0), (1, 1), (0, 2), (3, 0), (2, 1), (1, 2), (0, 3))


def ortho_values(count):
    u = np.arange(count, dtype=np.float64) - (count - 1) / 2.0
    q = np.stack(
        [
            np.ones_like(u),
            u,
            u * u - (count * count - 1) / 12.0,
            u * u * u - (3 * count * count - 7) / 20.0 * u,
        ],
        0,
    )
    return q / np.sqrt(np.sum(q * q, 1, keepdims=True))


def fit_tables():
    across, upward = ortho_values(WIDTH), ortho_values(4)
    columns = np.stack([across[a] for a, _ in ORDERS], 1)
    table = np.zeros((256, 32), np.float64)
    table[:128, 0:10] = columns
    table[128:, 10:20] = columns
    high, low = bf16_split(table)
    both = np.zeros((256, 128), high.dtype)
    both[:, 0:32] = high
    both[:, 32:64] = low
    rows = np.zeros((8, 128), np.float32)
    for r in range(4):
        line = [upward[b][r] / 4.0 for _, b in ORDERS]
        rows[r, 0:10] = line
        rows[r, 10:20] = line
    return both, rows


def column_of(row):
    return jnp.broadcast_to(row, (WIDTH, WIDTH)).T


def greet_peers(semaphore, lev, me):
    for k in range(1, LEVS):
        pl.semaphore_signal(
            semaphore,
            inc=1,
            device_id={"lev": lax.rem(lev + k, LEVS), "band": me},
            device_id_type=MESH,
        )


def greet_band(semaphore, lev, me):
    def greet(k, carry):
        pl.semaphore_signal(
            semaphore,
            inc=1,
            device_id={"lev": lev, "band": lax.rem(me + k, BANDS)},
            device_id_type=MESH,
        )
        return carry

    lax.fori_loop(1, BANDS, greet, 0)


def legendre_sums(first, waits, spec, leg, degree_ref, columns, scaled, factor, sums):
    spec_wait, leg_wait = waits
    lane = lax.broadcasted_iota(jnp.int32, (1, K), 1).astype(F32)

    def one_group(g, carry):
        spec_wait(g)
        start = pl.multiple_of(g * GROUP, GROUP)
        own = columns[pl.ds(pl.multiple_of(first + start, GROUP), GROUP), :]
        own = jnp.concatenate([own] * (K // WIDTH), axis=1)
        factor[...] = jnp.where(lane >= own, degree_ref[0:1, :], 0.0)

        def scale(q, inner):
            part = spec[q, pl.ds(start, GROUP), :].astype(F32) * factor[...]
            window = pl.ds(pl.multiple_of(q * GROUP, GROUP), GROUP)
            for tile in range(K // WIDTH):
                scaled[tile, window, :] = part[:, tile * WIDTH : (tile + 1) * WIDTH]
            return inner

        lax.fori_loop(0, 16, scale, 0)

        def one_slot(i, inner):
            even = jnp.concatenate(
                [scaled[tile, pl.ds(i, 16, stride=GROUP), :] for tile in range(K // WIDTH)],
                axis=1,
            )
            odd = even * degree_ref[1:2, :]
            both = jnp.concatenate([even.astype(BF16), odd.astype(BF16)], axis=0)
            result = lax.dot_general(
                both,
                leg[start + i],
                (((1,), (1,)), ((), ())),
                preferred_element_type=F32,
            )
            result = result.astype(BF16).astype(F32)
            sums[pl.ds(pl.multiple_of((start + i) * 16, 16), 16), :] = jnp.concatenate(
                [result[:16], result[16:]], axis=1
            )
            return inner

        for part in range(GROUP // LEG_PART):
            leg_wait(g * (GROUP // LEG_PART) + part)
            lax.fori_loop(
                part * LEG_PART, (part + 1) * LEG_PART, one_slot, 0, unroll=LEG_PART
            )
        return carry

    lax.fori_loop(0, SLOTS // GROUP, one_group, 0)


LEG_PART = 8


def combine_rows(first, columns, rows_ref, sums, turned):
    m = columns[pl.ds(first, SLOTS), :]
    lanes = lax.broadcasted_iota(jnp.int32, (SLOTS, WIDTH), 1)
    half_m = jnp.floor(m * 0.5)
    parity = 1.0 - 2.0 * (m - 2.0 * half_m)
    weight = jnp.where(m == 0.0, 1.0, 2.0)
    sign = jnp.where(lanes >= HALF, parity, 1.0) * weight
    x = m * (math.pi / NLON)
    x2 = x * x
    sin = x * (
        1.0
        + x2 * (-1.0 / 6 + x2 * (1.0 / 120 + x2 * (-1.0 / 5040 + x2 * (1.0 / 362880))))
    )
    cos = 1.0 + x2 * (
        -0.5
        + x2 * (1.0 / 24 + x2 * (-1.0 / 720 + x2 * (1.0 / 40320 - x2 * (1.0 / 3628800))))
    )
    xx = -4.0 * sin * sin * rows_ref[0:1, :]
    xy = 2.0 * (2.0 * sin * cos) * rows_ref[1:2, :]
    yy = rows_ref[2:3, :]
    first_lane = (lanes == 0) | (lanes == HALF)
    last_lane = (lanes == HALF - 1) | (lanes == WIDTH - 1)

    def one_time(t, carry):
        def pieces(q):
            c = sums[pl.ds(t * 4 + q, SLOTS, stride=16), :] * sign
            before = jnp.where(first_lane, 0.0, pltpu.roll(c, 1, 1))
            after = jnp.where(last_lane, pltpu.roll(c, HALF, 1), pltpu.roll(c, WIDTH - 1, 1))
            return c * xx, (before + after - 2.0 * c) * yy, (before - after) * xy

        pr_xx, pr_yy, pr_xy = pieces(0)
        pi_xx, pi_yy, pi_xy = pieces(1)
        cr_xx, cr_yy, cr_xy = pieces(2)
        ci_xx, ci_yy, ci_xy = pieces(3)
        a = (pr_xx - ci_xy, pi_xx + cr_xy)
        b = (-ci_xy - pr_yy, cr_xy - pi_yy)
        normal = (2.0 * pi_xy + cr_xx - cr_yy, -2.0 * pr_xy + ci_xx - ci_yy)
        for q, pair in enumerate((a, b, normal)):
            block = jnp.concatenate(pair, axis=0).T
            turned[q, pl.ds(t, WIDTH, stride=4), :] = block
        return carry

    lax.fori_loop(0, TIMES, one_time, 0, unroll=4)


def build_onehot(wave_ref, onehot):
    lane = lax.broadcasted_iota(jnp.int32, (WIDTH, WIDTH), 1).astype(F32)

    def one_block(j, carry):
        column = column_of(wave_ref[pl.ds(j, 1), :].astype(F32))
        rows = pl.ds(pl.multiple_of(j * WIDTH, WIDTH), WIDTH)
        for tile in range(K // WIDTH):
            onehot[rows, tile * WIDTH : (tile + 1) * WIDTH] = jnp.where(
                column == lane + float(tile * WIDTH), 1.0, 0.0
            ).astype(BF16)
        return carry

    lax.fori_loop(0, K // WIDTH, one_block, 0)


def candidate_tables(owner_ref, block_ref, goal, named):
    owner = owner_ref[...]
    owned = jnp.where(
        lax.broadcasted_iota(jnp.int32, (BANDS, CANDS), 0) == owner, 1.0, 0.0
    )
    order = jnp.where(
        lax.broadcasted_iota(jnp.int32, (CANDS, CANDS), 0)
        < lax.broadcasted_iota(jnp.int32, (CANDS, CANDS), 1),
        1.0,
        0.0,
    ).astype(BF16)
    earlier = jnp.dot(owned.astype(BF16), order, preferred_element_type=F32)
    slot = jnp.sum(earlier * owned, axis=0, keepdims=True).astype(jnp.int32)
    target = (slot & 3) * WIDTH + owner * 4 + (slot >> 2)
    goal[...] = jnp.where(
        lax.broadcasted_iota(jnp.int32, (4 * WIDTH, CANDS), 0) == target, 1.0, 0.0
    ).astype(BF16)
    cells = jnp.where(
        lax.broadcasted_iota(jnp.int32, (256, CANDS), 0) == block_ref[...], 1.0, 0.0
    )
    named[...] = cells.T.astype(BF16)


def join_plane(plane, coeffs, ordered_in):
    pick = lax.broadcasted_iota(jnp.int32, (48, WIDTH), 1) < 64
    for j in range(PLANE // 2):
        a = coeffs[plane * PLANE + 2 * j].astype(F32)
        b = coeffs[plane * PLANE + 2 * j + 1].astype(F32)
        real = jnp.where(pick, a, pltpu.roll(b, 64, 1))
        imag = jnp.where(pick, pltpu.roll(a, 64, 1), b)
        ordered_in[0:48, j * WIDTH : (j + 1) * WIDTH] = real.astype(BF16)
        ordered_in[48:96, j * WIDTH : (j + 1) * WIDTH] = imag.astype(BF16)


def order_plane(plane, number, ordered_in, onehot, ordered, spread):
    pick = lax.broadcasted_iota(jnp.int32, (8, WIDTH), 1) < 64
    depth = PLANE * SLOTS
    rows = pl.ds(pl.multiple_of(plane * depth, depth), depth)
    for j in range(8):
        at = slice(256 * j, 256 * (j + 1))
        part = jnp.dot(ordered_in[...], onehot[rows, at], preferred_element_type=F32)
        if number > 0:
            part = part + ordered[:, at]
        if number < PLANES - 1:
            ordered[:, at] = part
            continue
        for tile in range(2):
            h = 4 * j + 2 * tile
            for c in range(2):
                for f in range(3):
                    at = c * 48 + f * 16
                    a = part[at : at + 8, tile * WIDTH : (tile + 1) * WIDTH]
                    b = part[at + 8 : at + 16, tile * WIDTH : (tile + 1) * WIDTH]
                    to = c * 24 + f * 8
                    spread[h * 48 + to : h * 48 + to + 8, :] = jnp.where(
                        pick, a, pltpu.roll(b, 64, 1)
                    )
                    spread[(h + 1) * 48 + to : (h + 1) * 48 + to + 8, :] = jnp.where(
                        pick, pltpu.roll(a, 64, 1), b
                    )


def synthesis(band, spread, tables, vort_out, okubo_out, table):
    first_ref, twiddle_ref, second_ref, fit_ref, fit_rows = tables
    southern = band >= BANDS // 2
    for t in range(TIMES):
        for rr in range(2):
            row_low = jnp.where(southern, 3 - rr, rr)
            row_high = jnp.where(southern, 1 - rr, 2 + rr)
            parts = []
            for f in range(3):
                i = f * 8 + rr * 4 + t
                c = jnp.concatenate(
                    [spread[pl.ds(i, 32, stride=48), :], spread[pl.ds(24 + i, 32, stride=48), :]],
                    axis=0,
                ).T.astype(BF16)
                z = jnp.dot(
                    jnp.concatenate([c, c], axis=1), first_ref[...], preferred_element_type=F32
                )
                zr, zi = z[:, :WIDTH], z[:, WIDTH:]
                tc, ts = twiddle_ref[0], twiddle_ref[1]
                parts.append(jnp.concatenate([zr * tc - zi * ts, zr * ts + zi * tc], axis=0))
            z = jnp.concatenate(parts, axis=1)
            high = z.astype(BF16)
            low = (z - high.astype(F32)).astype(BF16)
            grid = jnp.dot(
                second_ref[...],
                jnp.concatenate([high, high, low], axis=0),
                preferred_element_type=F32,
            )
            a = grid[:, :WIDTH]
            b = grid[:, WIDTH : 2 * WIDTH]
            normal = grid[:, 2 * WIDTH :]
            vort = a - b
            okubo = normal * normal + 4.0 * (a * b)
            vort_out[t, pl.ds(row_low, 64, stride=4), :] = vort[:64]
            vort_out[t, pl.ds(row_high, 64, stride=4), :] = vort[64:]
            okubo_out[t, pl.ds(row_low, 64, stride=4), :] = okubo[:64]
            okubo_out[t, pl.ds(row_high, 64, stride=4), :] = okubo[64:]
            both = jnp.concatenate([vort, okubo], axis=1)
            high = both.astype(BF16)
            low = (both - high.astype(F32)).astype(BF16)
            from_high = jnp.dot(high, fit_ref[...], preferred_element_type=F32)
            from_low = jnp.dot(low, fit_ref[...], preferred_element_type=F32)
            fits = from_high + pltpu.roll(from_high, WIDTH - 32, 1) + from_low
            fits = (
                fits[:64] * fit_rows[pl.ds(row_low, 1), :]
                + fits[64:] * fit_rows[pl.ds(row_high, 1), :]
            )
            if rr == 0:
                table[t * 64 : (t + 1) * 64, :] = fits
            else:
                table[t * 64 : (t + 1) * 64, :] += fits


def pick_candidates(goal, named, table):
    values = table[...]
    high = values.astype(BF16).astype(F32)
    low = values - high
    chosen = jnp.dot(
        named[...],
        jnp.concatenate([high, low], axis=1).astype(BF16),
        preferred_element_type=F32,
    )
    total = jnp.zeros((WIDTH, 2 * WIDTH), F32)
    for g in range(4):
        high = chosen[:, :WIDTH]
        low = chosen[:, WIDTH:]
        if g:
            high = pltpu.roll(high, 32 * g, 1)
            low = pltpu.roll(low, 32 * g, 1)
        total += jnp.dot(
            goal[g * WIDTH : (g + 1) * WIDTH, :],
            jnp.concatenate([high, low], axis=1).astype(BF16),
            preferred_element_type=F32,
        )
    return total[:, :WIDTH] + total[:, WIDTH:]


def whole_kernel(
    spec_hbm,
    leg_hbm,
    wave_ref,
    owner_ref,
    block_ref,
    degree_ref,
    rows_ref,
    first_ref,
    twiddle_ref,
    second_ref,
    fit_ref,
    fit_rows,
    vort_out,
    okubo_out,
    fits_out,
    spec,
    leg,
    scaled,
    factor,
    columns,
    sums,
    turned,
    send,
    recv,
    onehot,
    goal,
    named,
    ordered_in,
    ordered,
    spread,
    table,
    outgoing,
    arrived,
    lines,
    spec_sem,
    leg_sem,
    send_sem,
    recv_sem,
    send_fit,
    recv_fit,
    level_sem,
):
    lev = lax.axis_index("lev")
    me = lax.axis_index("band")
    rank = lev * BANDS + me

    def spec_copy(g):
        window = pl.ds(pl.multiple_of(g * GROUP, GROUP), GROUP)
        return pltpu.make_async_copy(
            spec_hbm.at[:, window, :], spec.at[:, window, :], spec_sem.at[g]
        )

    def leg_copy(g):
        window = pl.ds(g * LEG_PART, LEG_PART)
        return pltpu.make_async_copy(leg_hbm.at[window], leg.at[window], leg_sem.at[g])

    for g in range(SLOTS // GROUP):
        spec_copy(g).start()
        for part in range(GROUP // LEG_PART):
            leg_copy(g * (GROUP // LEG_PART) + part).start()

    barrier = pltpu.get_barrier_semaphore()
    greet_peers(barrier, lev, me)
    greet_band(barrier, lev, me)

    columns[...] = column_of(wave_ref[pl.ds(me // 2, 1), :].astype(F32))
    first = pl.multiple_of(lax.rem(me, 2) * SLOTS, SLOTS)
    waits = (lambda g: spec_copy(g).wait(), lambda g: leg_copy(g).wait())
    legendre_sums(first, waits, spec, leg, degree_ref, columns, scaled, factor, sums)
    combine_rows(first, columns, rows_ref, sums, turned)

    for p in range(BANDS):
        for q in range(3):
            send[p, 16 * q : 16 * q + 16, :] = turned[q, p * 16 : p * 16 + 16, :].astype(BF16)

    pl.semaphore_wait(barrier, BANDS - 1 + LEVS - 1)

    my_plane = me // PLANE
    my_place = lax.rem(me, PLANE)

    def place(d):
        return jnp.where(d < BANDS // 2, d, BANDS + BANDS // 2 - 1 - d)

    shifts = (0, 1, 3, 2)
    for number, shift in enumerate(shifts):
        plane = lax.rem(my_plane + shift, PLANES)
        for k in range(0 if shift else 1, PLANE):
            d = plane * PLANE + lax.rem(my_place + k, PLANE)
            pltpu.make_async_remote_copy(
                src_ref=send.at[place(d)],
                dst_ref=recv.at[me],
                send_sem=send_sem,
                recv_sem=recv_sem.at[number],
                device_id={"lev": lev, "band": d},
                device_id_type=MESH,
            ).start()
    recv[me] = send[place(me)]
    greet_peers(level_sem, lev, me)

    def bulk(count, number):
        return pltpu.make_async_remote_copy(
            src_ref=send.at[pl.ds(0, count)],
            dst_ref=recv.at[pl.ds(0, count)],
            send_sem=send_sem,
            recv_sem=recv_sem.at[number],
            device_id={"lev": lev, "band": me},
            device_id_type=MESH,
        )

    build_onehot(wave_ref, onehot)
    candidate_tables(owner_ref, block_ref, goal, named)

    for number, shift in enumerate(shifts):
        plane = lax.rem(my_plane + PLANES - shift, PLANES)
        bulk(PLANE if shift else PLANE - 1, number).wait_recv()
        join_plane(plane, recv, ordered_in)
        order_plane(plane, number, ordered_in, onehot, ordered, spread)

    tables = (first_ref, twiddle_ref, second_ref, fit_ref, fit_rows)
    synthesis(me, spread, tables, vort_out, okubo_out, table)
    outgoing[...] = pick_candidates(goal, named, table).reshape(BANDS, 4, WIDTH)

    pl.semaphore_wait(level_sem, LEVS - 1)

    def post_fit(k, carry):
        other = lax.rem(rank + k, MEMBERS)
        owner = lax.rem(other, BANDS)
        pltpu.make_async_remote_copy(
            src_ref=outgoing.at[owner],
            dst_ref=arrived.at[rank],
            send_sem=send_fit,
            recv_sem=recv_fit,
            device_id={"lev": other // BANDS, "band": owner},
            device_id_type=MESH,
        ).start()
        return carry

    lax.fori_loop(1, MEMBERS, post_fit, 0)
    arrived[rank] = outgoing[me]
    everything = pltpu.make_async_remote_copy(
        src_ref=arrived.at[pl.ds(0, MEMBERS - 1)],
        dst_ref=arrived.at[pl.ds(0, MEMBERS - 1)],
        send_sem=send_fit,
        recv_sem=recv_fit,
        device_id={"lev": lev, "band": me},
        device_id_type=MESH,
    )
    everything.wait_recv()

    for r in range(ROUNDS):
        line = (arrived[0:32, r, :] + arrived[32:64, r, :]) + (
            arrived[64:96, r, :] + arrived[96:128, r, :]
        )
        for g in range(4):
            value = pltpu.roll(line, WIDTH - 32 * g, 1) if g else line
            lines[pl.ds(4 * r + g, BANDS, stride=CAP), :] = value
    fits_out[...] = lines[...].T[:20, :]

    bulk(BANDS - 1, 0).wait_send()
    everything.wait_send()


def copy_kernel(*refs):
    sources, targets, held, come, go = refs[:3], refs[3:6], refs[6:9], refs[9], refs[10]
    pieces = [(i, t) for i in range(2) for t in range(TIMES)] + [(2, None)]

    def view(ref, t):
        return ref if t is None else ref.at[t]

    inward = [
        pltpu.make_async_copy(view(sources[i], t), view(held[i], t), come.at[n])
        for n, (i, t) in enumerate(pieces)
    ]
    outward = [
        pltpu.make_async_copy(view(held[i], t), view(targets[i], t), go.at[n])
        for n, (i, t) in enumerate(pieces)
    ]
    for copy in inward:
        copy.start()
    for n in range(len(pieces)):
        inward[n].wait()
        outward[n].start()
    for copy in outward:
        copy.wait()


def copied(*results):
    hbm = pl.BlockSpec(memory_space=pl.ANY)
    return pl.pallas_call(
        copy_kernel,
        out_shape=tuple(jax.ShapeDtypeStruct(r.shape, r.dtype) for r in results),
        in_specs=[hbm] * 3,
        out_specs=(hbm,) * 3,
        scratch_shapes=[pltpu.VMEM(r.shape, r.dtype) for r in results]
        + [pltpu.SemaphoreType.DMA((2 * TIMES + 1,)), pltpu.SemaphoreType.DMA((2 * TIMES + 1,))],
        compiler_params=pltpu.CompilerParams(vmem_limit_bytes=60 * 1024 * 1024),
        name="results",
    )(*results)


def whole(spectra, legendre, waves, owner, block):
    vmem = pl.BlockSpec(memory_space=pltpu.VMEM)
    hbm = pl.BlockSpec(memory_space=pl.ANY)
    fit_table, fit_rows = fit_tables()
    grid = jax.ShapeDtypeStruct((TIMES, 256, WIDTH), F32)
    return pl.pallas_call(
        whole_kernel,
        out_shape=(grid, grid, jax.ShapeDtypeStruct((20, BANDS * CAP), F32)),
        in_specs=[hbm, hbm] + [vmem] * 10,
        out_specs=(vmem, vmem, vmem),
        scratch_shapes=[
            pltpu.VMEM((16, SLOTS, K), BF16),
            pltpu.VMEM((SLOTS, HALF, K), BF16),
            pltpu.VMEM((K // WIDTH, 16 * GROUP, WIDTH), F32),
            pltpu.VMEM((GROUP, K), F32),
            pltpu.VMEM((WIDTH, WIDTH), F32),
            pltpu.VMEM((SLOTS * 16, WIDTH), F32),
            pltpu.VMEM((3, 4 * WIDTH, WIDTH), F32),
            pltpu.VMEM((BANDS, 48, WIDTH), BF16),
            pltpu.VMEM((BANDS, 48, WIDTH), BF16),
            pltpu.VMEM((K, K), BF16),
            pltpu.VMEM((4 * WIDTH, CANDS), BF16),
            pltpu.VMEM((CANDS, 256), BF16),
            pltpu.VMEM((96, PLANE * SLOTS), BF16),
            pltpu.VMEM((96, K), F32),
            pltpu.VMEM((32 * 48, WIDTH), F32),
            pltpu.VMEM((256, WIDTH), F32),
            pltpu.VMEM((BANDS, 4, WIDTH), F32),
            pltpu.VMEM((MEMBERS, 4, WIDTH), F32),
            pltpu.VMEM((BANDS * CAP, WIDTH), F32),
            pltpu.SemaphoreType.DMA((SLOTS // GROUP,)),
            pltpu.SemaphoreType.DMA((SLOTS // LEG_PART,)),
            pltpu.SemaphoreType.DMA,
            pltpu.SemaphoreType.DMA((PLANES,)),
            pltpu.SemaphoreType.DMA,
            pltpu.SemaphoreType.DMA,
            pltpu.SemaphoreType.REGULAR,
        ],
        compiler_params=pltpu.CompilerParams(
            collective_id=0, has_side_effects=True, vmem_limit_bytes=56 * 1024 * 1024
        ),
        name="spectral_analysis",
    )(
        spectra,
        legendre,
        waves,
        owner,
        block,
        degree_table(),
        row_table(),
        first_table(),
        twiddle_table(),
        second_table(),
        fit_table,
        fit_rows,
    )


def local(spectra, legendre, wave_order, cand_block, cand_owner):
    results = whole(
        spectra.reshape(16, SLOTS, K),
        legendre,
        wave_order.reshape(K // WIDTH, WIDTH),
        cand_owner.reshape(1, CANDS),
        cand_block.reshape(1, CANDS),
    )
    vort, okubo, fits = copied(*results)

    def rows(field):
        shaped = field.reshape(TIMES, 64, 4, WIDTH).transpose(0, 2, 1, 3)
        return shaped.reshape(1, TIMES, 4, NLON)

    return rows(vort), rows(okubo), fits.T


def solution(mesh):
    placed = (
        P("lev", None, None, None, "band", None),
        P("band", None, None),
        P(),
        P("band"),
        P("band", None),
    )
    return jax.shard_map(
        local,
        mesh=mesh,
        in_specs=placed,
        out_specs=(P("lev", None, "band", None), P("lev", None, "band", None), P("band", None)),
        check_vma=False,
    )
```

```python
import math

import jax
import jax.numpy as jnp
import ml_dtypes
import numpy as np
from jax import lax
from jax.experimental import pallas as pl
from jax.experimental.pallas import tpu as pltpu
from jax.sharding import PartitionSpec as P

MESH = pl.DeviceIdType.MESH
F32 = jnp.float32
BF16 = jnp.bfloat16

BANDS = 32
LEVS = 4
SLOTS = 64
K = 2048
NLON = 8192
HALF = 64
TIMES = 4
GROUP = 16
PLANE = 8
PLANES = 4
MEMBERS = 128
WIDTH = 128
CANDS = 192
CAP = 12
PACK = 6
VALUES = 20


def bf16_split(table):
    high = table.astype(np.float32).astype(ml_dtypes.bfloat16)
    low = (table - high.astype(np.float64)).astype(np.float32).astype(ml_dtypes.bfloat16)
    return high, low


def degree_table():
    n = np.arange(K, dtype=np.float32)
    inverse = np.where(n >= 1, np.float32(-1.0) / np.maximum(n * (n + 1), np.float32(1.0)), 0.0)
    table = np.zeros((8, K), np.float32)
    table[0] = inverse
    table[1] = np.where(np.arange(K) % 2 == 0, 1.0, -1.0)
    return table


def row_table():
    hy = math.pi / 4096.0
    j = np.arange(HALF)
    hx = np.cos((63.5 - j) * hy) * 2.0 * math.pi / NLON
    table = np.zeros((8, WIDTH), np.float64)
    table[0, :HALF] = table[0, HALF:] = 1.0 / (hx * hx)
    table[1, :HALF] = 1.0 / (4.0 * hx * hy)
    table[1, HALF:] = -1.0 / (4.0 * hx * hy)
    table[2] = 1.0 / (hy * hy)
    return table.astype(np.float32)


def first_table():
    h = np.arange(32)[:, None]
    x = np.arange(WIDTH)[None, :]
    angle = 2.0 * np.pi * ((h * x) % 128) / 128.0
    cos, sin = np.cos(angle), np.sin(angle)
    table = np.concatenate(
        [np.concatenate([cos, sin], 1), np.concatenate([-sin, cos], 1)], 0
    )
    high, low = bf16_split(table)
    return np.concatenate([high, low], 0)


def twiddle_table():
    low = np.arange(64)[:, None]
    x = np.arange(WIDTH)[None, :]
    angle = 2.0 * np.pi * (low * x) / NLON
    cos, sin = np.cos(angle), np.sin(angle)
    return np.stack([np.concatenate([cos, cos], 0), np.concatenate([sin, sin], 0)], 0).astype(
        np.float32
    )


def second_table():
    y = np.arange(64)[:, None]
    low = np.arange(64)[None, :]
    angle = 2.0 * np.pi * ((y * low) % 64) / 64.0
    cos, sin = np.cos(angle), -np.sin(angle)
    zero = np.zeros_like(cos)
    table = np.concatenate(
        [
            np.concatenate([cos, zero, sin, zero], 1),
            np.concatenate([zero, cos, zero, sin], 1),
        ],
        0,
    )
    high, low_part = bf16_split(table)
    return np.concatenate([high, low_part, high], 1)


ORDERS = ((0, 0), (1, 0), (0, 1), (2, 0), (1, 1), (0, 2), (3, 0), (2, 1), (1, 2), (0, 3))


def ortho_values(count):
    u = np.arange(count, dtype=np.float64) - (count - 1) / 2.0
    q = np.stack(
        [
            np.ones_like(u),
            u,
            u * u - (count * count - 1) / 12.0,
            u * u * u - (3 * count * count - 7) / 20.0 * u,
        ],
        0,
    )
    return q / np.sqrt(np.sum(q * q, 1, keepdims=True))


def fit_tables():
    across, upward = ortho_values(WIDTH), ortho_values(4)
    columns = np.stack([across[a] for a, _ in ORDERS], 1)
    table = np.zeros((256, 32), np.float64)
    table[:128, 0:10] = columns
    table[128:, 10:20] = columns
    high, low = bf16_split(table)
    both = np.zeros((256, 128), high.dtype)
    both[:, 0:32] = high
    both[:, 32:64] = low
    rows = np.zeros((8, 128), np.float32)
    for r in range(4):
        line = [upward[b][r] / 4.0 for _, b in ORDERS]
        rows[r, 0:10] = line
        rows[r, 10:20] = line
    return both, rows


def column_of(row):
    return jnp.broadcast_to(row, (WIDTH, WIDTH)).T


def greet_peers(semaphore, lev, me):
    for k in range(1, LEVS):
        pl.semaphore_signal(
            semaphore,
            inc=1,
            device_id={"lev": lax.rem(lev + k, LEVS), "band": me},
            device_id_type=MESH,
        )


def greet_band(semaphore, lev, me):
    def greet(k, carry):
        pl.semaphore_signal(
            semaphore,
            inc=1,
            device_id={"lev": lev, "band": lax.rem(me + k, BANDS)},
            device_id_type=MESH,
        )
        return carry

    lax.fori_loop(1, BANDS, greet, 0)


def legendre_sums(first, waits, spec, leg, degree_ref, columns, scaled, factor, sums):
    spec_wait, leg_wait = waits
    lane = lax.broadcasted_iota(jnp.int32, (1, K), 1).astype(F32)

    def one_group(g, carry):
        spec_wait(g)
        start = pl.multiple_of(g * GROUP, GROUP)
        own = columns[pl.ds(pl.multiple_of(first + start, GROUP), GROUP), :]
        own = jnp.concatenate([own] * (K // WIDTH), axis=1)
        factor[...] = jnp.where(lane >= own, degree_ref[0:1, :], 0.0)

        def scale(q, inner):
            part = spec[q, pl.ds(start, GROUP), :].astype(F32) * factor[...]
            window = pl.ds(pl.multiple_of(q * GROUP, GROUP), GROUP)
            for tile in range(K // WIDTH):
                scaled[tile, window, :] = part[:, tile * WIDTH : (tile + 1) * WIDTH]
            return inner

        lax.fori_loop(0, 16, scale, 0, unroll=4)

        def one_slot(i, inner):
            even = jnp.concatenate(
                [scaled[tile, pl.ds(i, 16, stride=GROUP), :] for tile in range(K // WIDTH)],
                axis=1,
            )
            odd = even * degree_ref[1:2, :]
            both = jnp.concatenate([even.astype(BF16), odd.astype(BF16)], axis=0)
            result = lax.dot_general(
                both,
                leg[start + i],
                (((1,), (1,)), ((), ())),
                preferred_element_type=F32,
            )
            result = result.astype(BF16).astype(F32)
            sums[pl.ds(pl.multiple_of((start + i) * 16, 16), 16), :] = jnp.concatenate(
                [result[:16], result[16:]], axis=1
            )
            return inner

        leg_wait(g)
        lax.fori_loop(0, GROUP, one_slot, 0, unroll=GROUP)
        return carry

    lax.fori_loop(0, SLOTS // GROUP, one_group, 0)


def combine_rows(first, columns, rows_ref, sums, turned):
    m = columns[pl.ds(first, SLOTS), :]
    lanes = lax.broadcasted_iota(jnp.int32, (SLOTS, WIDTH), 1)
    half_m = jnp.floor(m * 0.5)
    parity = 1.0 - 2.0 * (m - 2.0 * half_m)
    weight = jnp.where(m == 0.0, 1.0, 2.0)
    sign = jnp.where(lanes >= HALF, parity, 1.0) * weight
    x = m * (math.pi / NLON)
    x2 = x * x
    sin = x * (
        1.0
        + x2 * (-1.0 / 6 + x2 * (1.0 / 120 + x2 * (-1.0 / 5040 + x2 * (1.0 / 362880))))
    )
    cos = 1.0 + x2 * (
        -0.5
        + x2 * (1.0 / 24 + x2 * (-1.0 / 720 + x2 * (1.0 / 40320 - x2 * (1.0 / 3628800))))
    )
    xx = -4.0 * sin * sin * rows_ref[0:1, :]
    xy = 2.0 * (2.0 * sin * cos) * rows_ref[1:2, :]
    yy = rows_ref[2:3, :]
    first_lane = (lanes == 0) | (lanes == HALF)
    last_lane = (lanes == HALF - 1) | (lanes == WIDTH - 1)

    def one_time(t, carry):
        def pieces(q):
            c = sums[pl.ds(t * 4 + q, SLOTS, stride=16), :] * sign
            before = jnp.where(first_lane, 0.0, pltpu.roll(c, 1, 1))
            after = jnp.where(last_lane, pltpu.roll(c, HALF, 1), pltpu.roll(c, WIDTH - 1, 1))
            return c * xx, (before + after - 2.0 * c) * yy, (before - after) * xy

        pr_xx, pr_yy, pr_xy = pieces(0)
        pi_xx, pi_yy, pi_xy = pieces(1)
        cr_xx, cr_yy, cr_xy = pieces(2)
        ci_xx, ci_yy, ci_xy = pieces(3)
        a = (pr_xx - ci_xy, pi_xx + cr_xy)
        b = (-ci_xy - pr_yy, cr_xy - pi_yy)
        normal = (2.0 * pi_xy + cr_xx - cr_yy, -2.0 * pr_xy + ci_xx - ci_yy)
        for q, pair in enumerate((a, b, normal)):
            block = jnp.concatenate(pair, axis=0).T
            turned[q, pl.ds(t, WIDTH, stride=4), :] = block
        return carry

    lax.fori_loop(0, TIMES, one_time, 0, unroll=4)


def build_onehot(wave_ref, onehot):
    lane = lax.broadcasted_iota(jnp.int32, (WIDTH, WIDTH), 1).astype(F32)

    def one_block(j, carry):
        column = column_of(wave_ref[pl.ds(j, 1), :].astype(F32))
        rows = pl.ds(pl.multiple_of(j * WIDTH, WIDTH), WIDTH)
        for tile in range(K // WIDTH):
            onehot[rows, tile * WIDTH : (tile + 1) * WIDTH] = jnp.where(
                column == lane + float(tile * WIDTH), 1.0, 0.0
            ).astype(BF16)
        return carry

    lax.fori_loop(0, K // WIDTH, one_block, 0)


def candidate_tables(owner_ref, block_ref, goal, named):
    owner = owner_ref[...]
    owned = jnp.where(
        lax.broadcasted_iota(jnp.int32, (BANDS, CANDS), 0) == owner, 1.0, 0.0
    )
    order = jnp.where(
        lax.broadcasted_iota(jnp.int32, (CANDS, CANDS), 0)
        < lax.broadcasted_iota(jnp.int32, (CANDS, CANDS), 1),
        1.0,
        0.0,
    ).astype(BF16)
    earlier = jnp.dot(owned.astype(BF16), order, preferred_element_type=F32)
    slot = jnp.sum(earlier * owned, axis=0, keepdims=True).astype(jnp.int32)
    second = jnp.where(slot >= PACK, 1, 0)
    target = (slot - PACK * second) * (2 * BANDS) + owner * 2 + second
    goal[...] = jnp.where(
        lax.broadcasted_iota(jnp.int32, (PACK * 2 * BANDS, CANDS), 0) == target, 1.0, 0.0
    ).astype(BF16)
    cells = jnp.where(
        lax.broadcasted_iota(jnp.int32, (256, CANDS), 0) == block_ref[...], 1.0, 0.0
    )
    named[...] = cells.T.astype(BF16)


def join_plane(plane, coeffs, ordered_in):
    pick = lax.broadcasted_iota(jnp.int32, (48, WIDTH), 1) < 64
    for j in range(PLANE // 2):
        a = coeffs[plane * PLANE + 2 * j].astype(F32)
        b = coeffs[plane * PLANE + 2 * j + 1].astype(F32)
        real = jnp.where(pick, a, pltpu.roll(b, 64, 1))
        imag = jnp.where(pick, pltpu.roll(a, 64, 1), b)
        ordered_in[0:48, j * WIDTH : (j + 1) * WIDTH] = real.astype(BF16)
        ordered_in[48:96, j * WIDTH : (j + 1) * WIDTH] = imag.astype(BF16)


def order_plane(plane, number, ordered_in, onehot, ordered, spread):
    pick = lax.broadcasted_iota(jnp.int32, (8, WIDTH), 1) < 64
    depth = PLANE * SLOTS
    rows = pl.ds(pl.multiple_of(plane * depth, depth), depth)
    for j in range(8):
        at = slice(256 * j, 256 * (j + 1))
        part = jnp.dot(ordered_in[...], onehot[rows, at], preferred_element_type=F32)
        if number > 0:
            part = part + ordered[:, at]
        if number < PLANES - 1:
            ordered[:, at] = part
            continue
        for tile in range(2):
            h = 4 * j + 2 * tile
            for c in range(2):
                for f in range(3):
                    at = c * 48 + f * 16
                    a = part[at : at + 8, tile * WIDTH : (tile + 1) * WIDTH]
                    b = part[at + 8 : at + 16, tile * WIDTH : (tile + 1) * WIDTH]
                    to = c * 24 + f * 8
                    spread[h * 48 + to : h * 48 + to + 8, :] = jnp.where(
                        pick, a, pltpu.roll(b, 64, 1)
                    )
                    spread[(h + 1) * 48 + to : (h + 1) * 48 + to + 8, :] = jnp.where(
                        pick, pltpu.roll(a, 64, 1), b
                    )


def synthesis(band, spread, tables, vort_out, okubo_out, table):
    first_ref, twiddle_ref, second_ref, fit_ref, fit_rows = tables
    southern = band >= BANDS // 2
    for t in range(TIMES):
        for rr in range(2):
            row_low = jnp.where(southern, 3 - rr, rr)
            row_high = jnp.where(southern, 1 - rr, 2 + rr)
            parts = []
            for f in range(3):
                i = f * 8 + rr * 4 + t
                c = jnp.concatenate(
                    [spread[pl.ds(i, 32, stride=48), :], spread[pl.ds(24 + i, 32, stride=48), :]],
                    axis=0,
                ).T.astype(BF16)
                z = jnp.dot(
                    jnp.concatenate([c, c], axis=1), first_ref[...], preferred_element_type=F32
                )
                zr, zi = z[:, :WIDTH], z[:, WIDTH:]
                tc, ts = twiddle_ref[0], twiddle_ref[1]
                parts.append(jnp.concatenate([zr * tc - zi * ts, zr * ts + zi * tc], axis=0))
            z = jnp.concatenate(parts, axis=1)
            high = z.astype(BF16)
            low = (z - high.astype(F32)).astype(BF16)
            grid = jnp.dot(
                second_ref[...],
                jnp.concatenate([high, high, low], axis=0),
                preferred_element_type=F32,
            )
            a = grid[:, :WIDTH]
            b = grid[:, WIDTH : 2 * WIDTH]
            normal = grid[:, 2 * WIDTH :]
            vort = a - b
            okubo = normal * normal + 4.0 * (a * b)
            vort_out[t, pl.ds(row_low, 64, stride=4), :] = vort[:64]
            vort_out[t, pl.ds(row_high, 64, stride=4), :] = vort[64:]
            okubo_out[t, pl.ds(row_low, 64, stride=4), :] = okubo[:64]
            okubo_out[t, pl.ds(row_high, 64, stride=4), :] = okubo[64:]
            both = jnp.concatenate([vort, okubo], axis=1)
            high = both.astype(BF16)
            low = (both - high.astype(F32)).astype(BF16)
            from_high = jnp.dot(high, fit_ref[...], preferred_element_type=F32)
            from_low = jnp.dot(low, fit_ref[...], preferred_element_type=F32)
            fits = from_high + pltpu.roll(from_high, WIDTH - 32, 1) + from_low
            fits = (
                fits[:64] * fit_rows[pl.ds(row_low, 1), :]
                + fits[64:] * fit_rows[pl.ds(row_high, 1), :]
            )
            if rr == 0:
                table[t * 64 : (t + 1) * 64, :] = fits
            else:
                table[t * 64 : (t + 1) * 64, :] += fits


def pick_candidates(goal, named, table):
    values = table[...]
    high = values.astype(BF16).astype(F32)
    low = values - high
    chosen = jnp.dot(
        named[...],
        jnp.concatenate([high, low], axis=1).astype(BF16),
        preferred_element_type=F32,
    )
    total = jnp.zeros((2 * BANDS, 2 * WIDTH), F32)
    for g in range(PACK):
        high = chosen[:, :WIDTH]
        low = chosen[:, WIDTH:]
        if g:
            high = pltpu.roll(high, VALUES * g, 1)
            low = pltpu.roll(low, VALUES * g, 1)
        total += jnp.dot(
            goal[g * 2 * BANDS : (g + 1) * 2 * BANDS, :],
            jnp.concatenate([high, low], axis=1).astype(BF16),
            preferred_element_type=F32,
        )
    return total[:, :WIDTH] + total[:, WIDTH:]


def whole_kernel(
    spec_hbm,
    leg_hbm,
    wave_ref,
    owner_ref,
    block_ref,
    degree_ref,
    rows_ref,
    first_ref,
    twiddle_ref,
    second_ref,
    fit_ref,
    fit_rows,
    vort_out,
    okubo_out,
    fits_out,
    spec,
    leg,
    scaled,
    factor,
    columns,
    sums,
    turned,
    send,
    recv,
    onehot,
    goal,
    named,
    ordered_in,
    ordered,
    spread,
    vort,
    okubo,
    table,
    outgoing,
    arrived,
    lines,
    spec_sem,
    leg_sem,
    send_sem,
    recv_sem,
    send_fit,
    recv_fit,
    level_sem,
    out_sem,
):
    lev = lax.axis_index("lev")
    me = lax.axis_index("band")
    rank = lev * BANDS + me

    def spec_copy(g):
        window = pl.ds(pl.multiple_of(g * GROUP, GROUP), GROUP)
        return pltpu.make_async_copy(
            spec_hbm.at[:, window, :], spec.at[:, window, :], spec_sem.at[g]
        )

    def leg_copy(g):
        window = pl.ds(pl.multiple_of(g * GROUP, GROUP), GROUP)
        return pltpu.make_async_copy(leg_hbm.at[window], leg.at[window], leg_sem.at[g])

    for g in range(SLOTS // GROUP):
        spec_copy(g).start()
        leg_copy(g).start()

    barrier = pltpu.get_barrier_semaphore()
    greet_peers(barrier, lev, me)
    greet_band(barrier, lev, me)

    columns[...] = column_of(wave_ref[pl.ds(me // 2, 1), :].astype(F32))
    first = pl.multiple_of(lax.rem(me, 2) * SLOTS, SLOTS)
    waits = (lambda g: spec_copy(g).wait(), lambda g: leg_copy(g).wait())
    legendre_sums(first, waits, spec, leg, degree_ref, columns, scaled, factor, sums)
    combine_rows(first, columns, rows_ref, sums, turned)

    for p in range(BANDS):
        for q in range(3):
            send[p, 16 * q : 16 * q + 16, :] = turned[q, p * 16 : p * 16 + 16, :].astype(BF16)

    pl.semaphore_wait(barrier, BANDS - 1 + LEVS - 1)

    my_plane = me // PLANE
    my_place = lax.rem(me, PLANE)

    def place(d):
        return jnp.where(d < BANDS // 2, d, BANDS + BANDS // 2 - 1 - d)

    shifts = (0, 1, 3, 2)
    for number, shift in enumerate(shifts):
        plane = lax.rem(my_plane + shift, PLANES)
        for k in range(0 if shift else 1, PLANE):
            d = plane * PLANE + lax.rem(my_place + k, PLANE)
            pltpu.make_async_remote_copy(
                src_ref=send.at[place(d)],
                dst_ref=recv.at[me],
                send_sem=send_sem,
                recv_sem=recv_sem.at[number],
                device_id={"lev": lev, "band": d},
                device_id_type=MESH,
            ).start()
    recv[me] = send[place(me)]
    greet_peers(level_sem, lev, me)

    def bulk(count, number):
        return pltpu.make_async_remote_copy(
            src_ref=send.at[pl.ds(0, count)],
            dst_ref=recv.at[pl.ds(0, count)],
            send_sem=send_sem,
            recv_sem=recv_sem.at[number],
            device_id={"lev": lev, "band": me},
            device_id_type=MESH,
        )

    build_onehot(wave_ref, onehot)
    candidate_tables(owner_ref, block_ref, goal, named)

    for number, shift in enumerate(shifts):
        plane = lax.rem(my_plane + PLANES - shift, PLANES)
        bulk(PLANE if shift else PLANE - 1, number).wait_recv()
        join_plane(plane, recv, ordered_in)
        order_plane(plane, number, ordered_in, onehot, ordered, spread)

    tables = (first_ref, twiddle_ref, second_ref, fit_ref, fit_rows)
    synthesis(me, spread, tables, vort, okubo, table)
    grid_copies = [
        pltpu.make_async_copy(vort, vort_out, out_sem.at[0]),
        pltpu.make_async_copy(okubo, okubo_out, out_sem.at[1]),
    ]
    for copy in grid_copies:
        copy.start()
    outgoing[...] = pick_candidates(goal, named, table).reshape(BANDS, 2, WIDTH)

    pl.semaphore_wait(level_sem, LEVS - 1)

    def post_fit(k, carry):
        other = lax.rem(rank + k, MEMBERS)
        owner = lax.rem(other, BANDS)
        pltpu.make_async_remote_copy(
            src_ref=outgoing.at[owner],
            dst_ref=arrived.at[rank],
            send_sem=send_fit,
            recv_sem=recv_fit,
            device_id={"lev": other // BANDS, "band": owner},
            device_id_type=MESH,
        ).start()
        return carry

    lax.fori_loop(1, MEMBERS, post_fit, 0, unroll=4)
    arrived[rank] = outgoing[me]
    everything = pltpu.make_async_remote_copy(
        src_ref=arrived.at[pl.ds(0, MEMBERS - 1)],
        dst_ref=arrived.at[pl.ds(0, MEMBERS - 1)],
        send_sem=send_fit,
        recv_sem=recv_fit,
        device_id={"lev": lev, "band": me},
        device_id_type=MESH,
    )
    everything.wait_recv()

    for r in range(CAP // PACK):
        line = (arrived[0:32, r, :] + arrived[32:64, r, :]) + (
            arrived[64:96, r, :] + arrived[96:128, r, :]
        )
        for g in range(PACK):
            value = pltpu.roll(line, WIDTH - VALUES * g, 1) if g else line
            lines[pl.ds(PACK * r + g, BANDS, stride=CAP), :] = value
    fits_out[...] = lines[...].T[:20, :]

    bulk(BANDS - 1, 0).wait_send()
    everything.wait_send()
    for copy in grid_copies:
        copy.wait()


def copy_kernel(*refs):
    sources, targets, held, come, go = refs[:3], refs[3:6], refs[6:9], refs[9], refs[10]
    pieces = [(i, t) for i in range(2) for t in range(TIMES)] + [(2, None)]

    def view(ref, t):
        return ref if t is None else ref.at[t]

    inward = [
        pltpu.make_async_copy(view(sources[i], t), view(held[i], t), come.at[n])
        for n, (i, t) in enumerate(pieces)
    ]
    outward = [
        pltpu.make_async_copy(view(held[i], t), view(targets[i], t), go.at[n])
        for n, (i, t) in enumerate(pieces)
    ]
    for copy in inward:
        copy.start()
    for n in range(len(pieces)):
        inward[n].wait()
        outward[n].start()
    for copy in outward:
        copy.wait()


def copied(*results):
    hbm = pl.BlockSpec(memory_space=pl.ANY)
    return pl.pallas_call(
        copy_kernel,
        out_shape=tuple(jax.ShapeDtypeStruct(r.shape, r.dtype) for r in results),
        in_specs=[hbm] * 3,
        out_specs=(hbm,) * 3,
        scratch_shapes=[pltpu.VMEM(r.shape, r.dtype) for r in results]
        + [pltpu.SemaphoreType.DMA((2 * TIMES + 1,)), pltpu.SemaphoreType.DMA((2 * TIMES + 1,))],
        compiler_params=pltpu.CompilerParams(vmem_limit_bytes=60 * 1024 * 1024),
        name="results",
    )(*results)


def whole(spectra, legendre, waves, owner, block):
    vmem = pl.BlockSpec(memory_space=pltpu.VMEM)
    hbm = pl.BlockSpec(memory_space=pl.ANY)
    fit_table, fit_rows = fit_tables()
    grid = jax.ShapeDtypeStruct((TIMES, 256, WIDTH), F32)
    return pl.pallas_call(
        whole_kernel,
        out_shape=(grid, grid, jax.ShapeDtypeStruct((20, BANDS * CAP), F32)),
        in_specs=[hbm, hbm] + [vmem] * 10,
        out_specs=(hbm, hbm, vmem),
        scratch_shapes=[
            pltpu.VMEM((16, SLOTS, K), BF16),
            pltpu.VMEM((SLOTS, HALF, K), BF16),
            pltpu.VMEM((K // WIDTH, 16 * GROUP, WIDTH), F32),
            pltpu.VMEM((GROUP, K), F32),
            pltpu.VMEM((WIDTH, WIDTH), F32),
            pltpu.VMEM((SLOTS * 16, WIDTH), F32),
            pltpu.VMEM((3, 4 * WIDTH, WIDTH), F32),
            pltpu.VMEM((BANDS, 48, WIDTH), BF16),
            pltpu.VMEM((BANDS, 48, WIDTH), BF16),
            pltpu.VMEM((K, K), BF16),
            pltpu.VMEM((PACK * 2 * BANDS, CANDS), BF16),
            pltpu.VMEM((CANDS, 256), BF16),
            pltpu.VMEM((96, PLANE * SLOTS), BF16),
            pltpu.VMEM((96, K), F32),
            pltpu.VMEM((32 * 48, WIDTH), F32),
            pltpu.VMEM((TIMES, 256, WIDTH), F32),
            pltpu.VMEM((TIMES, 256, WIDTH), F32),
            pltpu.VMEM((256, WIDTH), F32),
            pltpu.VMEM((BANDS, 2, WIDTH), F32),
            pltpu.VMEM((MEMBERS, 2, WIDTH), F32),
            pltpu.VMEM((BANDS * CAP, WIDTH), F32),
            pltpu.SemaphoreType.DMA((SLOTS // GROUP,)),
            pltpu.SemaphoreType.DMA((SLOTS // GROUP,)),
            pltpu.SemaphoreType.DMA,
            pltpu.SemaphoreType.DMA((PLANES,)),
            pltpu.SemaphoreType.DMA,
            pltpu.SemaphoreType.DMA,
            pltpu.SemaphoreType.REGULAR,
            pltpu.SemaphoreType.DMA((2,)),
        ],
        compiler_params=pltpu.CompilerParams(
            collective_id=0, has_side_effects=True, vmem_limit_bytes=56 * 1024 * 1024
        ),
        name="spectral_analysis",
    )(
        spectra,
        legendre,
        waves,
        owner,
        block,
        degree_table(),
        row_table(),
        first_table(),
        twiddle_table(),
        second_table(),
        fit_table,
        fit_rows,
    )


def local(spectra, legendre, wave_order, cand_block, cand_owner):
    results = whole(
        spectra.reshape(16, SLOTS, K),
        legendre,
        wave_order.reshape(K // WIDTH, WIDTH),
        cand_owner.reshape(1, CANDS),
        cand_block.reshape(1, CANDS),
    )
    vort, okubo, fits = copied(*results)

    def rows(field):
        shaped = field.reshape(TIMES, 64, 4, WIDTH).transpose(0, 2, 1, 3)
        return shaped.reshape(1, TIMES, 4, NLON)

    return rows(vort), rows(okubo), fits.T


def solution(mesh):
    placed = (
        P("lev", None, None, None, "band", None),
        P("band", None, None),
        P(),
        P("band"),
        P("band", None),
    )
    return jax.shard_map(
        local,
        mesh=mesh,
        in_specs=placed,
        out_specs=(P("lev", None, "band", None), P("lev", None, "band", None), P("band", None)),
        check_vma=False,
    )
```

```python
import math

import jax
import jax.numpy as jnp
import ml_dtypes
import numpy as np
from jax import lax
from jax.experimental import pallas as pl
from jax.experimental.pallas import tpu as pltpu
from jax.sharding import PartitionSpec as P

MESH = pl.DeviceIdType.MESH
F32 = jnp.float32
BF16 = jnp.bfloat16

BANDS = 32
LEVS = 4
SLOTS = 64
K = 2048
NLON = 8192
HALF = 64
TIMES = 4
GROUP = 16
PART = 32
ROWS = 24
PLANE = 8
PLANES = 4
MEMBERS = 128
WIDTH = 128
CANDS = 192
CAP = 12
PACK = 6
VALUES = 20


def bf16_split(table):
    high = table.astype(np.float32).astype(ml_dtypes.bfloat16)
    low = (table - high.astype(np.float64)).astype(np.float32).astype(ml_dtypes.bfloat16)
    return high, low


def degree_table():
    n = np.arange(K, dtype=np.float32)
    inverse = np.where(n >= 1, np.float32(-1.0) / np.maximum(n * (n + 1), np.float32(1.0)), 0.0)
    table = np.zeros((8, K), np.float32)
    table[0] = inverse
    table[1] = np.where(np.arange(K) % 2 == 0, 1.0, -1.0)
    return table


def row_table():
    hy = math.pi / 4096.0
    j = np.arange(HALF)
    hx = np.cos((63.5 - j) * hy) * 2.0 * math.pi / NLON
    table = np.zeros((8, WIDTH), np.float64)
    table[0, :HALF] = table[0, HALF:] = 1.0 / (hx * hx)
    table[1, :HALF] = 1.0 / (4.0 * hx * hy)
    table[1, HALF:] = -1.0 / (4.0 * hx * hy)
    table[2] = 1.0 / (hy * hy)
    return table.astype(np.float32)


def first_table():
    h = np.arange(32)[:, None]
    x = np.arange(WIDTH)[None, :]
    angle = 2.0 * np.pi * ((h * x) % 128) / 128.0
    cos, sin = np.cos(angle), np.sin(angle)
    table = np.concatenate(
        [np.concatenate([cos, sin], 1), np.concatenate([-sin, cos], 1)], 0
    )
    high, low = bf16_split(table)
    return np.concatenate([high, low], 0)


def twiddle_table():
    low = np.arange(64)[:, None]
    x = np.arange(WIDTH)[None, :]
    angle = 2.0 * np.pi * (low * x) / NLON
    cos, sin = np.cos(angle), np.sin(angle)
    return np.stack([np.concatenate([cos, cos], 0), np.concatenate([sin, sin], 0)], 0).astype(
        np.float32
    )


def second_table():
    y = np.arange(64)[:, None]
    low = np.arange(64)[None, :]
    angle = 2.0 * np.pi * ((y * low) % 64) / 64.0
    cos, sin = np.cos(angle), -np.sin(angle)
    zero = np.zeros_like(cos)
    table = np.concatenate(
        [
            np.concatenate([cos, zero, sin, zero], 1),
            np.concatenate([zero, cos, zero, sin], 1),
        ],
        0,
    )
    high, low_part = bf16_split(table)
    return np.concatenate([high, low_part, high], 1)


ORDERS = ((0, 0), (1, 0), (0, 1), (2, 0), (1, 1), (0, 2), (3, 0), (2, 1), (1, 2), (0, 3))


def ortho_values(count):
    u = np.arange(count, dtype=np.float64) - (count - 1) / 2.0
    q = np.stack(
        [
            np.ones_like(u),
            u,
            u * u - (count * count - 1) / 12.0,
            u * u * u - (3 * count * count - 7) / 20.0 * u,
        ],
        0,
    )
    return q / np.sqrt(np.sum(q * q, 1, keepdims=True))


def fit_tables():
    across, upward = ortho_values(WIDTH), ortho_values(4)
    columns = np.stack([across[a] for a, _ in ORDERS], 1)
    table = np.zeros((256, 32), np.float64)
    table[:128, 0:10] = columns
    table[128:, 10:20] = columns
    high, low = bf16_split(table)
    both = np.zeros((256, 128), high.dtype)
    both[:, 0:32] = high
    both[:, 32:64] = low
    rows = np.zeros((8, 128), np.float32)
    for r in range(4):
        line = [upward[b][r] / 4.0 for _, b in ORDERS]
        rows[r, 0:10] = line
        rows[r, 10:20] = line
    return both, rows


def column_of(row):
    return jnp.broadcast_to(row, (WIDTH, WIDTH)).T


def greet_peers(semaphore, lev, me):
    for k in range(1, LEVS):
        pl.semaphore_signal(
            semaphore,
            inc=1,
            device_id={"lev": lax.rem(lev + k, LEVS), "band": me},
            device_id_type=MESH,
        )


def greet_band(semaphore, lev, me):
    def greet(k, carry):
        pl.semaphore_signal(
            semaphore,
            inc=1,
            device_id={"lev": lev, "band": lax.rem(me + k, BANDS)},
            device_id_type=MESH,
        )
        return carry

    lax.fori_loop(1, BANDS, greet, 0)


def legendre_sums(groups, first, waits, spec, leg, degree_ref, columns, scaled, factor, sums):
    spec_wait, leg_wait = waits
    lane = lax.broadcasted_iota(jnp.int32, (1, K), 1).astype(F32)

    def one_group(g, carry):
        spec_wait(g)
        start = pl.multiple_of(g * GROUP, GROUP)
        own = columns[pl.ds(pl.multiple_of(first + start, GROUP), GROUP), :]
        own = jnp.concatenate([own] * (K // WIDTH), axis=1)
        factor[...] = jnp.where(lane >= own, degree_ref[0:1, :], 0.0)

        def scale(q, inner):
            part = spec[q, pl.ds(start, GROUP), :].astype(F32) * factor[...]
            window = pl.ds(pl.multiple_of(q * GROUP, GROUP), GROUP)
            for tile in range(K // WIDTH):
                scaled[tile, window, :] = part[:, tile * WIDTH : (tile + 1) * WIDTH]
            return inner

        lax.fori_loop(0, 16, scale, 0, unroll=4)

        def one_slot(i, inner):
            even = jnp.concatenate(
                [scaled[tile, pl.ds(i, 16, stride=GROUP), :] for tile in range(K // WIDTH)],
                axis=1,
            )
            odd = even * degree_ref[1:2, :]
            both = jnp.concatenate([even.astype(BF16), odd.astype(BF16)], axis=0)
            result = lax.dot_general(
                both,
                leg[start + i],
                (((1,), (1,)), ((), ())),
                preferred_element_type=F32,
            )
            result = result.astype(BF16).astype(F32)
            sums[pl.ds(pl.multiple_of((start + i) * 16, 16), 16), :] = jnp.concatenate(
                [result[:16], result[16:]], axis=1
            )
            return inner

        leg_wait(g)
        lax.fori_loop(0, GROUP, one_slot, 0, unroll=GROUP)
        return carry

    lax.fori_loop(groups[0], groups[1], one_group, 0)


def combine_rows(start, first, columns, rows_ref, sums, turned):
    m = columns[pl.ds(pl.multiple_of(first + start, PART), PART), :]
    lanes = lax.broadcasted_iota(jnp.int32, (PART, WIDTH), 1)
    half_m = jnp.floor(m * 0.5)
    parity = 1.0 - 2.0 * (m - 2.0 * half_m)
    weight = jnp.where(m == 0.0, 1.0, 2.0)
    sign = jnp.where(lanes >= HALF, parity, 1.0) * weight
    x = m * (math.pi / NLON)
    x2 = x * x
    sin = x * (
        1.0
        + x2 * (-1.0 / 6 + x2 * (1.0 / 120 + x2 * (-1.0 / 5040 + x2 * (1.0 / 362880))))
    )
    cos = 1.0 + x2 * (
        -0.5
        + x2 * (1.0 / 24 + x2 * (-1.0 / 720 + x2 * (1.0 / 40320 - x2 * (1.0 / 3628800))))
    )
    xx = -4.0 * sin * sin * rows_ref[0:1, :]
    xy = 2.0 * (2.0 * sin * cos) * rows_ref[1:2, :]
    yy = rows_ref[2:3, :]
    first_lane = (lanes == 0) | (lanes == HALF)
    last_lane = (lanes == HALF - 1) | (lanes == WIDTH - 1)

    def fields(t):
        def pieces(q):
            c = sums[pl.ds(start * 16 + t * 4 + q, PART, stride=16), :] * sign
            before = jnp.where(first_lane, 0.0, pltpu.roll(c, 1, 1))
            after = jnp.where(last_lane, pltpu.roll(c, HALF, 1), pltpu.roll(c, WIDTH - 1, 1))
            return c * xx, (before + after - 2.0 * c) * yy, (before - after) * xy

        pr_xx, pr_yy, pr_xy = pieces(0)
        pi_xx, pi_yy, pi_xy = pieces(1)
        cr_xx, cr_yy, cr_xy = pieces(2)
        ci_xx, ci_yy, ci_xy = pieces(3)
        a = (pr_xx - ci_xy, pi_xx + cr_xy)
        b = (-ci_xy - pr_yy, cr_xy - pi_yy)
        normal = (2.0 * pi_xy + cr_xx - cr_yy, -2.0 * pr_xy + ci_xx - ci_yy)
        return a, b, normal

    for pair in range(TIMES // 2):
        early, late = fields(2 * pair), fields(2 * pair + 1)
        for q in range(3):
            block = jnp.concatenate(early[q] + late[q], axis=0).T
            turned[q, pl.ds(pair, WIDTH, stride=2), :] = block


def build_onehot(wave_ref, onehot):
    lane = lax.broadcasted_iota(jnp.int32, (WIDTH, WIDTH), 1).astype(F32)
    quarter = lax.broadcasted_iota(jnp.int32, (1, WIDTH), 1) // PART

    def one_block(j, carry):
        a = wave_ref[pl.ds(2 * j, 1), :].astype(F32)
        b = wave_ref[pl.ds(2 * j + 1, 1), :].astype(F32)
        for part in range(2):
            shift = PART * part
            line = jnp.where(
                quarter < 2,
                jnp.where(quarter == 0, rolled(a, -shift), rolled(a, -PART - shift)),
                jnp.where(quarter == 2, rolled(b, 64 - shift), rolled(b, PART - shift)),
            )
            column = column_of(line)
            rows = pl.ds(pl.multiple_of(part * (K // 2) + j * WIDTH, WIDTH), WIDTH)
            for tile in range(K // WIDTH):
                onehot[rows, tile * WIDTH : (tile + 1) * WIDTH] = jnp.where(
                    column == lane + float(tile * WIDTH), 1.0, 0.0
                ).astype(BF16)
        return carry

    lax.fori_loop(0, K // (2 * WIDTH), one_block, 0)


def rolled(value, shift):
    shift = shift % WIDTH
    return pltpu.roll(value, shift, 1) if shift else value


def candidate_tables(owner_ref, block_ref, goal, named):
    owner = owner_ref[...]
    owned = jnp.where(
        lax.broadcasted_iota(jnp.int32, (BANDS, CANDS), 0) == owner, 1.0, 0.0
    )
    order = jnp.where(
        lax.broadcasted_iota(jnp.int32, (CANDS, CANDS), 0)
        < lax.broadcasted_iota(jnp.int32, (CANDS, CANDS), 1),
        1.0,
        0.0,
    ).astype(BF16)
    earlier = jnp.dot(owned.astype(BF16), order, preferred_element_type=F32)
    slot = jnp.sum(earlier * owned, axis=0, keepdims=True).astype(jnp.int32)
    second = jnp.where(slot >= PACK, 1, 0)
    target = (slot - PACK * second) * (2 * BANDS) + owner * 2 + second
    goal[...] = jnp.where(
        lax.broadcasted_iota(jnp.int32, (PACK * 2 * BANDS, CANDS), 0) == target, 1.0, 0.0
    ).astype(BF16)
    cells = jnp.where(
        lax.broadcasted_iota(jnp.int32, (256, CANDS), 0) == block_ref[...], 1.0, 0.0
    )
    named[...] = cells.T.astype(BF16)


def join_quad(quad, coeffs, ordered_in, at):
    quarter = lax.broadcasted_iota(jnp.int32, (ROWS, WIDTH), 1) // PART
    sources = [coeffs[4 * quad + k].astype(F32) for k in range(4)]
    rows = []
    for c in range(2):
        for x in range(2):
            group = 2 * x + c
            parts = [rolled(sources[k], (k - group) * PART) for k in range(4)]
            rows.append(
                jnp.where(
                    quarter < 2,
                    jnp.where(quarter == 0, parts[0], parts[1]),
                    jnp.where(quarter == 2, parts[2], parts[3]),
                )
            )
    ordered_in[:, at * WIDTH : (at + 1) * WIDTH] = jnp.concatenate(rows, axis=0).astype(BF16)


def order_slots(start, depth, begin, last, ordered_in, onehot, ordered, spread):
    pick = lax.broadcasted_iota(jnp.int32, (ROWS, WIDTH), 1) < 64
    rows = pl.ds(start, depth)
    for j in range(8):
        at = slice(256 * j, 256 * (j + 1))
        part = jnp.dot(
            ordered_in[:, :depth], onehot[rows, at], preferred_element_type=F32
        )
        if not begin:
            part = part + ordered[:, at]
        if not last:
            ordered[:, at] = part
            continue
        for tile in range(2):
            h = 4 * j + 2 * tile
            for c in range(2):
                a = part[c * 48 : c * 48 + 24, tile * WIDTH : (tile + 1) * WIDTH]
                b = part[c * 48 + 24 : c * 48 + 48, tile * WIDTH : (tile + 1) * WIDTH]
                to = h * 48 + c * 24
                spread[to : to + 24, :] = jnp.where(pick, a, pltpu.roll(b, 64, 1))
                spread[to + 48 : to + 72, :] = jnp.where(pick, pltpu.roll(a, 64, 1), b)


def synthesis(band, spread, tables, vort_out, okubo_out, table):
    first_ref, twiddle_ref, second_ref, fit_ref, fit_rows = tables
    southern = band >= BANDS // 2
    for pair in range(TIMES // 2):
        for r in range(4):
            row = jnp.where(southern, 3 - r, r)
            parts = []
            for f in range(3):
                i = f * 8 + r * 2 + pair
                c = jnp.concatenate(
                    [spread[pl.ds(i, 32, stride=48), :], spread[pl.ds(24 + i, 32, stride=48), :]],
                    axis=0,
                ).T.astype(BF16)
                z = jnp.dot(
                    jnp.concatenate([c, c], axis=1), first_ref[...], preferred_element_type=F32
                )
                zr, zi = z[:, :WIDTH], z[:, WIDTH:]
                tc, ts = twiddle_ref[0], twiddle_ref[1]
                parts.append(jnp.concatenate([zr * tc - zi * ts, zr * ts + zi * tc], axis=0))
            z = jnp.concatenate(parts, axis=1)
            high = z.astype(BF16)
            low = (z - high.astype(F32)).astype(BF16)
            grid = jnp.dot(
                second_ref[...],
                jnp.concatenate([high, high, low], axis=0),
                preferred_element_type=F32,
            )
            a = grid[:, :WIDTH]
            b = grid[:, WIDTH : 2 * WIDTH]
            normal = grid[:, 2 * WIDTH :]
            vort = a - b
            okubo = normal * normal + 4.0 * (a * b)
            for x in range(2):
                half = slice(64 * x, 64 * x + 64)
                vort_out[2 * pair + x, pl.ds(row, 64, stride=4), :] = vort[half]
                okubo_out[2 * pair + x, pl.ds(row, 64, stride=4), :] = okubo[half]
            both = jnp.concatenate([vort, okubo], axis=1)
            high = both.astype(BF16)
            low = (both - high.astype(F32)).astype(BF16)
            from_high = jnp.dot(high, fit_ref[...], preferred_element_type=F32)
            from_low = jnp.dot(low, fit_ref[...], preferred_element_type=F32)
            fits = from_high + pltpu.roll(from_high, WIDTH - 32, 1) + from_low
            fits = fits * fit_rows[pl.ds(row, 1), :]
            window = slice(128 * pair, 128 * pair + 128)
            if r == 0:
                table[window, :] = fits
            else:
                table[window, :] += fits


def pick_candidates(goal, named, table):
    values = table[...]
    high = values.astype(BF16).astype(F32)
    low = values - high
    chosen = jnp.dot(
        named[...],
        jnp.concatenate([high, low], axis=1).astype(BF16),
        preferred_element_type=F32,
    )
    total = jnp.zeros((2 * BANDS, 2 * WIDTH), F32)
    for g in range(PACK):
        high = chosen[:, :WIDTH]
        low = chosen[:, WIDTH:]
        if g:
            high = pltpu.roll(high, VALUES * g, 1)
            low = pltpu.roll(low, VALUES * g, 1)
        total += jnp.dot(
            goal[g * 2 * BANDS : (g + 1) * 2 * BANDS, :],
            jnp.concatenate([high, low], axis=1).astype(BF16),
            preferred_element_type=F32,
        )
    return total[:, :WIDTH] + total[:, WIDTH:]


def whole_kernel(
    spec_hbm,
    leg_hbm,
    wave_ref,
    owner_ref,
    block_ref,
    degree_ref,
    rows_ref,
    first_ref,
    twiddle_ref,
    second_ref,
    fit_ref,
    fit_rows,
    vort_out,
    okubo_out,
    fits_out,
    spec,
    leg,
    scaled,
    factor,
    columns,
    sums,
    turned,
    send,
    recv,
    onehot,
    goal,
    named,
    ordered_in,
    ordered,
    spread,
    vort,
    okubo,
    table,
    outgoing,
    arrived,
    lines,
    spec_sem,
    leg_sem,
    send_sem,
    recv_sem,
    send_fit,
    recv_fit,
    level_sem,
    out_sem,
):
    lev = lax.axis_index("lev")
    me = lax.axis_index("band")
    rank = lev * BANDS + me

    def spec_copy(g):
        window = pl.ds(pl.multiple_of(g * GROUP, GROUP), GROUP)
        return pltpu.make_async_copy(
            spec_hbm.at[:, window, :], spec.at[:, window, :], spec_sem.at[g]
        )

    def leg_copy(g):
        window = pl.ds(pl.multiple_of(g * GROUP, GROUP), GROUP)
        return pltpu.make_async_copy(leg_hbm.at[window], leg.at[window], leg_sem.at[g])

    for g in range(SLOTS // GROUP):
        spec_copy(g).start()
        leg_copy(g).start()

    barrier = pltpu.get_barrier_semaphore()
    greet_peers(barrier, lev, me)
    greet_band(barrier, lev, me)

    columns[...] = column_of(wave_ref[pl.ds(me // 2, 1), :].astype(F32))
    first = pl.multiple_of(lax.rem(me, 2) * SLOTS, SLOTS)
    waits = (lambda g: spec_copy(g).wait(), lambda g: leg_copy(g).wait())
    my_plane = me // PLANE
    my_place = lax.rem(me, PLANE)
    shifts = (0, 1, 3, 2)

    def place(d):
        return jnp.where(d < BANDS // 2, d, BANDS + BANDS // 2 - 1 - d)

    def one_half(half, carry):
        legendre_sums(
            (2 * half, 2 * half + 2),
            first,
            waits,
            spec,
            leg,
            degree_ref,
            columns,
            scaled,
            factor,
            sums,
        )
        combine_rows(
            pl.multiple_of(half * PART, PART), first, columns, rows_ref, sums, turned
        )
        for p in range(BANDS):
            send[half, p] = jnp.concatenate(
                [turned[q, p * 8 : p * 8 + 8, :] for q in range(3)], axis=0
            ).astype(BF16)

        @pl.when(half == 0)
        def _():
            pl.semaphore_wait(barrier, BANDS - 1 + LEVS - 1)

        for number, shift in enumerate(shifts):
            plane = lax.rem(my_plane + shift, PLANES)
            for k in range(0 if shift else 1, PLANE):
                d = plane * PLANE + lax.rem(my_place + k, PLANE)
                pltpu.make_async_remote_copy(
                    src_ref=send.at[half, place(d)],
                    dst_ref=recv.at[half, me],
                    send_sem=send_sem.at[half],
                    recv_sem=recv_sem.at[half * (1 + number)],
                    device_id={"lev": lev, "band": d},
                    device_id_type=MESH,
                ).start()
        recv[half, me] = send[half, place(me)]
        return carry

    lax.fori_loop(0, 2, one_half, 0)
    greet_peers(level_sem, lev, me)

    def bulk(half, count, number):
        return pltpu.make_async_remote_copy(
            src_ref=send.at[half, pl.ds(0, count)],
            dst_ref=recv.at[half, pl.ds(0, count)],
            send_sem=send_sem.at[half],
            recv_sem=recv_sem.at[number],
            device_id={"lev": lev, "band": me},
            device_id_type=MESH,
        )

    build_onehot(wave_ref, onehot)
    candidate_tables(owner_ref, block_ref, goal, named)

    bulk(0, BANDS - 1, 0).wait_recv()
    for quad in range(PLANE):
        join_quad(quad, recv.at[0], ordered_in, quad)
    order_slots(0, K // 2, True, False, ordered_in, onehot, ordered, spread)
    depth = PLANE * PART
    for number, shift in enumerate(shifts):
        plane = lax.rem(my_plane + PLANES - shift, PLANES)
        bulk(1, PLANE if shift else PLANE - 1, 1 + number).wait_recv()
        for k in range(2):
            join_quad(2 * plane + k, recv.at[1], ordered_in, k)
        start = pl.multiple_of(K // 2 + plane * depth, depth)
        order_slots(
            start, depth, False, number == PLANES - 1, ordered_in, onehot, ordered, spread
        )

    tables = (first_ref, twiddle_ref, second_ref, fit_ref, fit_rows)
    synthesis(me, spread, tables, vort, okubo, table)
    grid_copies = [
        pltpu.make_async_copy(vort, vort_out, out_sem.at[0]),
        pltpu.make_async_copy(okubo, okubo_out, out_sem.at[1]),
    ]
    for copy in grid_copies:
        copy.start()
    outgoing[...] = pick_candidates(goal, named, table).reshape(BANDS, 2, WIDTH)

    pl.semaphore_wait(level_sem, LEVS - 1)

    def post_fit(k, carry):
        other = lax.rem(rank + k, MEMBERS)
        owner = lax.rem(other, BANDS)
        pltpu.make_async_remote_copy(
            src_ref=outgoing.at[owner],
            dst_ref=arrived.at[rank],
            send_sem=send_fit,
            recv_sem=recv_fit,
            device_id={"lev": other // BANDS, "band": owner},
            device_id_type=MESH,
        ).start()
        return carry

    lax.fori_loop(1, MEMBERS, post_fit, 0, unroll=4)
    arrived[rank] = outgoing[me]
    everything = pltpu.make_async_remote_copy(
        src_ref=arrived.at[pl.ds(0, MEMBERS - 1)],
        dst_ref=arrived.at[pl.ds(0, MEMBERS - 1)],
        send_sem=send_fit,
        recv_sem=recv_fit,
        device_id={"lev": lev, "band": me},
        device_id_type=MESH,
    )
    everything.wait_recv()

    for r in range(CAP // PACK):
        line = (arrived[0:32, r, :] + arrived[32:64, r, :]) + (
            arrived[64:96, r, :] + arrived[96:128, r, :]
        )
        for g in range(PACK):
            value = pltpu.roll(line, WIDTH - VALUES * g, 1) if g else line
            lines[pl.ds(PACK * r + g, BANDS, stride=CAP), :] = value
    fits_out[...] = lines[...].T[:20, :]

    bulk(0, BANDS - 1, 0).wait_send()
    bulk(1, BANDS - 1, 0).wait_send()
    everything.wait_send()
    for copy in grid_copies:
        copy.wait()


def copy_kernel(*refs):
    sources, targets, held, come, go = refs[:3], refs[3:6], refs[6:9], refs[9], refs[10]
    pieces = [(i, t) for i in range(2) for t in range(TIMES)] + [(2, None)]

    def view(ref, t):
        return ref if t is None else ref.at[t]

    inward = [
        pltpu.make_async_copy(view(sources[i], t), view(held[i], t), come.at[n])
        for n, (i, t) in enumerate(pieces)
    ]
    outward = [
        pltpu.make_async_copy(view(held[i], t), view(targets[i], t), go.at[n])
        for n, (i, t) in enumerate(pieces)
    ]
    for copy in inward:
        copy.start()
    for n in range(len(pieces)):
        inward[n].wait()
        outward[n].start()
    for copy in outward:
        copy.wait()


def copied(*results):
    hbm = pl.BlockSpec(memory_space=pl.ANY)
    return pl.pallas_call(
        copy_kernel,
        out_shape=tuple(jax.ShapeDtypeStruct(r.shape, r.dtype) for r in results),
        in_specs=[hbm] * 3,
        out_specs=(hbm,) * 3,
        scratch_shapes=[pltpu.VMEM(r.shape, r.dtype) for r in results]
        + [pltpu.SemaphoreType.DMA((2 * TIMES + 1,)), pltpu.SemaphoreType.DMA((2 * TIMES + 1,))],
        compiler_params=pltpu.CompilerParams(vmem_limit_bytes=60 * 1024 * 1024),
        name="results",
    )(*results)


def whole(spectra, legendre, waves, owner, block):
    vmem = pl.BlockSpec(memory_space=pltpu.VMEM)
    hbm = pl.BlockSpec(memory_space=pl.ANY)
    fit_table, fit_rows = fit_tables()
    grid = jax.ShapeDtypeStruct((TIMES, 256, WIDTH), F32)
    return pl.pallas_call(
        whole_kernel,
        out_shape=(grid, grid, jax.ShapeDtypeStruct((20, BANDS * CAP), F32)),
        in_specs=[hbm, hbm] + [vmem] * 10,
        out_specs=(hbm, hbm, vmem),
        scratch_shapes=[
            pltpu.VMEM((16, SLOTS, K), BF16),
            pltpu.VMEM((SLOTS, HALF, K), BF16),
            pltpu.VMEM((K // WIDTH, 16 * GROUP, WIDTH), F32),
            pltpu.VMEM((GROUP, K), F32),
            pltpu.VMEM((WIDTH, WIDTH), F32),
            pltpu.VMEM((SLOTS * 16, WIDTH), F32),
            pltpu.VMEM((3, 2 * WIDTH, WIDTH), F32),
            pltpu.VMEM((2, BANDS, ROWS, WIDTH), BF16),
            pltpu.VMEM((2, BANDS, ROWS, WIDTH), BF16),
            pltpu.VMEM((K, K), BF16),
            pltpu.VMEM((PACK * 2 * BANDS, CANDS), BF16),
            pltpu.VMEM((CANDS, 256), BF16),
            pltpu.VMEM((96, K // 2), BF16),
            pltpu.VMEM((96, K), F32),
            pltpu.VMEM((32 * 48, WIDTH), F32),
            pltpu.VMEM((TIMES, 256, WIDTH), F32),
            pltpu.VMEM((TIMES, 256, WIDTH), F32),
            pltpu.VMEM((256, WIDTH), F32),
            pltpu.VMEM((BANDS, 2, WIDTH), F32),
            pltpu.VMEM((MEMBERS, 2, WIDTH), F32),
            pltpu.VMEM((BANDS * CAP, WIDTH), F32),
            pltpu.SemaphoreType.DMA((SLOTS // GROUP,)),
            pltpu.SemaphoreType.DMA((SLOTS // GROUP,)),
            pltpu.SemaphoreType.DMA((2,)),
            pltpu.SemaphoreType.DMA((1 + PLANES,)),
            pltpu.SemaphoreType.DMA,
            pltpu.SemaphoreType.DMA,
            pltpu.SemaphoreType.REGULAR,
            pltpu.SemaphoreType.DMA((2,)),
        ],
        compiler_params=pltpu.CompilerParams(
            collective_id=0, has_side_effects=True, vmem_limit_bytes=56 * 1024 * 1024
        ),
        name="spectral_analysis",
    )(
        spectra,
        legendre,
        waves,
        owner,
        block,
        degree_table(),
        row_table(),
        first_table(),
        twiddle_table(),
        second_table(),
        fit_table,
        fit_rows,
    )


def local(spectra, legendre, wave_order, cand_block, cand_owner):
    results = whole(
        spectra.reshape(16, SLOTS, K),
        legendre,
        wave_order.reshape(K // WIDTH, WIDTH),
        cand_owner.reshape(1, CANDS),
        cand_block.reshape(1, CANDS),
    )
    vort, okubo, fits = copied(*results)

    def rows(field):
        shaped = field.reshape(TIMES, 64, 4, WIDTH).transpose(0, 2, 1, 3)
        return shaped.reshape(1, TIMES, 4, NLON)

    return rows(vort), rows(okubo), fits.T


def solution(mesh):
    placed = (
        P("lev", None, None, None, "band", None),
        P("band", None, None),
        P(),
        P("band"),
        P("band", None),
    )
    return jax.shard_map(
        local,
        mesh=mesh,
        in_specs=placed,
        out_specs=(P("lev", None, "band", None), P("lev", None, "band", None), P("band", None)),
        check_vma=False,
    )
```

```python
import math

import jax
import jax.numpy as jnp
import ml_dtypes
import numpy as np
from jax import lax
from jax.experimental import pallas as pl
from jax.experimental.pallas import tpu as pltpu
from jax.sharding import PartitionSpec as P

MESH = pl.DeviceIdType.MESH
F32 = jnp.float32
BF16 = jnp.bfloat16

BANDS = 32
LEVS = 4
SLOTS = 64
K = 2048
NLON = 8192
HALF = 64
TIMES = 4
GROUP = 16
PART = 32
ROWS = 24
PLANE = 8
PLANES = 4
MEMBERS = 128
WIDTH = 128
CANDS = 192
CAP = 12
PACK = 6
VALUES = 20


def bf16_split(table):
    high = table.astype(np.float32).astype(ml_dtypes.bfloat16)
    low = (table - high.astype(np.float64)).astype(np.float32).astype(ml_dtypes.bfloat16)
    return high, low


def degree_table():
    n = np.arange(K, dtype=np.float32)
    inverse = np.where(n >= 1, np.float32(-1.0) / np.maximum(n * (n + 1), np.float32(1.0)), 0.0)
    table = np.zeros((8, K), np.float32)
    table[0] = inverse
    table[1] = np.where(np.arange(K) % 2 == 0, 1.0, -1.0)
    return table


def row_table():
    hy = math.pi / 4096.0
    j = np.arange(HALF)
    hx = np.cos((63.5 - j) * hy) * 2.0 * math.pi / NLON
    table = np.zeros((8, WIDTH), np.float64)
    table[0, :HALF] = table[0, HALF:] = 1.0 / (hx * hx)
    table[1, :HALF] = 1.0 / (4.0 * hx * hy)
    table[1, HALF:] = -1.0 / (4.0 * hx * hy)
    table[2] = 1.0 / (hy * hy)
    return table.astype(np.float32)


def first_table():
    h = np.arange(32)[:, None]
    x = np.arange(WIDTH)[None, :]
    angle = 2.0 * np.pi * ((h * x) % 128) / 128.0
    cos, sin = np.cos(angle), np.sin(angle)
    table = np.concatenate(
        [np.concatenate([cos, sin], 1), np.concatenate([-sin, cos], 1)], 0
    )
    high, low = bf16_split(table)
    return np.concatenate([high, low], 0)


def twiddle_table():
    low = np.arange(64)[:, None]
    x = np.arange(WIDTH)[None, :]
    angle = 2.0 * np.pi * (low * x) / NLON
    cos, sin = np.cos(angle), np.sin(angle)
    return np.stack([np.concatenate([cos, cos], 0), np.concatenate([sin, sin], 0)], 0).astype(
        np.float32
    )


def second_table():
    y = np.arange(64)[:, None]
    low = np.arange(64)[None, :]
    angle = 2.0 * np.pi * ((y * low) % 64) / 64.0
    cos, sin = np.cos(angle), -np.sin(angle)
    zero = np.zeros_like(cos)
    table = np.concatenate(
        [
            np.concatenate([cos, zero, sin, zero], 1),
            np.concatenate([zero, cos, zero, sin], 1),
        ],
        0,
    )
    high, low_part = bf16_split(table)
    return np.concatenate([high, low_part, high], 1)


ORDERS = ((0, 0), (1, 0), (0, 1), (2, 0), (1, 1), (0, 2), (3, 0), (2, 1), (1, 2), (0, 3))


def ortho_values(count):
    u = np.arange(count, dtype=np.float64) - (count - 1) / 2.0
    q = np.stack(
        [
            np.ones_like(u),
            u,
            u * u - (count * count - 1) / 12.0,
            u * u * u - (3 * count * count - 7) / 20.0 * u,
        ],
        0,
    )
    return q / np.sqrt(np.sum(q * q, 1, keepdims=True))


def fit_tables():
    across, upward = ortho_values(WIDTH), ortho_values(4)
    columns = np.stack([across[a] for a, _ in ORDERS], 1)
    table = np.zeros((256, 32), np.float64)
    table[:128, 0:10] = columns
    table[128:, 10:20] = columns
    high, low = bf16_split(table)
    both = np.zeros((256, 128), high.dtype)
    both[:, 0:32] = high
    both[:, 32:64] = low
    rows = np.zeros((8, 128), np.float32)
    for r in range(4):
        line = [upward[b][r] / 4.0 for _, b in ORDERS]
        rows[r, 0:10] = line
        rows[r, 10:20] = line
    return both, rows


def column_of(row):
    return jnp.broadcast_to(row, (WIDTH, WIDTH)).T


def greet_peers(semaphore, lev, me):
    for k in range(1, LEVS):
        pl.semaphore_signal(
            semaphore,
            inc=1,
            device_id={"lev": lax.rem(lev + k, LEVS), "band": me},
            device_id_type=MESH,
        )


def greet_band(semaphore, lev, me):
    def greet(k, carry):
        pl.semaphore_signal(
            semaphore,
            inc=1,
            device_id={"lev": lev, "band": lax.rem(me + k, BANDS)},
            device_id_type=MESH,
        )
        return carry

    lax.fori_loop(1, BANDS, greet, 0)


def legendre_sums(groups, first, waits, spec, leg, degree_ref, columns, scaled, factor, sums):
    spec_wait, leg_wait = waits
    lane = lax.broadcasted_iota(jnp.int32, (1, K), 1).astype(F32)

    def one_group(g, carry):
        spec_wait(g)
        start = pl.multiple_of(g * GROUP, GROUP)
        own = columns[pl.ds(pl.multiple_of(first + start, GROUP), GROUP), :]
        own = jnp.concatenate([own] * (K // WIDTH), axis=1)
        factor[...] = jnp.where(lane >= own, degree_ref[0:1, :], 0.0)

        def scale(q, inner):
            part = spec[q, pl.ds(start, GROUP), :].astype(F32) * factor[...]
            window = pl.ds(pl.multiple_of(q * GROUP, GROUP), GROUP)
            for tile in range(K // WIDTH):
                scaled[tile, window, :] = part[:, tile * WIDTH : (tile + 1) * WIDTH]
            return inner

        lax.fori_loop(0, 16, scale, 0, unroll=4)

        def one_slot(i, inner):
            even = jnp.concatenate(
                [scaled[tile, pl.ds(i, 16, stride=GROUP), :] for tile in range(K // WIDTH)],
                axis=1,
            )
            odd = even * degree_ref[1:2, :]
            both = jnp.concatenate([even.astype(BF16), odd.astype(BF16)], axis=0)
            result = lax.dot_general(
                both,
                leg[start + i],
                (((1,), (1,)), ((), ())),
                preferred_element_type=F32,
            )
            result = result.astype(BF16).astype(F32)
            sums[pl.ds(pl.multiple_of((start + i) * 16, 16), 16), :] = jnp.concatenate(
                [result[:16], result[16:]], axis=1
            )
            return inner

        leg_wait(g)
        lax.fori_loop(0, GROUP, one_slot, 0, unroll=GROUP)
        return carry

    lax.fori_loop(groups[0], groups[1], one_group, 0)


def combine_rows(start, first, columns, rows_ref, sums, turned):
    m = columns[pl.ds(pl.multiple_of(first + start, PART), PART), :]
    lanes = lax.broadcasted_iota(jnp.int32, (PART, WIDTH), 1)
    half_m = jnp.floor(m * 0.5)
    parity = 1.0 - 2.0 * (m - 2.0 * half_m)
    weight = jnp.where(m == 0.0, 1.0, 2.0)
    sign = jnp.where(lanes >= HALF, parity, 1.0) * weight
    x = m * (math.pi / NLON)
    x2 = x * x
    sin = x * (
        1.0
        + x2 * (-1.0 / 6 + x2 * (1.0 / 120 + x2 * (-1.0 / 5040 + x2 * (1.0 / 362880))))
    )
    cos = 1.0 + x2 * (
        -0.5
        + x2 * (1.0 / 24 + x2 * (-1.0 / 720 + x2 * (1.0 / 40320 - x2 * (1.0 / 3628800))))
    )
    xx = -4.0 * sin * sin * rows_ref[0:1, :]
    xy = 2.0 * (2.0 * sin * cos) * rows_ref[1:2, :]
    yy = rows_ref[2:3, :]
    first_lane = (lanes == 0) | (lanes == HALF)
    last_lane = (lanes == HALF - 1) | (lanes == WIDTH - 1)

    def fields(t):
        def pieces(q):
            c = sums[pl.ds(start * 16 + t * 4 + q, PART, stride=16), :] * sign
            before = jnp.where(first_lane, 0.0, pltpu.roll(c, 1, 1))
            after = jnp.where(last_lane, pltpu.roll(c, HALF, 1), pltpu.roll(c, WIDTH - 1, 1))
            return c * xx, (before + after - 2.0 * c) * yy, (before - after) * xy

        pr_xx, pr_yy, pr_xy = pieces(0)
        pi_xx, pi_yy, pi_xy = pieces(1)
        cr_xx, cr_yy, cr_xy = pieces(2)
        ci_xx, ci_yy, ci_xy = pieces(3)
        a = (pr_xx - ci_xy, pi_xx + cr_xy)
        b = (-ci_xy - pr_yy, cr_xy - pi_yy)
        normal = (2.0 * pi_xy + cr_xx - cr_yy, -2.0 * pr_xy + ci_xx - ci_yy)
        return a, b, normal

    for pair in range(TIMES // 2):
        early, late = fields(2 * pair), fields(2 * pair + 1)
        for q in range(3):
            block = jnp.concatenate(early[q] + late[q], axis=0).T
            turned[q, pl.ds(pair, WIDTH, stride=2), :] = block


def build_onehot(wave_ref, onehot):
    lane = lax.broadcasted_iota(jnp.int32, (WIDTH, WIDTH), 1).astype(F32)
    quarter = lax.broadcasted_iota(jnp.int32, (1, WIDTH), 1) // PART

    def one_block(j, carry):
        a = wave_ref[pl.ds(2 * j, 1), :].astype(F32)
        b = wave_ref[pl.ds(2 * j + 1, 1), :].astype(F32)
        for part in range(2):
            shift = PART * part
            line = jnp.where(
                quarter < 2,
                jnp.where(quarter == 0, rolled(a, -shift), rolled(a, -PART - shift)),
                jnp.where(quarter == 2, rolled(b, 64 - shift), rolled(b, PART - shift)),
            )
            column = column_of(line)
            rows = pl.ds(pl.multiple_of(part * (K // 2) + j * WIDTH, WIDTH), WIDTH)
            for tile in range(K // WIDTH):
                onehot[rows, tile * WIDTH : (tile + 1) * WIDTH] = jnp.where(
                    column == lane + float(tile * WIDTH), 1.0, 0.0
                ).astype(BF16)
        return carry

    lax.fori_loop(0, K // (2 * WIDTH), one_block, 0)


def rolled(value, shift):
    shift = shift % WIDTH
    return pltpu.roll(value, shift, 1) if shift else value


def candidate_tables(owner_ref, block_ref, goal, named):
    owner = owner_ref[...]
    owned = jnp.where(
        lax.broadcasted_iota(jnp.int32, (BANDS, CANDS), 0) == owner, 1.0, 0.0
    )
    order = jnp.where(
        lax.broadcasted_iota(jnp.int32, (CANDS, CANDS), 0)
        < lax.broadcasted_iota(jnp.int32, (CANDS, CANDS), 1),
        1.0,
        0.0,
    ).astype(BF16)
    earlier = jnp.dot(owned.astype(BF16), order, preferred_element_type=F32)
    slot = jnp.sum(earlier * owned, axis=0, keepdims=True).astype(jnp.int32)
    second = jnp.where(slot >= PACK, 1, 0)
    target = (slot - PACK * second) * (2 * BANDS) + owner * 2 + second
    goal[...] = jnp.where(
        lax.broadcasted_iota(jnp.int32, (PACK * 2 * BANDS, CANDS), 0) == target, 1.0, 0.0
    ).astype(BF16)
    cells = jnp.where(
        lax.broadcasted_iota(jnp.int32, (256, CANDS), 0) == block_ref[...], 1.0, 0.0
    )
    named[...] = cells.T.astype(BF16)


def join_quad(quad, coeffs, ordered_in, at):
    quarter = lax.broadcasted_iota(jnp.int32, (ROWS, WIDTH), 1) // PART
    sources = [coeffs[4 * quad + k].astype(F32) for k in range(4)]
    rows = []
    for c in range(2):
        for x in range(2):
            group = 2 * x + c
            parts = [rolled(sources[k], (k - group) * PART) for k in range(4)]
            rows.append(
                jnp.where(
                    quarter < 2,
                    jnp.where(quarter == 0, parts[0], parts[1]),
                    jnp.where(quarter == 2, parts[2], parts[3]),
                )
            )
    ordered_in[:, at * WIDTH : (at + 1) * WIDTH] = jnp.concatenate(rows, axis=0).astype(BF16)


def order_slots(start, depth, begin, last, ordered_in, onehot, ordered, spread):
    pick = lax.broadcasted_iota(jnp.int32, (ROWS, WIDTH), 1) < 64
    rows = pl.ds(start, depth)
    for j in range(8):
        at = slice(256 * j, 256 * (j + 1))
        part = jnp.dot(
            ordered_in[:, :depth], onehot[rows, at], preferred_element_type=F32
        )
        if not begin:
            part = part + ordered[:, at]
        if not last:
            ordered[:, at] = part
            continue
        for tile in range(2):
            h = 4 * j + 2 * tile
            for c in range(2):
                a = part[c * 48 : c * 48 + 24, tile * WIDTH : (tile + 1) * WIDTH]
                b = part[c * 48 + 24 : c * 48 + 48, tile * WIDTH : (tile + 1) * WIDTH]
                to = h * 48 + c * 24
                spread[to : to + 24, :] = jnp.where(pick, a, pltpu.roll(b, 64, 1))
                spread[to + 48 : to + 72, :] = jnp.where(pick, pltpu.roll(a, 64, 1), b)


def synthesis(band, spread, tables, vort_out, okubo_out, table, stage, cells):
    first_ref, twiddle_ref, second_ref, fit_ref, fit_rows = tables
    southern = band >= BANDS // 2
    steps = [(pair, r) for pair in range(TIMES // 2) for r in range(4)]
    tc, ts = twiddle_ref[0], twiddle_ref[1]
    for n, (pair, r) in enumerate(steps):
        for f in range(3):
            i = f * 8 + r * 2 + pair
            c = jnp.concatenate(
                [spread[pl.ds(i, 32, stride=48), :], spread[pl.ds(24 + i, 32, stride=48), :]],
                axis=0,
            ).T.astype(BF16)
            z = jnp.dot(
                jnp.concatenate([c, c], axis=1), first_ref[...], preferred_element_type=F32
            )
            zr, zi = z[:, :WIDTH], z[:, WIDTH:]
            z = jnp.concatenate([zr * tc - zi * ts, zr * ts + zi * tc], axis=0)
            high = z.astype(BF16)
            low = (z - high.astype(F32)).astype(BF16)
            at = slice(f * WIDTH, (f + 1) * WIDTH)
            stage[n, 0:256, at] = high
            stage[n, 256:512, at] = low
    for n, (pair, r) in enumerate(steps):
        row = jnp.where(southern, 3 - r, r)
        grid = jnp.dot(
            second_ref[...],
            jnp.concatenate([stage[n, 0:256, :], stage[n]], axis=0),
            preferred_element_type=F32,
        )
        a = grid[:, :WIDTH]
        b = grid[:, WIDTH : 2 * WIDTH]
        normal = grid[:, 2 * WIDTH :]
        vort = a - b
        okubo = normal * normal + 4.0 * (a * b)
        for x in range(2):
            half = slice(64 * x, 64 * x + 64)
            vort_out[2 * pair + x, pl.ds(row, 64, stride=4), :] = vort[half]
            okubo_out[2 * pair + x, pl.ds(row, 64, stride=4), :] = okubo[half]
        both = jnp.concatenate([vort, okubo], axis=1)
        high = both.astype(BF16)
        cells[n, 0:128, :] = high
        cells[n, 128:256, :] = (both - high.astype(F32)).astype(BF16)
    for pair in range(TIMES // 2):
        total = jnp.zeros((WIDTH, WIDTH), F32)
        for r in range(4):
            row = jnp.where(southern, 3 - r, r)
            both = jnp.dot(cells[4 * pair + r], fit_ref[...], preferred_element_type=F32)
            high, low = both[:WIDTH], both[WIDTH:]
            fits = high + pltpu.roll(high, WIDTH - 32, 1) + low
            total += fits * fit_rows[pl.ds(row, 1), :]
        table[128 * pair : 128 * pair + 128, :] = total


def pick_candidates(goal, named, table):
    values = table[...]
    high = values.astype(BF16).astype(F32)
    low = values - high
    chosen = jnp.dot(
        named[...],
        jnp.concatenate([high, low], axis=1).astype(BF16),
        preferred_element_type=F32,
    )
    total = jnp.zeros((2 * BANDS, 2 * WIDTH), F32)
    for g in range(PACK):
        high = chosen[:, :WIDTH]
        low = chosen[:, WIDTH:]
        if g:
            high = pltpu.roll(high, VALUES * g, 1)
            low = pltpu.roll(low, VALUES * g, 1)
        total += jnp.dot(
            goal[g * 2 * BANDS : (g + 1) * 2 * BANDS, :],
            jnp.concatenate([high, low], axis=1).astype(BF16),
            preferred_element_type=F32,
        )
    return total[:, :WIDTH] + total[:, WIDTH:]


def whole_kernel(
    spec_hbm,
    leg_hbm,
    wave_hbm,
    owner_hbm,
    block_hbm,
    degree_hbm,
    rows_hbm,
    first_hbm,
    twiddle_hbm,
    second_hbm,
    fit_hbm,
    fit_rows_hbm,
    vort_out,
    okubo_out,
    fits_out,
    wave_ref,
    owner_ref,
    block_ref,
    degree_ref,
    rows_ref,
    first_ref,
    twiddle_ref,
    second_ref,
    fit_ref,
    fit_rows,
    spec,
    leg,
    scaled,
    factor,
    columns,
    sums,
    turned,
    send,
    recv,
    onehot,
    goal,
    named,
    ordered_in,
    ordered,
    spread,
    vort,
    okubo,
    table,
    stage,
    cells,
    outgoing,
    arrived,
    lines,
    spec_sem,
    leg_sem,
    send_sem,
    recv_sem,
    send_fit,
    recv_fit,
    level_sem,
    out_sem,
    table_sem,
):
    lev = lax.axis_index("lev")
    me = lax.axis_index("band")
    rank = lev * BANDS + me

    def spec_copy(g):
        window = pl.ds(pl.multiple_of(g * GROUP, GROUP), GROUP)
        return pltpu.make_async_copy(
            spec_hbm.at[:, window, :], spec.at[:, window, :], spec_sem.at[g]
        )

    def leg_copy(g):
        window = pl.ds(pl.multiple_of(g * GROUP, GROUP), GROUP)
        return pltpu.make_async_copy(leg_hbm.at[window], leg.at[window], leg_sem.at[g])

    table_copies = [
        pltpu.make_async_copy(source, target, table_sem.at[n])
        for n, (source, target) in enumerate(
            (
                (wave_hbm, wave_ref),
                (degree_hbm, degree_ref),
                (rows_hbm, rows_ref),
                (owner_hbm, owner_ref),
                (block_hbm, block_ref),
                (first_hbm, first_ref),
                (twiddle_hbm, twiddle_ref),
                (second_hbm, second_ref),
                (fit_hbm, fit_ref),
                (fit_rows_hbm, fit_rows),
            )
        )
    ]
    for copy in table_copies[:3]:
        copy.start()
    for g in range(SLOTS // GROUP):
        spec_copy(g).start()
        leg_copy(g).start()
    for copy in table_copies[3:]:
        copy.start()

    barrier = pltpu.get_barrier_semaphore()
    greet_peers(barrier, lev, me)
    greet_band(barrier, lev, me)

    for copy in table_copies[:3]:
        copy.wait()
    columns[...] = column_of(wave_ref[pl.ds(me // 2, 1), :].astype(F32))
    first = pl.multiple_of(lax.rem(me, 2) * SLOTS, SLOTS)
    waits = (lambda g: spec_copy(g).wait(), lambda g: leg_copy(g).wait())
    my_plane = me // PLANE
    my_place = lax.rem(me, PLANE)
    shifts = (0, 1, 3, 2)

    def place(d):
        return jnp.where(d < BANDS // 2, d, BANDS + BANDS // 2 - 1 - d)

    def one_half(half, carry):
        legendre_sums(
            (2 * half, 2 * half + 2),
            first,
            waits,
            spec,
            leg,
            degree_ref,
            columns,
            scaled,
            factor,
            sums,
        )
        combine_rows(
            pl.multiple_of(half * PART, PART), first, columns, rows_ref, sums, turned
        )
        for p in range(BANDS):
            send[half, p] = jnp.concatenate(
                [turned[q, p * 8 : p * 8 + 8, :] for q in range(3)], axis=0
            ).astype(BF16)

        @pl.when(half == 0)
        def _():
            pl.semaphore_wait(barrier, BANDS - 1 + LEVS - 1)

        for number, shift in enumerate(shifts):
            plane = lax.rem(my_plane + shift, PLANES)
            for k in range(0 if shift else 1, PLANE):
                d = plane * PLANE + lax.rem(my_place + k, PLANE)
                pltpu.make_async_remote_copy(
                    src_ref=send.at[half, place(d)],
                    dst_ref=recv.at[half, me],
                    send_sem=send_sem.at[half],
                    recv_sem=recv_sem.at[half * (1 + number)],
                    device_id={"lev": lev, "band": d},
                    device_id_type=MESH,
                ).start()
        recv[half, me] = send[half, place(me)]
        return carry

    lax.fori_loop(0, 2, one_half, 0)
    greet_peers(level_sem, lev, me)

    def bulk(half, count, number):
        return pltpu.make_async_remote_copy(
            src_ref=send.at[half, pl.ds(0, count)],
            dst_ref=recv.at[half, pl.ds(0, count)],
            send_sem=send_sem.at[half],
            recv_sem=recv_sem.at[number],
            device_id={"lev": lev, "band": me},
            device_id_type=MESH,
        )

    build_onehot(wave_ref, onehot)
    for copy in table_copies[3:]:
        copy.wait()
    candidate_tables(owner_ref, block_ref, goal, named)

    bulk(0, BANDS - 1, 0).wait_recv()
    for quad in range(PLANE):
        join_quad(quad, recv.at[0], ordered_in, quad)
    order_slots(0, K // 2, True, False, ordered_in, onehot, ordered, spread)
    depth = PLANE * PART
    for number, shift in enumerate(shifts):
        plane = lax.rem(my_plane + PLANES - shift, PLANES)
        bulk(1, PLANE if shift else PLANE - 1, 1 + number).wait_recv()
        for k in range(2):
            join_quad(2 * plane + k, recv.at[1], ordered_in, k)
        start = pl.multiple_of(K // 2 + plane * depth, depth)
        order_slots(
            start, depth, False, number == PLANES - 1, ordered_in, onehot, ordered, spread
        )

    tables = (first_ref, twiddle_ref, second_ref, fit_ref, fit_rows)
    synthesis(me, spread, tables, vort, okubo, table, stage, cells)
    grid_copies = [
        pltpu.make_async_copy(vort, vort_out, out_sem.at[0]),
        pltpu.make_async_copy(okubo, okubo_out, out_sem.at[1]),
    ]
    for copy in grid_copies:
        copy.start()
    outgoing[...] = pick_candidates(goal, named, table).reshape(BANDS, 2, WIDTH)

    pl.semaphore_wait(level_sem, LEVS - 1)

    def post_fit(k, carry):
        other = lax.rem(rank + k, MEMBERS)
        owner = lax.rem(other, BANDS)
        pltpu.make_async_remote_copy(
            src_ref=outgoing.at[owner],
            dst_ref=arrived.at[rank],
            send_sem=send_fit,
            recv_sem=recv_fit,
            device_id={"lev": other // BANDS, "band": owner},
            device_id_type=MESH,
        ).start()
        return carry

    lax.fori_loop(1, MEMBERS, post_fit, 0, unroll=4)
    arrived[rank] = outgoing[me]
    everything = pltpu.make_async_remote_copy(
        src_ref=arrived.at[pl.ds(0, MEMBERS - 1)],
        dst_ref=arrived.at[pl.ds(0, MEMBERS - 1)],
        send_sem=send_fit,
        recv_sem=recv_fit,
        device_id={"lev": lev, "band": me},
        device_id_type=MESH,
    )
    everything.wait_recv()

    for r in range(CAP // PACK):
        line = (arrived[0:32, r, :] + arrived[32:64, r, :]) + (
            arrived[64:96, r, :] + arrived[96:128, r, :]
        )
        for g in range(PACK):
            value = pltpu.roll(line, WIDTH - VALUES * g, 1) if g else line
            lines[pl.ds(PACK * r + g, BANDS, stride=CAP), :] = value
    fits_out[...] = lines[...].T[:20, :]

    bulk(0, BANDS - 1, 0).wait_send()
    bulk(1, BANDS - 1, 0).wait_send()
    everything.wait_send()
    for copy in grid_copies:
        copy.wait()


def copy_kernel(*refs):
    sources, targets, held, come, go = refs[:3], refs[3:6], refs[6:9], refs[9], refs[10]
    pieces = [(i, t) for i in range(2) for t in range(TIMES)] + [(2, None)]

    def view(ref, t):
        return ref if t is None else ref.at[t]

    inward = [
        pltpu.make_async_copy(view(sources[i], t), view(held[i], t), come.at[n])
        for n, (i, t) in enumerate(pieces)
    ]
    outward = [
        pltpu.make_async_copy(view(held[i], t), view(targets[i], t), go.at[n])
        for n, (i, t) in enumerate(pieces)
    ]
    for copy in inward:
        copy.start()
    for n in range(len(pieces)):
        inward[n].wait()
        outward[n].start()
    for copy in outward:
        copy.wait()


def copied(*results):
    hbm = pl.BlockSpec(memory_space=pl.ANY)
    return pl.pallas_call(
        copy_kernel,
        out_shape=tuple(jax.ShapeDtypeStruct(r.shape, r.dtype) for r in results),
        in_specs=[hbm] * 3,
        out_specs=(hbm,) * 3,
        scratch_shapes=[pltpu.VMEM(r.shape, r.dtype) for r in results]
        + [pltpu.SemaphoreType.DMA((2 * TIMES + 1,)), pltpu.SemaphoreType.DMA((2 * TIMES + 1,))],
        compiler_params=pltpu.CompilerParams(vmem_limit_bytes=60 * 1024 * 1024),
        name="results",
    )(*results)


def whole(spectra, legendre, waves, owner, block):
    vmem = pl.BlockSpec(memory_space=pltpu.VMEM)
    hbm = pl.BlockSpec(memory_space=pl.ANY)
    fit_table, fit_rows = fit_tables()
    grid = jax.ShapeDtypeStruct((TIMES, 256, WIDTH), F32)
    return pl.pallas_call(
        whole_kernel,
        out_shape=(grid, grid, jax.ShapeDtypeStruct((20, BANDS * CAP), F32)),
        in_specs=[hbm] * 12,
        out_specs=(hbm, hbm, vmem),
        scratch_shapes=[
            pltpu.VMEM((K // WIDTH, WIDTH), jnp.int32),
            pltpu.VMEM((1, CANDS), jnp.int32),
            pltpu.VMEM((1, CANDS), jnp.int32),
            pltpu.VMEM((8, K), F32),
            pltpu.VMEM((8, WIDTH), F32),
            pltpu.VMEM((WIDTH, 2 * WIDTH), BF16),
            pltpu.VMEM((2, WIDTH, WIDTH), F32),
            pltpu.VMEM((WIDTH, 6 * WIDTH), BF16),
            pltpu.VMEM((2 * WIDTH, WIDTH), BF16),
            pltpu.VMEM((8, WIDTH), F32),
            pltpu.VMEM((16, SLOTS, K), BF16),
            pltpu.VMEM((SLOTS, HALF, K), BF16),
            pltpu.VMEM((K // WIDTH, 16 * GROUP, WIDTH), F32),
            pltpu.VMEM((GROUP, K), F32),
            pltpu.VMEM((WIDTH, WIDTH), F32),
            pltpu.VMEM((SLOTS * 16, WIDTH), F32),
            pltpu.VMEM((3, 2 * WIDTH, WIDTH), F32),
            pltpu.VMEM((2, BANDS, ROWS, WIDTH), BF16),
            pltpu.VMEM((2, BANDS, ROWS, WIDTH), BF16),
            pltpu.VMEM((K, K), BF16),
            pltpu.VMEM((PACK * 2 * BANDS, CANDS), BF16),
            pltpu.VMEM((CANDS, 256), BF16),
            pltpu.VMEM((96, K // 2), BF16),
            pltpu.VMEM((96, K), F32),
            pltpu.VMEM((32 * 48, WIDTH), F32),
            pltpu.VMEM((TIMES, 256, WIDTH), F32),
            pltpu.VMEM((TIMES, 256, WIDTH), F32),
            pltpu.VMEM((256, WIDTH), F32),
            pltpu.VMEM((8, 512, 3 * WIDTH), BF16),
            pltpu.VMEM((8, 256, 256), BF16),
            pltpu.VMEM((BANDS, 2, WIDTH), F32),
            pltpu.VMEM((MEMBERS, 2, WIDTH), F32),
            pltpu.VMEM((BANDS * CAP, WIDTH), F32),
            pltpu.SemaphoreType.DMA((SLOTS // GROUP,)),
            pltpu.SemaphoreType.DMA((SLOTS // GROUP,)),
            pltpu.SemaphoreType.DMA((2,)),
            pltpu.SemaphoreType.DMA((1 + PLANES,)),
            pltpu.SemaphoreType.DMA,
            pltpu.SemaphoreType.DMA,
            pltpu.SemaphoreType.REGULAR,
            pltpu.SemaphoreType.DMA((2,)),
            pltpu.SemaphoreType.DMA((10,)),
        ],
        compiler_params=pltpu.CompilerParams(
            collective_id=0, has_side_effects=True, vmem_limit_bytes=56 * 1024 * 1024
        ),
        name="spectral_analysis",
    )(
        spectra,
        legendre,
        waves,
        owner,
        block,
        degree_table(),
        row_table(),
        first_table(),
        twiddle_table(),
        second_table(),
        fit_table,
        fit_rows,
    )


def local(spectra, legendre, wave_order, cand_block, cand_owner):
    results = whole(
        spectra.reshape(16, SLOTS, K),
        legendre,
        wave_order.reshape(K // WIDTH, WIDTH),
        cand_owner.reshape(1, CANDS),
        cand_block.reshape(1, CANDS),
    )
    vort, okubo, fits = copied(*results)

    def rows(field):
        shaped = field.reshape(TIMES, 64, 4, WIDTH).transpose(0, 2, 1, 3)
        return shaped.reshape(1, TIMES, 4, NLON)

    return rows(vort), rows(okubo), fits.T


def solution(mesh):
    placed = (
        P("lev", None, None, None, "band", None),
        P("band", None, None),
        P(),
        P("band"),
        P("band", None),
    )
    return jax.shard_map(
        local,
        mesh=mesh,
        in_specs=placed,
        out_specs=(P("lev", None, "band", None), P("lev", None, "band", None), P("band", None)),
        check_vma=False,
    )
```

```python
import math

import jax
import jax.numpy as jnp
import ml_dtypes
import numpy as np
from jax import lax
from jax.experimental import pallas as pl
from jax.experimental.pallas import tpu as pltpu
from jax.sharding import PartitionSpec as P

MESH = pl.DeviceIdType.MESH
F32 = jnp.float32
BF16 = jnp.bfloat16

BANDS = 32
LEVS = 4
SLOTS = 64
K = 2048
NLON = 8192
HALF = 64
TIMES = 4
GROUP = 16
PART = 32
ROWS = 24
PLANE = 8
PLANES = 4
MEMBERS = 128
WIDTH = 128
CANDS = 192
CAP = 12
PACK = 6
VALUES = 20


def bf16_split(table):
    high = table.astype(np.float32).astype(ml_dtypes.bfloat16)
    low = (table - high.astype(np.float64)).astype(np.float32).astype(ml_dtypes.bfloat16)
    return high, low


def degree_table():
    n = np.arange(K, dtype=np.float32)
    inverse = np.where(n >= 1, np.float32(-1.0) / np.maximum(n * (n + 1), np.float32(1.0)), 0.0)
    table = np.zeros((8, K), np.float32)
    table[0] = inverse
    table[1] = np.where(np.arange(K) % 2 == 0, 1.0, -1.0)
    return table


def row_table():
    hy = math.pi / 4096.0
    j = np.arange(HALF)
    hx = np.cos((63.5 - j) * hy) * 2.0 * math.pi / NLON
    table = np.zeros((8, WIDTH), np.float64)
    table[0, :HALF] = table[0, HALF:] = 1.0 / (hx * hx)
    table[1, :HALF] = 1.0 / (4.0 * hx * hy)
    table[1, HALF:] = -1.0 / (4.0 * hx * hy)
    table[2] = 1.0 / (hy * hy)
    return table.astype(np.float32)


def first_table():
    h = np.arange(32)[:, None]
    x = np.arange(WIDTH)[None, :]
    angle = 2.0 * np.pi * ((h * x) % 128) / 128.0
    cos, sin = np.cos(angle), np.sin(angle)
    table = np.concatenate(
        [np.concatenate([cos, sin], 1), np.concatenate([-sin, cos], 1)], 0
    )
    high, low = bf16_split(table)
    return np.concatenate([high, low], 0)


def twiddle_table():
    low = np.arange(64)[:, None]
    x = np.arange(WIDTH)[None, :]
    angle = 2.0 * np.pi * (low * x) / NLON
    cos, sin = np.cos(angle), np.sin(angle)
    return np.stack([np.concatenate([cos, cos], 0), np.concatenate([sin, sin], 0)], 0).astype(
        np.float32
    )


def second_table():
    y = np.arange(64)[:, None]
    low = np.arange(64)[None, :]
    angle = 2.0 * np.pi * ((y * low) % 64) / 64.0
    cos, sin = np.cos(angle), -np.sin(angle)
    zero = np.zeros_like(cos)
    table = np.concatenate(
        [
            np.concatenate([cos, zero, sin, zero], 1),
            np.concatenate([zero, cos, zero, sin], 1),
        ],
        0,
    )
    high, low_part = bf16_split(table)
    return np.concatenate([high, low_part, high], 1)


ORDERS = ((0, 0), (1, 0), (0, 1), (2, 0), (1, 1), (0, 2), (3, 0), (2, 1), (1, 2), (0, 3))


def ortho_values(count):
    u = np.arange(count, dtype=np.float64) - (count - 1) / 2.0
    q = np.stack(
        [
            np.ones_like(u),
            u,
            u * u - (count * count - 1) / 12.0,
            u * u * u - (3 * count * count - 7) / 20.0 * u,
        ],
        0,
    )
    return q / np.sqrt(np.sum(q * q, 1, keepdims=True))


def fit_tables():
    across, upward = ortho_values(WIDTH), ortho_values(4)
    columns = np.stack([across[a] for a, _ in ORDERS], 1)
    table = np.zeros((256, 32), np.float64)
    table[:128, 0:10] = columns
    table[128:, 10:20] = columns
    high, low = bf16_split(table)
    both = np.zeros((256, 128), high.dtype)
    both[:, 0:32] = high
    both[:, 32:64] = low
    rows = np.zeros((8, 128), np.float32)
    for r in range(4):
        line = [upward[b][r] / 4.0 for _, b in ORDERS]
        rows[r, 0:10] = line
        rows[r, 10:20] = line
    return both, rows


def column_of(row):
    return jnp.broadcast_to(row, (WIDTH, WIDTH)).T


def greet_peers(semaphore, lev, me):
    for k in range(1, LEVS):
        pl.semaphore_signal(
            semaphore,
            inc=1,
            device_id={"lev": lax.rem(lev + k, LEVS), "band": me},
            device_id_type=MESH,
        )


def greet_band(semaphore, lev, me):
    def greet(k, carry):
        pl.semaphore_signal(
            semaphore,
            inc=1,
            device_id={"lev": lev, "band": lax.rem(me + k, BANDS)},
            device_id_type=MESH,
        )
        return carry

    lax.fori_loop(1, BANDS, greet, 0)


def legendre_sums(groups, first, waits, spec, leg, degree_ref, columns, scaled, factor, sums):
    spec_wait, leg_wait = waits
    lane = lax.broadcasted_iota(jnp.int32, (1, K), 1).astype(F32)

    def one_group(g, carry):
        spec_wait(g)
        start = pl.multiple_of(g * GROUP, GROUP)
        own = columns[pl.ds(pl.multiple_of(first + start, GROUP), GROUP), :]
        own = jnp.concatenate([own] * (K // WIDTH), axis=1)
        factor[...] = jnp.where(lane >= own, degree_ref[0:1, :], 0.0)

        def scale(q, inner):
            part = spec[q, pl.ds(start, GROUP), :].astype(F32) * factor[...]
            window = pl.ds(pl.multiple_of(q * GROUP, GROUP), GROUP)
            for tile in range(K // WIDTH):
                scaled[tile, window, :] = part[:, tile * WIDTH : (tile + 1) * WIDTH]
            return inner

        lax.fori_loop(0, 16, scale, 0, unroll=4)

        def one_slot(i, inner):
            even = jnp.concatenate(
                [scaled[tile, pl.ds(i, 16, stride=GROUP), :] for tile in range(K // WIDTH)],
                axis=1,
            )
            odd = even * degree_ref[1:2, :]
            both = jnp.concatenate([even.astype(BF16), odd.astype(BF16)], axis=0)
            result = lax.dot_general(
                both,
                leg[start + i],
                (((1,), (1,)), ((), ())),
                preferred_element_type=F32,
            )
            result = result.astype(BF16).astype(F32)
            sums[pl.ds(pl.multiple_of((start + i) * 16, 16), 16), :] = jnp.concatenate(
                [result[:16], result[16:]], axis=1
            )
            return inner

        leg_wait(g)
        lax.fori_loop(0, GROUP, one_slot, 0, unroll=GROUP)
        return carry

    lax.fori_loop(groups[0], groups[1], one_group, 0)


def row_weights(first, columns, rows_ref, weights):
    m = columns[pl.ds(first, SLOTS), :]
    lanes = lax.broadcasted_iota(jnp.int32, (SLOTS, WIDTH), 1)
    half_m = jnp.floor(m * 0.5)
    parity = 1.0 - 2.0 * (m - 2.0 * half_m)
    weight = jnp.where(m == 0.0, 1.0, 2.0)
    sign = jnp.where(lanes >= HALF, parity, 1.0) * weight
    x = m * (math.pi / NLON)
    x2 = x * x
    sin = x * (
        1.0
        + x2 * (-1.0 / 6 + x2 * (1.0 / 120 + x2 * (-1.0 / 5040 + x2 * (1.0 / 362880))))
    )
    cos = 1.0 + x2 * (
        -0.5
        + x2 * (1.0 / 24 + x2 * (-1.0 / 720 + x2 * (1.0 / 40320 - x2 * (1.0 / 3628800))))
    )
    xx = -4.0 * sin * sin * rows_ref[0:1, :]
    xy = 2.0 * (2.0 * sin * cos) * rows_ref[1:2, :]
    weights[0], weights[1], weights[2] = sign, xx, xy


def combine_rows(start, weights, rows_ref, sums, turned):
    window = pl.ds(start, PART)
    sign, xx, xy = weights[0, window, :], weights[1, window, :], weights[2, window, :]
    lanes = lax.broadcasted_iota(jnp.int32, (PART, WIDTH), 1)
    yy = rows_ref[2:3, :]
    first_lane = (lanes == 0) | (lanes == HALF)
    last_lane = (lanes == HALF - 1) | (lanes == WIDTH - 1)

    def fields(t):
        def pieces(q):
            c = sums[pl.ds(start * 16 + t * 4 + q, PART, stride=16), :] * sign
            before = jnp.where(first_lane, 0.0, pltpu.roll(c, 1, 1))
            after = jnp.where(last_lane, pltpu.roll(c, HALF, 1), pltpu.roll(c, WIDTH - 1, 1))
            return c * xx, (before + after - 2.0 * c) * yy, (before - after) * xy

        pr_xx, pr_yy, pr_xy = pieces(0)
        pi_xx, pi_yy, pi_xy = pieces(1)
        cr_xx, cr_yy, cr_xy = pieces(2)
        ci_xx, ci_yy, ci_xy = pieces(3)
        a = (pr_xx - ci_xy, pi_xx + cr_xy)
        b = (-ci_xy - pr_yy, cr_xy - pi_yy)
        normal = (2.0 * pi_xy + cr_xx - cr_yy, -2.0 * pr_xy + ci_xx - ci_yy)
        return a, b, normal

    for pair in range(TIMES // 2):
        early, late = fields(2 * pair), fields(2 * pair + 1)
        for q in range(3):
            block = jnp.concatenate(early[q] + late[q], axis=0).T
            turned[q, pl.ds(pair, WIDTH, stride=2), :] = block


def build_onehot(wave_ref, onehot):
    lane = lax.broadcasted_iota(jnp.int32, (WIDTH, WIDTH), 1).astype(F32)
    quarter = lax.broadcasted_iota(jnp.int32, (1, WIDTH), 1) // PART

    def one_block(j, carry):
        a = wave_ref[pl.ds(2 * j, 1), :].astype(F32)
        b = wave_ref[pl.ds(2 * j + 1, 1), :].astype(F32)
        for part in range(2):
            shift = PART * part
            line = jnp.where(
                quarter < 2,
                jnp.where(quarter == 0, rolled(a, -shift), rolled(a, -PART - shift)),
                jnp.where(quarter == 2, rolled(b, 64 - shift), rolled(b, PART - shift)),
            )
            column = column_of(line)
            rows = pl.ds(pl.multiple_of(part * (K // 2) + j * WIDTH, WIDTH), WIDTH)
            for tile in range(K // WIDTH):
                onehot[rows, tile * WIDTH : (tile + 1) * WIDTH] = jnp.where(
                    column == lane + float(tile * WIDTH), 1.0, 0.0
                ).astype(BF16)
        return carry

    lax.fori_loop(0, K // (2 * WIDTH), one_block, 0)


def rolled(value, shift):
    shift = shift % WIDTH
    return pltpu.roll(value, shift, 1) if shift else value


def candidate_tables(owner_ref, block_ref, goal, named):
    owner = owner_ref[...]
    owned = jnp.where(
        lax.broadcasted_iota(jnp.int32, (BANDS, CANDS), 0) == owner, 1.0, 0.0
    )
    order = jnp.where(
        lax.broadcasted_iota(jnp.int32, (CANDS, CANDS), 0)
        < lax.broadcasted_iota(jnp.int32, (CANDS, CANDS), 1),
        1.0,
        0.0,
    ).astype(BF16)
    earlier = jnp.dot(owned.astype(BF16), order, preferred_element_type=F32)
    slot = jnp.sum(earlier * owned, axis=0, keepdims=True).astype(jnp.int32)
    second = jnp.where(slot >= PACK, 1, 0)
    target = (slot - PACK * second) * (2 * BANDS) + owner * 2 + second
    goal[...] = jnp.where(
        lax.broadcasted_iota(jnp.int32, (PACK * 2 * BANDS, CANDS), 0) == target, 1.0, 0.0
    ).astype(BF16)
    cells = jnp.where(
        lax.broadcasted_iota(jnp.int32, (256, CANDS), 0) == block_ref[...], 1.0, 0.0
    )
    named[...] = cells.T.astype(BF16)


def join_quad(quad, coeffs, ordered_in, at):
    quarter = lax.broadcasted_iota(jnp.int32, (ROWS, WIDTH), 1) // PART
    sources = [coeffs[4 * quad + k].astype(F32) for k in range(4)]
    rows = []
    for c in range(2):
        for x in range(2):
            group = 2 * x + c
            parts = [rolled(sources[k], (k - group) * PART) for k in range(4)]
            rows.append(
                jnp.where(
                    quarter < 2,
                    jnp.where(quarter == 0, parts[0], parts[1]),
                    jnp.where(quarter == 2, parts[2], parts[3]),
                )
            )
    ordered_in[:, at * WIDTH : (at + 1) * WIDTH] = jnp.concatenate(rows, axis=0).astype(BF16)


def order_slots(start, depth, begin, last, ordered_in, onehot, ordered, spread):
    pick = lax.broadcasted_iota(jnp.int32, (ROWS, WIDTH), 1) < 64
    rows = pl.ds(start, depth)
    for j in range(8):
        at = slice(256 * j, 256 * (j + 1))
        part = jnp.dot(
            ordered_in[:, :depth], onehot[rows, at], preferred_element_type=F32
        )
        if not begin:
            part = part + ordered[:, at]
        if not last:
            ordered[:, at] = part
            continue
        for tile in range(2):
            h = 4 * j + 2 * tile
            for c in range(2):
                a = part[c * 48 : c * 48 + 24, tile * WIDTH : (tile + 1) * WIDTH]
                b = part[c * 48 + 24 : c * 48 + 48, tile * WIDTH : (tile + 1) * WIDTH]
                to = h * 48 + c * 24
                spread[to : to + 24, :] = jnp.where(pick, a, pltpu.roll(b, 64, 1))
                spread[to + 48 : to + 72, :] = jnp.where(pick, pltpu.roll(a, 64, 1), b)


def synthesis(band, spread, tables, vort_out, okubo_out, table, stage, cells):
    first_ref, twiddle_ref, second_ref, fit_ref, fit_rows = tables
    southern = band >= BANDS // 2
    steps = [(pair, r) for pair in range(TIMES // 2) for r in range(4)]
    tc, ts = twiddle_ref[0], twiddle_ref[1]
    for n, (pair, r) in enumerate(steps):
        for f in range(3):
            i = f * 8 + r * 2 + pair
            c = jnp.concatenate(
                [spread[pl.ds(i, 32, stride=48), :], spread[pl.ds(24 + i, 32, stride=48), :]],
                axis=0,
            ).T.astype(BF16)
            z = jnp.dot(
                jnp.concatenate([c, c], axis=1), first_ref[...], preferred_element_type=F32
            )
            zr, zi = z[:, :WIDTH], z[:, WIDTH:]
            z = jnp.concatenate([zr * tc - zi * ts, zr * ts + zi * tc], axis=0)
            high = z.astype(BF16)
            low = (z - high.astype(F32)).astype(BF16)
            at = slice(f * WIDTH, (f + 1) * WIDTH)
            stage[n, 0:256, at] = high
            stage[n, 256:512, at] = low
    for n, (pair, r) in enumerate(steps):
        row = jnp.where(southern, 3 - r, r)
        grid = jnp.dot(
            second_ref[...],
            jnp.concatenate([stage[n, 0:256, :], stage[n]], axis=0),
            preferred_element_type=F32,
        )
        a = grid[:, :WIDTH]
        b = grid[:, WIDTH : 2 * WIDTH]
        normal = grid[:, 2 * WIDTH :]
        vort = a - b
        okubo = normal * normal + 4.0 * (a * b)
        for x in range(2):
            half = slice(64 * x, 64 * x + 64)
            vort_out[2 * pair + x, pl.ds(row, 64, stride=4), :] = vort[half]
            okubo_out[2 * pair + x, pl.ds(row, 64, stride=4), :] = okubo[half]
        both = jnp.concatenate([vort, okubo], axis=1)
        high = both.astype(BF16)
        cells[n, 0:128, :] = high
        cells[n, 128:256, :] = (both - high.astype(F32)).astype(BF16)
    for pair in range(TIMES // 2):
        total = jnp.zeros((WIDTH, WIDTH), F32)
        for r in range(4):
            row = jnp.where(southern, 3 - r, r)
            both = jnp.dot(cells[4 * pair + r], fit_ref[...], preferred_element_type=F32)
            high, low = both[:WIDTH], both[WIDTH:]
            fits = high + pltpu.roll(high, WIDTH - 32, 1) + low
            total += fits * fit_rows[pl.ds(row, 1), :]
        table[128 * pair : 128 * pair + 128, :] = total


def pick_candidates(goal, named, table):
    values = table[...]
    high = values.astype(BF16).astype(F32)
    low = values - high
    chosen = jnp.dot(
        named[...],
        jnp.concatenate([high, low], axis=1).astype(BF16),
        preferred_element_type=F32,
    )
    parts = jnp.dot(goal[...], chosen.astype(BF16), preferred_element_type=F32)
    parts = parts[:, :WIDTH] + parts[:, WIDTH:]
    total = parts[: 2 * BANDS]
    for g in range(1, PACK):
        total += pltpu.roll(parts[2 * BANDS * g : 2 * BANDS * (g + 1)], VALUES * g, 1)
    return total


def whole_kernel(
    spec_hbm,
    leg_hbm,
    wave_hbm,
    owner_hbm,
    block_hbm,
    degree_hbm,
    rows_hbm,
    first_hbm,
    twiddle_hbm,
    second_hbm,
    fit_hbm,
    fit_rows_hbm,
    vort_out,
    okubo_out,
    fits_out,
    wave_ref,
    owner_ref,
    block_ref,
    degree_ref,
    rows_ref,
    first_ref,
    twiddle_ref,
    second_ref,
    fit_ref,
    fit_rows,
    spec,
    leg,
    scaled,
    factor,
    columns,
    weights,
    sums,
    turned,
    send,
    recv,
    onehot,
    goal,
    named,
    ordered_in,
    ordered,
    spread,
    vort,
    okubo,
    table,
    stage,
    cells,
    outgoing,
    arrived,
    joined,
    lines,
    spec_sem,
    leg_sem,
    send_sem,
    recv_sem,
    send_fit,
    recv_fit,
    level_sem,
    out_sem,
    table_sem,
):
    lev = lax.axis_index("lev")
    me = lax.axis_index("band")
    rank = lev * BANDS + me

    def spec_copy(g):
        window = pl.ds(pl.multiple_of(g * GROUP, GROUP), GROUP)
        return pltpu.make_async_copy(
            spec_hbm.at[:, window, :], spec.at[:, window, :], spec_sem.at[g]
        )

    def leg_copy(g):
        window = pl.ds(pl.multiple_of(g * GROUP, GROUP), GROUP)
        return pltpu.make_async_copy(leg_hbm.at[window], leg.at[window], leg_sem.at[g])

    table_copies = [
        pltpu.make_async_copy(source, target, table_sem.at[n])
        for n, (source, target) in enumerate(
            (
                (wave_hbm, wave_ref),
                (degree_hbm, degree_ref),
                (rows_hbm, rows_ref),
                (owner_hbm, owner_ref),
                (block_hbm, block_ref),
                (first_hbm, first_ref),
                (twiddle_hbm, twiddle_ref),
                (second_hbm, second_ref),
                (fit_hbm, fit_ref),
                (fit_rows_hbm, fit_rows),
            )
        )
    ]
    for copy in table_copies[:3]:
        copy.start()
    for g in range(SLOTS // GROUP):
        spec_copy(g).start()
        leg_copy(g).start()
    for copy in table_copies[3:]:
        copy.start()

    barrier = pltpu.get_barrier_semaphore()
    greet_peers(barrier, lev, me)
    greet_band(barrier, lev, me)

    for copy in table_copies[:3]:
        copy.wait()
    columns[...] = column_of(wave_ref[pl.ds(me // 2, 1), :].astype(F32))
    first = pl.multiple_of(lax.rem(me, 2) * SLOTS, SLOTS)
    row_weights(first, columns, rows_ref, weights)
    waits = (lambda g: spec_copy(g).wait(), lambda g: leg_copy(g).wait())
    my_plane = me // PLANE
    my_place = lax.rem(me, PLANE)
    shifts = (0, 1, 3, 2)

    def place(d):
        return jnp.where(d < BANDS // 2, d, BANDS + BANDS // 2 - 1 - d)

    def one_half(half, carry):
        legendre_sums(
            (2 * half, 2 * half + 2),
            first,
            waits,
            spec,
            leg,
            degree_ref,
            columns,
            scaled,
            factor,
            sums,
        )
        combine_rows(
            pl.multiple_of(half * PART, PART), weights, rows_ref, sums, turned
        )
        for p in range(BANDS):
            send[half, p] = jnp.concatenate(
                [turned[q, p * 8 : p * 8 + 8, :] for q in range(3)], axis=0
            ).astype(BF16)

        @pl.when(half == 0)
        def _():
            pl.semaphore_wait(barrier, BANDS - 1 + LEVS - 1)

        for number, shift in enumerate(shifts):
            plane = lax.rem(my_plane + shift, PLANES)
            for k in range(0 if shift else 1, PLANE):
                d = plane * PLANE + lax.rem(my_place + k, PLANE)
                pltpu.make_async_remote_copy(
                    src_ref=send.at[half, place(d)],
                    dst_ref=recv.at[half, me],
                    send_sem=send_sem.at[half],
                    recv_sem=recv_sem.at[half * (1 + number)],
                    device_id={"lev": lev, "band": d},
                    device_id_type=MESH,
                ).start()
        recv[half, me] = send[half, place(me)]
        return carry

    lax.fori_loop(0, 2, one_half, 0)
    greet_peers(level_sem, lev, me)

    def bulk(half, count, number):
        return pltpu.make_async_remote_copy(
            src_ref=send.at[half, pl.ds(0, count)],
            dst_ref=recv.at[half, pl.ds(0, count)],
            send_sem=send_sem.at[half],
            recv_sem=recv_sem.at[number],
            device_id={"lev": lev, "band": me},
            device_id_type=MESH,
        )

    build_onehot(wave_ref, onehot)
    for copy in table_copies[3:]:
        copy.wait()
    candidate_tables(owner_ref, block_ref, goal, named)

    bulk(0, BANDS - 1, 0).wait_recv()
    for quad in range(PLANE):
        join_quad(quad, recv.at[0], ordered_in, quad)
    order_slots(0, K // 2, True, False, ordered_in, onehot, ordered, spread)
    depth = PLANE * PART
    for number, shift in enumerate(shifts):
        plane = lax.rem(my_plane + PLANES - shift, PLANES)
        bulk(1, PLANE if shift else PLANE - 1, 1 + number).wait_recv()
        for k in range(2):
            join_quad(2 * plane + k, recv.at[1], ordered_in, k)
        start = pl.multiple_of(K // 2 + plane * depth, depth)
        order_slots(
            start, depth, False, number == PLANES - 1, ordered_in, onehot, ordered, spread
        )

    tables = (first_ref, twiddle_ref, second_ref, fit_ref, fit_rows)
    synthesis(me, spread, tables, vort, okubo, table, stage, cells)
    grid_copies = [
        pltpu.make_async_copy(vort, vort_out, out_sem.at[0]),
        pltpu.make_async_copy(okubo, okubo_out, out_sem.at[1]),
    ]
    for copy in grid_copies:
        copy.start()
    outgoing[...] = pick_candidates(goal, named, table).reshape(BANDS, 2, WIDTH)

    pl.semaphore_wait(level_sem, LEVS - 1)

    def post_fit(k, carry):
        other = lax.rem(rank + k, MEMBERS)
        owner = lax.rem(other, BANDS)
        pltpu.make_async_remote_copy(
            src_ref=outgoing.at[owner],
            dst_ref=arrived.at[rank],
            send_sem=send_fit,
            recv_sem=recv_fit,
            device_id={"lev": other // BANDS, "band": owner},
            device_id_type=MESH,
        ).start()
        return carry

    lax.fori_loop(1, MEMBERS, post_fit, 0, unroll=16)
    arrived[rank] = outgoing[me]
    everything = pltpu.make_async_remote_copy(
        src_ref=arrived.at[pl.ds(0, MEMBERS - 1)],
        dst_ref=arrived.at[pl.ds(0, MEMBERS - 1)],
        send_sem=send_fit,
        recv_sem=recv_fit,
        device_id={"lev": lev, "band": me},
        device_id_type=MESH,
    )
    everything.wait_recv()

    joined[...] = (arrived[0:32] + arrived[32:64]) + (arrived[64:96] + arrived[96:128])
    for r in range(CAP // PACK):
        line = joined[:, r, :]
        for g in range(PACK):
            value = pltpu.roll(line, WIDTH - VALUES * g, 1) if g else line
            lines[pl.ds(PACK * r + g, BANDS, stride=CAP), :] = value
    fits_out[...] = lines[...].T[:20, :]

    bulk(0, BANDS - 1, 0).wait_send()
    bulk(1, BANDS - 1, 0).wait_send()
    everything.wait_send()
    for copy in grid_copies:
        copy.wait()


def copy_kernel(*refs):
    sources, targets, held, come, go = refs[:3], refs[3:6], refs[6:9], refs[9], refs[10]
    pieces = [(i, t) for i in range(2) for t in range(TIMES)] + [(2, None)]

    def view(ref, t):
        return ref if t is None else ref.at[t]

    inward = [
        pltpu.make_async_copy(view(sources[i], t), view(held[i], t), come.at[n])
        for n, (i, t) in enumerate(pieces)
    ]
    outward = [
        pltpu.make_async_copy(view(held[i], t), view(targets[i], t), go.at[n])
        for n, (i, t) in enumerate(pieces)
    ]
    for copy in inward:
        copy.start()
    for n in range(len(pieces)):
        inward[n].wait()
        outward[n].start()
    for copy in outward:
        copy.wait()


def copied(*results):
    hbm = pl.BlockSpec(memory_space=pl.ANY)
    return pl.pallas_call(
        copy_kernel,
        out_shape=tuple(jax.ShapeDtypeStruct(r.shape, r.dtype) for r in results),
        in_specs=[hbm] * 3,
        out_specs=(hbm,) * 3,
        scratch_shapes=[pltpu.VMEM(r.shape, r.dtype) for r in results]
        + [pltpu.SemaphoreType.DMA((2 * TIMES + 1,)), pltpu.SemaphoreType.DMA((2 * TIMES + 1,))],
        compiler_params=pltpu.CompilerParams(vmem_limit_bytes=60 * 1024 * 1024),
        name="results",
    )(*results)


def whole(spectra, legendre, waves, owner, block):
    vmem = pl.BlockSpec(memory_space=pltpu.VMEM)
    hbm = pl.BlockSpec(memory_space=pl.ANY)
    fit_table, fit_rows = fit_tables()
    grid = jax.ShapeDtypeStruct((TIMES, 256, WIDTH), F32)
    return pl.pallas_call(
        whole_kernel,
        out_shape=(grid, grid, jax.ShapeDtypeStruct((20, BANDS * CAP), F32)),
        in_specs=[hbm] * 12,
        out_specs=(hbm, hbm, vmem),
        scratch_shapes=[
            pltpu.VMEM((K // WIDTH, WIDTH), jnp.int32),
            pltpu.VMEM((1, CANDS), jnp.int32),
            pltpu.VMEM((1, CANDS), jnp.int32),
            pltpu.VMEM((8, K), F32),
            pltpu.VMEM((8, WIDTH), F32),
            pltpu.VMEM((WIDTH, 2 * WIDTH), BF16),
            pltpu.VMEM((2, WIDTH, WIDTH), F32),
            pltpu.VMEM((WIDTH, 6 * WIDTH), BF16),
            pltpu.VMEM((2 * WIDTH, WIDTH), BF16),
            pltpu.VMEM((8, WIDTH), F32),
            pltpu.VMEM((16, SLOTS, K), BF16),
            pltpu.VMEM((SLOTS, HALF, K), BF16),
            pltpu.VMEM((K // WIDTH, 16 * GROUP, WIDTH), F32),
            pltpu.VMEM((GROUP, K), F32),
            pltpu.VMEM((WIDTH, WIDTH), F32),
            pltpu.VMEM((3, SLOTS, WIDTH), F32),
            pltpu.VMEM((SLOTS * 16, WIDTH), F32),
            pltpu.VMEM((3, 2 * WIDTH, WIDTH), F32),
            pltpu.VMEM((2, BANDS, ROWS, WIDTH), BF16),
            pltpu.VMEM((2, BANDS, ROWS, WIDTH), BF16),
            pltpu.VMEM((K, K), BF16),
            pltpu.VMEM((PACK * 2 * BANDS, CANDS), BF16),
            pltpu.VMEM((CANDS, 256), BF16),
            pltpu.VMEM((96, K // 2), BF16),
            pltpu.VMEM((96, K), F32),
            pltpu.VMEM((32 * 48, WIDTH), F32),
            pltpu.VMEM((TIMES, 256, WIDTH), F32),
            pltpu.VMEM((TIMES, 256, WIDTH), F32),
            pltpu.VMEM((256, WIDTH), F32),
            pltpu.VMEM((8, 512, 3 * WIDTH), BF16),
            pltpu.VMEM((8, 256, 256), BF16),
            pltpu.VMEM((BANDS, 2, WIDTH), F32),
            pltpu.VMEM((MEMBERS, 2, WIDTH), F32),
            pltpu.VMEM((BANDS, 2, WIDTH), F32),
            pltpu.VMEM((BANDS * CAP, WIDTH), F32),
            pltpu.SemaphoreType.DMA((SLOTS // GROUP,)),
            pltpu.SemaphoreType.DMA((SLOTS // GROUP,)),
            pltpu.SemaphoreType.DMA((2,)),
            pltpu.SemaphoreType.DMA((1 + PLANES,)),
            pltpu.SemaphoreType.DMA,
            pltpu.SemaphoreType.DMA,
            pltpu.SemaphoreType.REGULAR,
            pltpu.SemaphoreType.DMA((2,)),
            pltpu.SemaphoreType.DMA((10,)),
        ],
        compiler_params=pltpu.CompilerParams(
            collective_id=0, has_side_effects=True, vmem_limit_bytes=56 * 1024 * 1024
        ),
        name="spectral_analysis",
    )(
        spectra,
        legendre,
        waves,
        owner,
        block,
        degree_table(),
        row_table(),
        first_table(),
        twiddle_table(),
        second_table(),
        fit_table,
        fit_rows,
    )


def local(spectra, legendre, wave_order, cand_block, cand_owner):
    results = whole(
        spectra.reshape(16, SLOTS, K),
        legendre,
        wave_order.reshape(K // WIDTH, WIDTH),
        cand_owner.reshape(1, CANDS),
        cand_block.reshape(1, CANDS),
    )
    vort, okubo, fits = copied(*results)

    def rows(field):
        shaped = field.reshape(TIMES, 64, 4, WIDTH).transpose(0, 2, 1, 3)
        return shaped.reshape(1, TIMES, 4, NLON)

    return rows(vort), rows(okubo), fits.T


def solution(mesh):
    placed = (
        P("lev", None, None, None, "band", None),
        P("band", None, None),
        P(),
        P("band"),
        P("band", None),
    )
    return jax.shard_map(
        local,
        mesh=mesh,
        in_specs=placed,
        out_specs=(P("lev", None, "band", None), P("lev", None, "band", None), P("band", None)),
        check_vma=False,
    )
```
